512 devices in a mesh: lon: 32 (over z, core), lat: 16 (over y, x).
Axes of the slice: x: 4, y: 4, z: 16, core: 2. Of those that a mesh axis runs over, the one named last changes fastest.
Arguments:
- wind_u: float32 [2, 5760, 2048], P(None, 'lon', 'lat'), may hold values from -6 to 6
- wind_v: float32 [2, 5760, 2048], P(None, 'lon', 'lat'), may hold values from -6 to 6
- thickness: float32 [2, 5760, 2048], P(None, 'lon', 'lat'), may hold values from 0.5 to 1.5
Outputs:
- wind_u_next: float32 [2, 5760, 2048], P(None, 'lon', 'lat')
- wind_v_next: float32 [2, 5760, 2048], P(None, 'lon', 'lat')
- thickness_next: float32 [2, 5760, 2048], P(None, 'lon', 'lat')
The draws below stay inside these ranges and needn't reach their ends.
All inputs are finite; a program needn't handle non-finite values.
Results may differ from the reference program's by a relative error of at most 0.000073.
Values sent between devices are 32-bit elements; how exact they have to be, the bound alone decides.
No kernel may reach another device: no remote copies, remote signals or barrier semaphores. Data moves between devices by JAX's collectives and lax.ppermute only.
A program may use at most 64 MiB of HBM per device.

```python
import math
import jax
import jax.numpy as jnp

NLON = 5760
LEV = 2
LAT_DEV = 128
NLAT = 2048
N_LAT = 16


def block_levels(rng, shape, pieces, low, top_value):
    loudness, own = 1.0, jax.random.fold_in(rng, 6)
    for dim, parts in pieces:
        steps = jnp.exp(jax.random.uniform(jax.random.fold_in(own, dim), (parts,), jnp.float32, low / len(pieces), top_value / len(pieces)))
        loudness = loudness * jnp.repeat(steps, shape[dim] // parts).reshape([-1 if axis == dim else 1 for axis in range(len(shape))])
    return loudness


def gaussian(key, extent, deviation, most, cuts=(), kind=jnp.bfloat16):
    values = deviation * jax.random.normal(key, extent, jnp.float32)
    if cuts:
        values = values * block_levels(key, extent, cuts, -0.22, 0.18)
    return jnp.clip(values, -most, most).astype(kind)


def setup_inputs(seed: int = 0) -> dict:
    key_list = jax.random.split(jax.random.key(seed), 4)
    return {
        "wind_u": gaussian(key_list[0], (LEV, NLON, NLAT), 1.0, 6.0, ((1, 32), (2, 16)), jnp.float32),
        "wind_v": gaussian(key_list[1], (LEV, NLON, NLAT), 1.0, 6.0, ((1, 32), (2, 16)), jnp.float32),
        "thickness": jnp.clip(0.5 + 1.0 * jax.random.uniform(key_list[2], (LEV, NLON, NLAT), jnp.float32) ** block_levels(key_list[2], (LEV, NLON, NLAT), ((1, 32), (2, 16)), -0.2, 0.2), 0.5, 1.5),
    }


def row_latitude(row_index, nlat_all):
    return -0.5 * math.pi + (row_index.astype(jnp.float32) + 0.5) * (math.pi / nlat_all)


def polar_filter(values, latitude):
    ratio = jnp.cos(latitude) / math.cos(0.25 * math.pi)
    wave_index = jnp.arange(NLON, dtype=jnp.float32)
    sine = jnp.sin(wave_index * (math.pi / NLON))
    damping = ratio[:, None] ** 2 / jnp.maximum(sine[None, :] ** 2, ratio[:, None] ** 2)
    spectrum = jnp.fft.fft(values, axis=-1)
    return jnp.real(jnp.fft.ifft(spectrum * damping, axis=-1)).astype(values.dtype)


def step_rows(wind_u, wind_v, thickness):
    nlat_all = LAT_DEV * N_LAT
    latitude = row_latitude(jnp.arange(nlat_all, dtype=jnp.int32), nlat_all)
    lat_step = math.pi / nlat_all
    lon_step = 2.0 * math.pi / NLON
    time_step = 0.25 * lat_step
    coslat = jnp.cos(latitude)[:, None]
    rotation = (0.3 * jnp.sin(latitude))[:, None]
    flux_x = polar_filter(wind_u * thickness, latitude)
    flux_y = polar_filter(wind_v * thickness * coslat, latitude)
    x_coef = time_step / (2.0 * lon_step * coslat)
    y_coef = time_step / (2.0 * lat_step * coslat)
    padded_y = jnp.pad(flux_y, ((0, 0), (1, 1), (0, 0)))
    new_mass = thickness - x_coef * (jnp.roll(flux_x, -1, axis=2) - jnp.roll(flux_x, 1, axis=2))
    new_mass = new_mass - y_coef * (padded_y[:, 2:] - padded_y[:, :-2])
    padded_m = jnp.pad(new_mass, ((0, 0), (1, 1), (0, 0)))
    push_u = -x_coef * (jnp.roll(new_mass, -1, axis=2) - jnp.roll(new_mass, 1, axis=2)) + rotation * wind_v
    push_v = -(time_step / (2.0 * lat_step)) * (padded_m[:, 2:] - padded_m[:, :-2]) - rotation * wind_u
    wind_u_next = wind_u + polar_filter(push_u, latitude)
    wind_v_next = wind_v + polar_filter(push_v, latitude)
    return wind_u_next, wind_v_next, new_mass


def reference(wind_u, wind_v, thickness):
    outs = step_rows(jnp.swapaxes(wind_u, 1, 2), jnp.swapaxes(wind_v, 1, 2), jnp.swapaxes(thickness, 1, 2))
    return (jnp.swapaxes(outs[0], 1, 2), jnp.swapaxes(outs[1], 1, 2), jnp.swapaxes(outs[2], 1, 2))
```

```python
import functools
import math

import jax
import jax.numpy as jnp
import numpy as np
from jax import lax
from jax.experimental import pallas as pl
from jax.experimental.pallas import tpu as pltpu
from jax.sharding import PartitionSpec as P

HIGH = lax.Precision.HIGHEST

NLON = 5760
NLAT = 2048
PARTS = 32
SEG = 180
LANES = 128
TAIL = SEG - LANES
HALF = 64
ROWS = 8
WAVES = PARTS // 2 + 1
WIDE = 2 * LANES
SCALE = 1.0 / NLON
CHUNK = 5 * ROWS


def places(variant):
    b = np.arange(SEG)
    return np.where(b < LANES, b, b + variant * HALF)


def dft_tables():
    b = np.arange(SEG)
    angle = (np.outer(b, b) % SEG) * (2.0 * math.pi / SEG)
    cos, sin = np.cos(angle), np.sin(angle)
    forward, inverse = [], []
    for variant in (0, 1):
        at = places(variant)
        table = np.zeros((2 * WIDE, 2 * WIDE))
        table[np.ix_(at, b)] = cos
        table[np.ix_(at, WIDE + b)] = -sin
        table[np.ix_(WIDE + at, b)] = sin
        table[np.ix_(WIDE + at, WIDE + b)] = cos
        forward.append(table)
        table = np.zeros((2 * WIDE, 2 * WIDE))
        table[np.ix_(b, at)] = cos
        table[np.ix_(b, WIDE + at)] = sin
        table[np.ix_(WIDE + b, at)] = -sin
        table[np.ix_(WIDE + b, WIDE + at)] = cos
        inverse.append(table)
    return np.stack(forward).astype(np.float32), np.stack(inverse).astype(np.float32)


def twiddle_table():
    angle = np.zeros((WAVES, WIDE))
    turn = np.outer(np.arange(WAVES), np.arange(SEG)) * (2.0 * math.pi / NLON)
    for variant in (0, 1):
        angle[:, places(variant)] = turn
    return np.concatenate([np.cos(angle), np.sin(angle)]).astype(np.float32)


def wave_table():
    k = np.arange(WAVES)[:, None] + PARTS * np.arange(SEG)[None, :]
    step = np.float32(math.pi / NLON)
    here = np.sin(k.astype(np.float32) * step) ** 2
    there = np.sin(((NLON - k) % NLON).astype(np.float32) * step) ** 2
    slope = 2.0 * np.sin(2.0 * math.pi * k / NLON)
    table = np.zeros((3 * WAVES, WIDE), np.float32)
    table[:, :SEG] = np.concatenate([here, there, slope])
    return table


def row_table():
    j = np.arange(-1, NLAT + 1)
    phi = np.float32(-0.5 * math.pi) + (j.astype(np.float32) + np.float32(0.5)) * np.float32(math.pi / NLAT)
    phi = phi.astype(np.float64)
    lat_step, lon_step = math.pi / NLAT, 2.0 * math.pi / NLON
    time_step = 0.25 * lat_step
    cos = np.cos(phi)
    y_coef = time_step / (2.0 * lat_step * cos)
    y_coef[0] = y_coef[-1] = 0.0
    table = np.zeros((NLAT, LANES))
    table[:, 0] = (cos / math.cos(0.25 * math.pi))[1:-1] ** 2
    table[:, 1] = (time_step / (2.0 * lon_step * cos))[1:-1]
    table[:, 2] = y_coef[1:-1]
    table[:, 3] = 0.3 * np.sin(phi)[1:-1]
    table[:, 4] = cos[1:-1]
    table[:, 5] = np.repeat(y_coef[0:NLAT:ROWS], ROWS)
    table[:, 6] = np.repeat(y_coef[ROWS + 1 :: ROWS], ROWS)
    return table.reshape(NLAT // ROWS, ROWS, LANES).astype(np.float32)


PUSH_COEF = 0.25 / 2.0


def add(x, y):
    if x is None:
        return y
    return x if y is None else x + y


def sub(x, y):
    if y is None:
        return x
    return -y if x is None else x - y


def times(z, cos, sin):
    re, im = z
    if abs(sin) < 1e-15:
        return (re * cos, None if im is None else im * cos)
    if im is None:
        return (re * cos, re * sin)
    return (re * cos - im * sin, re * sin + im * cos)


def real_fft(values):
    n = len(values)
    if n == 2:
        return [(values[0] + values[1], None), (values[0] - values[1], None)]
    even, odd = real_fft(values[0::2]), real_fft(values[1::2])
    out = [None] * (n // 2 + 1)
    out[0] = (even[0][0] + odd[0][0], None)
    out[n // 2] = (even[0][0] - odd[0][0], None)
    for k in range(1, n // 4):
        re, im = times(odd[k], math.cos(2 * math.pi * k / n), -math.sin(2 * math.pi * k / n))
        out[k] = (add(even[k][0], re), add(even[k][1], im))
        out[n // 2 - k] = (sub(even[k][0], re), sub(im, even[k][1]))
    out[n // 4] = (even[n // 4][0], -odd[n // 4][0])
    return out


def real_ifft(waves):
    n = 2 * (len(waves) - 1)
    if n == 2:
        return [waves[0][0] + waves[1][0], waves[0][0] - waves[1][0]]
    even, odd = [None] * (n // 4 + 1), [None] * (n // 4 + 1)
    even[0] = (waves[0][0] + waves[n // 2][0], None)
    odd[0] = (waves[0][0] - waves[n // 2][0], None)
    for k in range(1, n // 4):
        (re, im), (far_re, far_im) = waves[k], waves[n // 2 - k]
        even[k] = (re + far_re, im - far_im)
        odd[k] = times((re - far_re, im + far_im), math.cos(2 * math.pi * k / n), math.sin(2 * math.pi * k / n))
    even[n // 4] = (2.0 * waves[n // 4][0], None)
    odd[n // 4] = (-2.0 * waves[n // 4][1], None)
    out = [None] * n
    out[0::2], out[1::2] = real_ifft(even), real_ifft(odd)
    return out


def pack_kernel(u_ref, v_ref, h_ref, out_ref, tail_ref):
    tail_ref[...] = jnp.zeros_like(tail_ref)
    for level in range(2):
        span = slice(level * 16, level * 16 + 16)
        for f, ref in enumerate((u_ref, v_ref, h_ref)):
            out_ref[span, f * ROWS : (f + 1) * ROWS, :] = ref[level, :LANES, :].T.reshape(16, ROWS, LANES)
        for f, pair in ((3, (u_ref, v_ref)), (4, (h_ref, h_ref))):
            for half, ref in enumerate(pair):
                tail_ref[half * HALF : half * HALF + TAIL, :] = ref[level, LANES:, :]
            out_ref[span, f * ROWS : (f + 1) * ROWS, :] = tail_ref[...].T.reshape(16, ROWS, LANES)


def unpack_kernel(in_ref, u_ref, v_ref, h_ref, u_out, v_out, h_out):
    for level in range(2):
        span = slice(level * 16, level * 16 + 16)

        def back(f):
            return in_ref[span, f * ROWS : (f + 1) * ROWS, :].reshape(LANES, LANES).T

        tails = (back(3), back(4))
        for f, (ref, out) in enumerate(((u_ref, u_out), (v_ref, v_out), (h_ref, h_out))):
            out[level, :LANES, :] = ref[level, :LANES, :] + back(f)
            half = HALF * (f == 1)
            out[level, LANES:, :] = ref[level, LANES:, :] + tails[f // 2][half : half + TAIL]


def dot(x, y):
    return jnp.dot(x, y, precision=HIGH, preferred_element_type=jnp.float32)


H, U, UH, V, VH = range(5)
BLOCK = WAVES * ROWS


def forward_kernel(x_ref, table_ref, twiddle_ref, wave_ref, row_ref, spec_ref, up_ref, down_ref, left_ref):
    def tile(a, f):
        return x_ref[a, f * ROWS : (f + 1) * ROWS, :]

    def product(f, g):
        return lambda a: tile(a, f) * tile(a, g)

    columns = (
        (lambda a: tile(a, 0), 0, (U,)),
        (lambda a: tile(a, 1), 0, (V,)),
        (lambda a: tile(a, 2), 0, (H,)),
        (product(0, 2), 0, (UH,)),
        (product(1, 2), 0, (VH,)),
        (lambda a: tile(a, 3), 1, (U, V)),
        (lambda a: tile(a, 4), 1, (H,)),
        (product(3, 4), 1, (UH, VH)),
    )
    for get, part, fields in columns:
        lanes = slice(part * LANES, (part + 1) * LANES)
        late = slice(WIDE + part * LANES, WIDE + (part + 1) * LANES)
        for k1, (re, im) in enumerate(real_fft([get(a) for a in range(PARTS)])):
            cos = twiddle_ref[k1 : k1 + 1, lanes]
            sin = twiddle_ref[WAVES + k1 : WAVES + k1 + 1, lanes]
            if im is None:
                new_re, new_im = re * cos, -re * sin
            else:
                new_re, new_im = re * cos + im * sin, im * cos - re * sin
            for f in fields:
                rows = slice(f * BLOCK + k1 * ROWS, f * BLOCK + (k1 + 1) * ROWS)
                left_ref[rows, lanes] = new_re
                left_ref[rows, late] = new_im
    spec_ref[: V * BLOCK, :] = dot(left_ref[: V * BLOCK, :], table_ref[0])
    spec_ref[V * BLOCK :, :] = dot(left_ref[V * BLOCK :, :], table_ref[1])

    row = row_ref[0]
    ratio2, x_coef, coslat = row[:, 0:1], row[:, 1:2], row[:, 4:5]
    real, imag = slice(0, WIDE), slice(WIDE, 2 * WIDE)
    zeros = jnp.zeros((2, WIDE), jnp.float32)
    for k1 in range(WAVES):
        here, there, slope = (wave_ref[i * WAVES + k1 : i * WAVES + k1 + 1, :] for i in range(3))
        damp = 0.5 * (ratio2 / jnp.maximum(here, ratio2) + ratio2 / jnp.maximum(there, ratio2))

        def rows(f):
            return slice(f * BLOCK + k1 * ROWS, f * BLOCK + (k1 + 1) * ROWS)

        across = x_coef * slope * damp
        gain_re = across * spec_ref[rows(UH), imag]
        gain_im = -across * spec_ref[rows(UH), real]
        spec_ref[rows(UH), real] = gain_re
        spec_ref[rows(UH), imag] = gain_im
        mass_re = spec_ref[rows(H), real] + gain_re
        mass_im = spec_ref[rows(H), imag] + gain_im
        scale = damp * coslat
        flux_re = scale * spec_ref[rows(VH), real]
        flux_im = scale * spec_ref[rows(VH), imag]
        spec_ref[rows(VH), real] = flux_re
        spec_ref[rows(VH), imag] = flux_im
        up_ref[k1] = jnp.concatenate([mass_re[7:8], mass_im[7:8], flux_re[6:8], flux_im[6:8], zeros], axis=0)
        down_ref[k1] = jnp.concatenate([mass_re[0:1], mass_im[0:1], flux_re[0:2], flux_im[0:2], zeros], axis=0)


def inverse_kernel(spec_ref, below_ref, above_ref, table_ref, twiddle_ref, wave_ref, row_ref, out_ref, left_ref, right_ref):
    row = row_ref[0]
    ratio2, x_coef, y_coef, rotation = (row[:, i : i + 1] for i in range(4))
    y_below, y_above = row[0:1, 5:6], row[0:1, 6:7]
    spans = (slice(0, WIDE), slice(WIDE, 2 * WIDE))
    for k1 in range(WAVES):
        here, there, slope = (wave_ref[i * WAVES + k1 : i * WAVES + k1 + 1, :] for i in range(3))
        damp = (0.5 * SCALE) * (ratio2 / jnp.maximum(here, ratio2) + ratio2 / jnp.maximum(there, ratio2))

        def rows(f):
            return slice(f * BLOCK + k1 * ROWS, f * BLOCK + (k1 + 1) * ROWS)

        mass = []
        for part, span in enumerate(spans):
            flux = spec_ref[rows(VH), span]
            gain = spec_ref[rows(UH), span]
            mass_below, mass_above = below_ref[k1, part : part + 1, :], above_ref[k1, part : part + 1, :]
            fluxes_below = below_ref[k1, 2 + 2 * part : 4 + 2 * part, :]
            fluxes_above = above_ref[k1, 2 + 2 * part : 4 + 2 * part, :]
            prev = jnp.concatenate([fluxes_below[1:2], flux[:-1]], axis=0)
            following = jnp.concatenate([flux[1:], fluxes_above[0:1]], axis=0)
            change = gain - y_coef * (following - prev)
            new = spec_ref[rows(H), span] + change
            new_below = mass_below - y_below * (flux[0:1] - fluxes_below[0:1])
            new_above = mass_above - y_above * (fluxes_above[1:2] - flux[7:8])
            mass.append(new)
            prev = jnp.concatenate([new_below, new[:-1]], axis=0)
            following = jnp.concatenate([new[1:], new_above], axis=0)
            push = -PUSH_COEF * (following - prev) - rotation * spec_ref[rows(U), span]
            left_ref[rows(2), span] = damp * push
            left_ref[rows(0), span] = SCALE * change
        across = x_coef * slope
        left_ref[rows(1), spans[0]] = damp * (across * mass[1] + rotation * spec_ref[rows(V), spans[0]])
        left_ref[rows(1), spans[1]] = damp * (rotation * spec_ref[rows(V), spans[1]] - across * mass[0])
    right_ref[: 2 * BLOCK, :] = dot(left_ref[: 2 * BLOCK, :], table_ref[0])
    right_ref[2 * BLOCK :, :] = dot(left_ref[2 * BLOCK :, :], table_ref[1])
    for f, part, fields in ((0, 0, (1,)), (1, 0, (2,)), (2, 0, (0,)), (3, 1, (1, 2)), (4, 1, (0,))):
        lanes = slice(part * LANES, (part + 1) * LANES)
        late = slice(WIDE + part * LANES, WIDE + (part + 1) * LANES)
        waves = []
        for k1 in range(WAVES):
            cos = twiddle_ref[k1 : k1 + 1, lanes]
            sin = twiddle_ref[WAVES + k1 : WAVES + k1 + 1, lanes]
            spots = [slice(g * BLOCK + k1 * ROWS, g * BLOCK + (k1 + 1) * ROWS) for g in fields]
            re = functools.reduce(lambda x, y: x + y, [right_ref[s, lanes] for s in spots])
            im = functools.reduce(lambda x, y: x + y, [right_ref[s, late] for s in spots])
            waves.append((re * cos - im * sin, None if k1 in (0, WAVES - 1) else im * cos + re * sin))
        for a, value in enumerate(real_ifft(waves)):
            out_ref[a, f * ROWS : (f + 1) * ROWS, :] = value


def in_vmem():
    return pl.BlockSpec(memory_space=pltpu.VMEM)


PARAMS = pltpu.CompilerParams(vmem_limit_bytes=40 * 2**20)


def like(*shape):
    return jax.ShapeDtypeStruct(shape, jnp.float32)


def neighbour_pairs(up):
    pairs = []
    for lat in range(16):
        for level in range(2):
            for r in range(15):
                pairs.append(((level * 16 + r) * 16 + lat, (level * 16 + r + 1) * 16 + lat))
            if lat < 15:
                pairs.append(((level * 16 + 15) * 16 + lat, level * 16 * 16 + lat + 1))
    return pairs if up else [(b, a) for a, b in pairs]


def pack(u, v, h):
    return pl.pallas_call(
        pack_kernel,
        out_shape=like(PARTS, CHUNK, LANES),
        in_specs=[in_vmem()] * 3,
        out_specs=in_vmem(),
        scratch_shapes=[pltpu.VMEM((LANES, LANES), jnp.float32)],
        compiler_params=PARAMS,
        name="pack",
    )(u, v, h)


def forward(whole, row):
    return pl.pallas_call(
        forward_kernel,
        out_shape=(like(5 * BLOCK, 2 * WIDE), like(WAVES, ROWS, WIDE), like(WAVES, ROWS, WIDE)),
        in_specs=[in_vmem()] * 5,
        out_specs=(in_vmem(),) * 3,
        scratch_shapes=[pltpu.VMEM((5 * BLOCK, 2 * WIDE), jnp.float32)],
        compiler_params=PARAMS,
        name="forward",
    )(whole, dft_tables()[0], twiddle_table(), wave_table(), row)


def inverse(spec, below, above, row):
    return pl.pallas_call(
        inverse_kernel,
        out_shape=like(PARTS, CHUNK, LANES),
        in_specs=[in_vmem()] * 7,
        out_specs=in_vmem(),
        scratch_shapes=[pltpu.VMEM((3 * BLOCK, 2 * WIDE), jnp.float32)] * 2,
        compiler_params=PARAMS,
        name="inverse",
    )(spec, below, above, dft_tables()[1], twiddle_table(), wave_table(), row)


def unpack(back, u, v, h):
    return pl.pallas_call(
        unpack_kernel,
        out_shape=(like(2, SEG, LANES),) * 3,
        in_specs=[in_vmem()] * 4,
        out_specs=(in_vmem(),) * 3,
        compiler_params=PARAMS,
        name="unpack",
    )(back, u, v, h)


def row_of(group):
    return lax.dynamic_slice_in_dim(jnp.asarray(row_table()), group, 1, axis=0)


def step(u, v, h):
    row = row_of(lax.axis_index("lat") * 16 + lax.axis_index("lon") % 16)
    whole = lax.all_to_all(pack(u, v, h), "lon", 0, 0, tiled=True)
    spec, up, down = forward(whole, row)
    below = lax.ppermute(up, ("lon", "lat"), neighbour_pairs(True))
    above = lax.ppermute(down, ("lon", "lat"), neighbour_pairs(False))
    back = lax.all_to_all(inverse(spec, below, above, row), "lon", 0, 0, tiled=True)
    return unpack(back, u, v, h)


def solution(mesh):
    spec = P(None, "lon", "lat")
    return jax.shard_map(step, mesh=mesh, in_specs=(spec,) * 3, out_specs=(spec,) * 3, check_vma=False)
```

```python
import functools
import math

import jax
import jax.numpy as jnp
import numpy as np
from jax import lax
from jax.experimental import pallas as pl
from jax.experimental.pallas import tpu as pltpu
from jax.sharding import PartitionSpec as P

HIGH = lax.Precision.HIGHEST

NLON = 5760
NLAT = 2048
PARTS = 32
SEG = 180
LANES = 128
TAIL = SEG - LANES
HALF = 64
ROWS = 8
WAVES = PARTS // 2 + 1
WIDE = 2 * LANES
SCALE = 1.0 / NLON
CHUNK = 4 * ROWS + ROWS // 2


def places(half):
    b = np.arange(SEG)
    return np.where(b < LANES, b, b + half * HALF)


def dft_table():
    b = np.arange(SEG)
    angle = (np.outer(b, b) % SEG) * (2.0 * math.pi / SEG)
    cos, sin = np.cos(angle), np.sin(angle)
    table = np.zeros((2 * WIDE, 2 * WIDE))
    for half in (0, 1):
        at = places(half)
        table[np.ix_(at, b)] = cos
        table[np.ix_(at, WIDE + b)] = -sin
        table[np.ix_(WIDE + at, b)] = sin
        table[np.ix_(WIDE + at, WIDE + b)] = cos
    return table.astype(np.float32)


def twiddle_table():
    angle = np.zeros((WAVES, WIDE))
    turn = np.outer(np.arange(WAVES), np.arange(SEG)) * (2.0 * math.pi / NLON)
    for half in (0, 1):
        angle[:, places(half)] = turn
    return np.concatenate([np.cos(angle), np.sin(angle)]).astype(np.float32)


def wave_table():
    k = np.arange(WAVES)[:, None] + PARTS * np.arange(SEG)[None, :]
    step = np.float32(math.pi / NLON)
    here = np.sin(k.astype(np.float32) * step) ** 2
    there = np.sin(((NLON - k) % NLON).astype(np.float32) * step) ** 2
    slope = 2.0 * np.sin(2.0 * math.pi * k / NLON)
    table = np.zeros((3 * WAVES, WIDE), np.float32)
    table[:, :SEG] = np.concatenate([here, there, slope])
    return table


def row_table():
    j = np.arange(-1, NLAT + 1)
    phi = np.float32(-0.5 * math.pi) + (j.astype(np.float32) + np.float32(0.5)) * np.float32(math.pi / NLAT)
    phi = phi.astype(np.float64)
    lat_step, lon_step = math.pi / NLAT, 2.0 * math.pi / NLON
    time_step = 0.25 * lat_step
    cos = np.cos(phi)
    y_coef = time_step / (2.0 * lat_step * cos)
    y_coef[0] = y_coef[-1] = 0.0
    table = np.zeros((NLAT, LANES))
    table[:, 0] = (cos / math.cos(0.25 * math.pi))[1:-1] ** 2
    table[:, 1] = (time_step / (2.0 * lon_step * cos))[1:-1]
    table[:, 2] = y_coef[1:-1]
    table[:, 3] = 0.3 * np.sin(phi)[1:-1]
    table[:, 4] = cos[1:-1]
    table[:, 5] = np.repeat(y_coef[0:NLAT:ROWS], ROWS)
    table[:, 6] = np.repeat(y_coef[ROWS + 1 :: ROWS], ROWS)
    return table.reshape(NLAT // ROWS, ROWS, LANES).astype(np.float32)


PUSH_COEF = 0.25 / 2.0


def add(x, y):
    if x is None:
        return y
    return x if y is None else x + y


def sub(x, y):
    if y is None:
        return x
    return -y if x is None else x - y


def times(z, cos, sin):
    re, im = z
    if abs(sin) < 1e-15:
        return (re * cos, None if im is None else im * cos)
    if im is None:
        return (re * cos, re * sin)
    return (re * cos - im * sin, re * sin + im * cos)


def real_fft(values):
    n = len(values)
    if n == 2:
        return [(values[0] + values[1], None), (values[0] - values[1], None)]
    even, odd = real_fft(values[0::2]), real_fft(values[1::2])
    out = [None] * (n // 2 + 1)
    out[0] = (even[0][0] + odd[0][0], None)
    out[n // 2] = (even[0][0] - odd[0][0], None)
    for k in range(1, n // 4):
        re, im = times(odd[k], math.cos(2 * math.pi * k / n), -math.sin(2 * math.pi * k / n))
        out[k] = (add(even[k][0], re), add(even[k][1], im))
        out[n // 2 - k] = (sub(even[k][0], re), sub(im, even[k][1]))
    out[n // 4] = (even[n // 4][0], -odd[n // 4][0])
    return out


def real_ifft(waves):
    n = 2 * (len(waves) - 1)
    if n == 2:
        return [waves[0][0] + waves[1][0], waves[0][0] - waves[1][0]]
    even, odd = [None] * (n // 4 + 1), [None] * (n // 4 + 1)
    even[0] = (waves[0][0] + waves[n // 2][0], None)
    odd[0] = (waves[0][0] - waves[n // 2][0], None)
    for k in range(1, n // 4):
        (re, im), (far_re, far_im) = waves[k], waves[n // 2 - k]
        even[k] = (re + far_re, im - far_im)
        odd[k] = times((re - far_re, im + far_im), math.cos(2 * math.pi * k / n), math.sin(2 * math.pi * k / n))
    even[n // 4] = (2.0 * waves[n // 4][0], None)
    odd[n // 4] = (-2.0 * waves[n // 4][1], None)
    out = [None] * n
    out[0::2], out[1::2] = real_ifft(even), real_ifft(odd)
    return out


def first_half(shape):
    return lax.broadcasted_iota(jnp.int32, shape, 1) < HALF


def spot(level, r, turned):
    return CHUNK * (level * 16 + (15 - r if turned else r))


def pack_kernel(turn_ref, u_ref, v_ref, h_ref, out_ref, tail_ref):
    tail_ref[...] = jnp.zeros_like(tail_ref)
    for level in range(2):
        tiles = [ref[pl.ds(level, LANES, 2), :].T for ref in (u_ref, v_ref, h_ref)]
        for pair in ((u_ref, v_ref), (h_ref, h_ref)):
            for half, ref in enumerate(pair):
                tail_ref[half * HALF : half * HALF + TAIL, :] = ref[pl.ds(2 * LANES + level, TAIL, 2), :]
            tiles.append(tail_ref[...].T)
        for turned in (False, True):

            @pl.when(turn_ref[0] == int(turned))
            def _():
                for r in range(16):
                    at = spot(level, r, turned)
                    for f in range(4):
                        out_ref[at + f * ROWS : at + (f + 1) * ROWS, :] = tiles[f][r * ROWS : (r + 1) * ROWS]
                    low, high = tiles[4][r * ROWS : r * ROWS + 4], tiles[4][r * ROWS + 4 : (r + 1) * ROWS]
                    out_ref[at + 4 * ROWS : at + CHUNK, :] = jnp.where(first_half(low.shape), low, high)


def unpack_kernel(turn_ref, in_ref, u_ref, v_ref, h_ref, u_out, v_out, h_out, tile_ref):
    for level in range(2):
        for turned in (False, True):

            @pl.when(turn_ref[0] == int(turned))
            def _():
                for r in range(16):
                    at = spot(level, r, turned)
                    for f in range(4):
                        tile_ref[f, r * ROWS : (r + 1) * ROWS, :] = in_ref[at + f * ROWS : at + (f + 1) * ROWS, :]
                    tail = in_ref[at + 4 * ROWS : at + CHUNK, :]
                    tile_ref[4, r * ROWS : (r + 1) * ROWS, :] = jnp.concatenate([tail, tail], axis=0)

        tails = tile_ref[3].T, tile_ref[4].T
        early = lax.broadcasted_iota(jnp.int32, (TAIL, LANES), 1) % ROWS < ROWS // 2
        tails = (tails[0][:TAIL], tails[0][HALF : HALF + TAIL], jnp.where(early, tails[1][:TAIL], tails[1][HALF : HALF + TAIL]))
        for f, (ref, out) in enumerate(((u_ref, u_out), (v_ref, v_out), (h_ref, h_out))):
            here = pl.ds(level, LANES, 2)
            out[here, :] = ref[here, :] + tile_ref[f].T
            here = pl.ds(2 * LANES + level, TAIL, 2)
            out[here, :] = ref[here, :] + tails[f]


def dot(x, y, contract):
    return lax.dot_general(
        x, y, (((1,), (contract,)), ((), ())), precision=HIGH, preferred_element_type=jnp.float32
    )


H, U, UH, V, VH = range(5)
BLOCK = WAVES * ROWS


def forward_kernel(x_ref, table_ref, twiddle_ref, wave_ref, row_ref, spec_ref, up_ref, down_ref, left_ref):
    def tile(a, f):
        at = a * CHUNK + f * ROWS
        return x_ref[at : at + ROWS, :]

    def tail(a):
        here = x_ref[a * CHUNK + 4 * ROWS : (a + 1) * CHUNK, :]
        there = pltpu.roll(here, HALF, 1)
        first = first_half(here.shape)
        return jnp.concatenate([jnp.where(first, here, there), jnp.where(first, there, here)], axis=0)

    def product(f, g):
        return lambda a: tile(a, f) * tile(a, g)

    columns = (
        (lambda a: tile(a, 0), 0, (U,)),
        (lambda a: tile(a, 1), 0, (V,)),
        (lambda a: tile(a, 2), 0, (H,)),
        (product(0, 2), 0, (UH,)),
        (product(1, 2), 0, (VH,)),
        (lambda a: tile(a, 3), 1, (U, V)),
        (tail, 1, (H,)),
        (lambda a: tile(a, 3) * tail(a), 1, (UH, VH)),
    )
    first = first_half((ROWS, LANES))
    for get, part, fields in columns:
        lanes = slice(part * LANES, (part + 1) * LANES)
        late = slice(WIDE + part * LANES, WIDE + (part + 1) * LANES)
        for k1, (re, im) in enumerate(real_fft([get(a) for a in range(PARTS)])):
            cos = twiddle_ref[k1 : k1 + 1, lanes]
            sin = twiddle_ref[WAVES + k1 : WAVES + k1 + 1, lanes]
            if im is None:
                new_re, new_im = re * cos, -re * sin
            else:
                new_re, new_im = re * cos + im * sin, im * cos - re * sin
            for f in fields:
                rows = slice(f * BLOCK + k1 * ROWS, f * BLOCK + (k1 + 1) * ROWS)
                if part == 0:
                    left_ref[rows, lanes], left_ref[rows, late] = new_re, new_im
                else:
                    mine = jnp.logical_not(first) if f >= V else first
                    left_ref[rows, lanes] = jnp.where(mine, new_re, 0.0)
                    left_ref[rows, late] = jnp.where(mine, new_im, 0.0)
    spec_ref[...] = dot(left_ref[...], table_ref[...], 0)

    row = row_ref[0]
    ratio2, x_coef, coslat = row[:, 0:1], row[:, 1:2], row[:, 4:5]
    real, imag = slice(0, WIDE), slice(WIDE, 2 * WIDE)
    zeros = jnp.zeros((2, WIDE), jnp.float32)
    for k1 in range(WAVES):
        here, there, slope = (wave_ref[i * WAVES + k1 : i * WAVES + k1 + 1, :] for i in range(3))
        damp = 0.5 * (ratio2 / jnp.maximum(here, ratio2) + ratio2 / jnp.maximum(there, ratio2))

        def rows(f):
            return slice(f * BLOCK + k1 * ROWS, f * BLOCK + (k1 + 1) * ROWS)

        across = x_coef * slope * damp
        gain_re = across * spec_ref[rows(UH), imag]
        gain_im = -across * spec_ref[rows(UH), real]
        spec_ref[rows(UH), real] = gain_re
        spec_ref[rows(UH), imag] = gain_im
        mass_re = spec_ref[rows(H), real] + gain_re
        mass_im = spec_ref[rows(H), imag] + gain_im
        scale = damp * coslat
        flux_re = scale * spec_ref[rows(VH), real]
        flux_im = scale * spec_ref[rows(VH), imag]
        spec_ref[rows(VH), real] = flux_re
        spec_ref[rows(VH), imag] = flux_im
        up_ref[k1] = jnp.concatenate([mass_re[7:8], mass_im[7:8], flux_re[6:8], flux_im[6:8], zeros], axis=0)
        down_ref[k1] = jnp.concatenate([mass_re[0:1], mass_im[0:1], flux_re[0:2], flux_im[0:2], zeros], axis=0)


def inverse_kernel(spec_ref, below_ref, above_ref, table_ref, twiddle_ref, wave_ref, row_ref, out_ref, left_ref, right_ref):
    row = row_ref[0]
    ratio2, x_coef, y_coef, rotation = (row[:, i : i + 1] for i in range(4))
    y_below, y_above = row[0:1, 5:6], row[0:1, 6:7]
    spans = (slice(0, WIDE), slice(WIDE, 2 * WIDE))
    for k1 in range(WAVES):
        here, there, slope = (wave_ref[i * WAVES + k1 : i * WAVES + k1 + 1, :] for i in range(3))
        damp = (0.5 * SCALE) * (ratio2 / jnp.maximum(here, ratio2) + ratio2 / jnp.maximum(there, ratio2))

        def rows(f):
            return slice(f * BLOCK + k1 * ROWS, f * BLOCK + (k1 + 1) * ROWS)

        mass = []
        for part, span in enumerate(spans):
            flux = spec_ref[rows(VH), span]
            gain = spec_ref[rows(UH), span]
            mass_below, mass_above = below_ref[k1, part : part + 1, :], above_ref[k1, part : part + 1, :]
            fluxes_below = below_ref[k1, 2 + 2 * part : 4 + 2 * part, :]
            fluxes_above = above_ref[k1, 2 + 2 * part : 4 + 2 * part, :]
            prev = jnp.concatenate([fluxes_below[1:2], flux[:-1]], axis=0)
            following = jnp.concatenate([flux[1:], fluxes_above[0:1]], axis=0)
            change = gain - y_coef * (following - prev)
            new = spec_ref[rows(H), span] + change
            new_below = mass_below - y_below * (flux[0:1] - fluxes_below[0:1])
            new_above = mass_above - y_above * (fluxes_above[1:2] - flux[7:8])
            mass.append(new)
            prev = jnp.concatenate([new_below, new[:-1]], axis=0)
            following = jnp.concatenate([new[1:], new_above], axis=0)
            push = -PUSH_COEF * (following - prev) - rotation * spec_ref[rows(U), span]
            left_ref[rows(2), span] = damp * push
            left_ref[rows(0), span] = SCALE * change
        across = x_coef * slope
        left_ref[rows(1), spans[0]] = damp * (across * mass[1] + rotation * spec_ref[rows(V), spans[0]])
        left_ref[rows(1), spans[1]] = damp * (rotation * spec_ref[rows(V), spans[1]] - across * mass[0])
    right_ref[...] = dot(left_ref[...], table_ref[...], 1)
    first = first_half((ROWS, LANES))
    for f, part, fields in ((0, 0, (1,)), (1, 0, (2,)), (2, 0, (0,)), (3, 1, (1, 2)), (4, 1, (0,))):
        lanes = slice(part * LANES, (part + 1) * LANES)
        late = slice(WIDE + part * LANES, WIDE + (part + 1) * LANES)
        waves = []
        for k1 in range(WAVES):
            cos = twiddle_ref[k1 : k1 + 1, lanes]
            sin = twiddle_ref[WAVES + k1 : WAVES + k1 + 1, lanes]
            spots = [slice(g * BLOCK + k1 * ROWS, g * BLOCK + (k1 + 1) * ROWS) for g in fields]
            re, im = right_ref[spots[0], lanes], right_ref[spots[0], late]
            if len(spots) == 2:
                re = jnp.where(first, re, right_ref[spots[1], lanes])
                im = jnp.where(first, im, right_ref[spots[1], late])
            waves.append((re * cos - im * sin, None if k1 in (0, WAVES - 1) else im * cos + re * sin))
        for a, value in enumerate(real_ifft(waves)):
            at = a * CHUNK + f * ROWS
            if f == 4:
                half = ROWS // 2
                value = jnp.where(first_half((half, LANES)), value[:half], value[half:])
            out_ref[at : at + value.shape[0], :] = value


def in_vmem():
    return pl.BlockSpec(memory_space=pltpu.VMEM)


PARAMS = pltpu.CompilerParams(vmem_limit_bytes=40 * 2**20)


def like(*shape):
    return jax.ShapeDtypeStruct(shape, jnp.float32)


def place(level, r, lat):
    return (level * 16 + (15 - r if lat % 2 else r)) * 16 + lat


def neighbour_pairs(up):
    pairs = []
    for level in range(2):
        for lat in range(16):
            pairs += [(place(level, r, lat), place(level, r + 1, lat)) for r in range(15)]
        pairs += [(place(level, 15, lat), place(level, 0, lat + 1)) for lat in range(15)]
    return pairs if up else [(b, a) for a, b in pairs]


def in_smem():
    return pl.BlockSpec(memory_space=pltpu.SMEM)


def pack(turned, u, v, h):
    return pl.pallas_call(
        pack_kernel,
        out_shape=like(PARTS * CHUNK, LANES),
        in_specs=[in_smem()] + [in_vmem()] * 3,
        out_specs=in_vmem(),
        scratch_shapes=[pltpu.VMEM((LANES, LANES), jnp.float32)],
        compiler_params=PARAMS,
        name="pack",
    )(turned, u, v, h)


def forward(whole, row):
    return pl.pallas_call(
        forward_kernel,
        out_shape=(like(5 * BLOCK, 2 * WIDE), like(WAVES, ROWS, WIDE), like(WAVES, ROWS, WIDE)),
        in_specs=[in_vmem()] * 5,
        out_specs=(in_vmem(),) * 3,
        scratch_shapes=[pltpu.VMEM((5 * BLOCK, 2 * WIDE), jnp.float32)],
        compiler_params=PARAMS,
        name="forward",
    )(whole, dft_table(), twiddle_table(), wave_table(), row)


def inverse(spec, below, above, row):
    return pl.pallas_call(
        inverse_kernel,
        out_shape=like(PARTS * CHUNK, LANES),
        in_specs=[in_vmem()] * 7,
        out_specs=in_vmem(),
        scratch_shapes=[pltpu.VMEM((3 * BLOCK, 2 * WIDE), jnp.float32)] * 2,
        compiler_params=PARAMS,
        name="inverse",
    )(spec, below, above, dft_table(), twiddle_table(), wave_table(), row)


def unpack(turned, back, u, v, h):
    return pl.pallas_call(
        unpack_kernel,
        out_shape=(like(2 * SEG, LANES),) * 3,
        in_specs=[in_smem()] + [in_vmem()] * 4,
        out_specs=(in_vmem(),) * 3,
        scratch_shapes=[pltpu.VMEM((5, LANES, LANES), jnp.float32)],
        compiler_params=PARAMS,
        name="unpack",
    )(turned, back, u, v, h)


def row_of(group):
    return lax.dynamic_slice_in_dim(jnp.asarray(row_table()), group, 1, axis=0)


def exchange(chunks):
    moved = lax.all_to_all(chunks.reshape(PARTS, CHUNK, 1, LANES), "lon", 0, 0, tiled=True)
    return moved.reshape(PARTS * CHUNK, LANES)


def step(u, v, h):
    lat = lax.axis_index("lat")
    turned = lat % 2
    r = lax.axis_index("lon") % 16
    row = row_of(lat * 16 + jnp.where(turned == 1, 15 - r, r))
    turned = turned.reshape(1)
    u, v, h = (jnp.swapaxes(x, 0, 1).reshape(2 * SEG, LANES) for x in (u, v, h))
    spec, up, down = forward(exchange(pack(turned, u, v, h)), row)
    below = lax.ppermute(up, ("lon", "lat"), neighbour_pairs(True))
    above = lax.ppermute(down, ("lon", "lat"), neighbour_pairs(False))
    outs = unpack(turned, exchange(inverse(spec, below, above, row)), u, v, h)
    return tuple(jnp.swapaxes(x.reshape(SEG, 2, LANES), 0, 1) for x in outs)


def solution(mesh):
    spec = P(None, "lon", "lat")
    return jax.shard_map(step, mesh=mesh, in_specs=(spec,) * 3, out_specs=(spec,) * 3, check_vma=False)
```

```python
import functools
import math

import jax
import jax.numpy as jnp
import numpy as np
from jax import lax
from jax.experimental import pallas as pl
from jax.experimental.pallas import tpu as pltpu
from jax.sharding import PartitionSpec as P

NLON = 5760
NLAT = 2048
PARTS = 32
SEG = 180
LANES = 128
TAIL = SEG - LANES
HALF = 64
ROWS = 8
WAVES = PARTS // 2 + 1
WIDE = 2 * LANES
SCALE = 1.0 / NLON
CHUNK = 4 * ROWS + ROWS // 2


def places(half):
    b = np.arange(SEG)
    return np.where(b < LANES, b, b + half * HALF)


def dft_table():
    b = np.arange(SEG)
    angle = (np.outer(b, b) % SEG) * (2.0 * math.pi / SEG)
    cos, sin = np.cos(angle), np.sin(angle)
    table = np.zeros((2 * WIDE, 2 * WIDE))
    for half in (0, 1):
        at = places(half)
        table[np.ix_(at, b)] = cos
        table[np.ix_(at, WIDE + b)] = -sin
        table[np.ix_(WIDE + at, b)] = sin
        table[np.ix_(WIDE + at, WIDE + b)] = cos
    return table.astype(np.float32)


def twiddle_table():
    angle = np.zeros((WAVES, WIDE))
    turn = np.outer(np.arange(WAVES), np.arange(SEG)) * (2.0 * math.pi / NLON)
    for half in (0, 1):
        angle[:, places(half)] = turn
    return np.concatenate([np.cos(angle), np.sin(angle)]).astype(np.float32)


def wave_table():
    k = np.arange(WAVES)[:, None] + PARTS * np.arange(SEG)[None, :]
    step = np.float32(math.pi / NLON)
    here = np.sin(k.astype(np.float32) * step) ** 2
    there = np.sin(((NLON - k) % NLON).astype(np.float32) * step) ** 2
    slope = 2.0 * np.sin(2.0 * math.pi * k / NLON)
    table = np.zeros((3 * WAVES, WIDE), np.float32)
    table[:, :SEG] = np.concatenate([here, there, slope])
    return table


def row_table():
    j = np.arange(-1, NLAT + 1)
    phi = np.float32(-0.5 * math.pi) + (j.astype(np.float32) + np.float32(0.5)) * np.float32(math.pi / NLAT)
    phi = phi.astype(np.float64)
    lat_step, lon_step = math.pi / NLAT, 2.0 * math.pi / NLON
    time_step = 0.25 * lat_step
    cos = np.cos(phi)
    y_coef = time_step / (2.0 * lat_step * cos)
    y_coef[0] = y_coef[-1] = 0.0
    table = np.zeros((NLAT, LANES))
    table[:, 0] = (cos / math.cos(0.25 * math.pi))[1:-1] ** 2
    table[:, 1] = (time_step / (2.0 * lon_step * cos))[1:-1]
    table[:, 2] = y_coef[1:-1]
    table[:, 3] = 0.3 * np.sin(phi)[1:-1]
    table[:, 4] = cos[1:-1]
    table[:, 5] = np.repeat(y_coef[0:NLAT:ROWS], ROWS)
    table[:, 6] = np.repeat(y_coef[ROWS + 1 :: ROWS], ROWS)
    return table.reshape(NLAT // ROWS, ROWS, LANES).astype(np.float32)


PUSH_COEF = 0.25 / 2.0


def add(x, y):
    if x is None:
        return y
    return x if y is None else x + y


def sub(x, y):
    if y is None:
        return x
    return -y if x is None else x - y


def times(z, cos, sin):
    re, im = z
    if abs(sin) < 1e-15:
        return (re * cos, None if im is None else im * cos)
    if im is None:
        return (re * cos, re * sin)
    return (re * cos - im * sin, re * sin + im * cos)


def real_fft(values):
    n = len(values)
    if n == 2:
        return [(values[0] + values[1], None), (values[0] - values[1], None)]
    even, odd = real_fft(values[0::2]), real_fft(values[1::2])
    out = [None] * (n // 2 + 1)
    out[0] = (even[0][0] + odd[0][0], None)
    out[n // 2] = (even[0][0] - odd[0][0], None)
    for k in range(1, n // 4):
        re, im = times(odd[k], math.cos(2 * math.pi * k / n), -math.sin(2 * math.pi * k / n))
        out[k] = (add(even[k][0], re), add(even[k][1], im))
        out[n // 2 - k] = (sub(even[k][0], re), sub(im, even[k][1]))
    out[n // 4] = (even[n // 4][0], -odd[n // 4][0])
    return out


def real_ifft(waves):
    n = 2 * (len(waves) - 1)
    if n == 2:
        return [waves[0][0] + waves[1][0], waves[0][0] - waves[1][0]]
    even, odd = [None] * (n // 4 + 1), [None] * (n // 4 + 1)
    even[0] = (waves[0][0] + waves[n // 2][0], None)
    odd[0] = (waves[0][0] - waves[n // 2][0], None)
    for k in range(1, n // 4):
        (re, im), (far_re, far_im) = waves[k], waves[n // 2 - k]
        even[k] = (re + far_re, im - far_im)
        odd[k] = times((re - far_re, im + far_im), math.cos(2 * math.pi * k / n), math.sin(2 * math.pi * k / n))
    even[n // 4] = (2.0 * waves[n // 4][0], None)
    odd[n // 4] = (-2.0 * waves[n // 4][1], None)
    out = [None] * n
    out[0::2], out[1::2] = real_ifft(even), real_ifft(odd)
    return out


def first_half(shape):
    return lax.broadcasted_iota(jnp.int32, shape, 1) < HALF


def spot(level, r, turned):
    return CHUNK * (level * 16 + (15 - r if turned else r))


def pack_kernel(turn_ref, u_hbm, v_hbm, h_hbm, out_ref, u_ref, v_ref, h_ref, tail_ref, sems):
    moves = [
        pltpu.make_async_copy(src, dst, sems.at[i])
        for i, (src, dst) in enumerate(((u_hbm, u_ref), (v_hbm, v_ref), (h_hbm, h_ref)))
    ]
    for move in moves:
        move.start()
    tail_ref[...] = jnp.zeros_like(tail_ref)
    for move in moves:
        move.wait()
    for level in range(2):
        tiles = [ref[pl.ds(level, LANES, 2), :].T for ref in (u_ref, v_ref, h_ref)]
        for pair in ((u_ref, v_ref), (h_ref, h_ref)):
            for half, ref in enumerate(pair):
                tail_ref[half * HALF : half * HALF + TAIL, :] = ref[pl.ds(2 * LANES + level, TAIL, 2), :]
            tiles.append(tail_ref[...].T)
        for turned in (False, True):

            @pl.when(turn_ref[0] == int(turned))
            def _():
                for r in range(16):
                    at = spot(level, r, turned)
                    for f in range(4):
                        out_ref[at + f * ROWS : at + (f + 1) * ROWS, :] = tiles[f][r * ROWS : (r + 1) * ROWS]
                    low, high = tiles[4][r * ROWS : r * ROWS + 4], tiles[4][r * ROWS + 4 : (r + 1) * ROWS]
                    out_ref[at + 4 * ROWS : at + CHUNK, :] = jnp.where(first_half(low.shape), low, high)


def unpack_kernel(turn_ref, in_ref, u_ref, v_ref, h_ref, u_out, v_out, h_out, tile_ref):
    for level in range(2):
        for turned in (False, True):

            @pl.when(turn_ref[0] == int(turned))
            def _():
                for r in range(16):
                    at = spot(level, r, turned)
                    for f in range(4):
                        tile_ref[f, r * ROWS : (r + 1) * ROWS, :] = in_ref[at + f * ROWS : at + (f + 1) * ROWS, :]
                    tail = in_ref[at + 4 * ROWS : at + CHUNK, :]
                    tile_ref[4, r * ROWS : (r + 1) * ROWS, :] = jnp.concatenate([tail, tail], axis=0)

        tails = tile_ref[3].T, tile_ref[4].T
        early = lax.broadcasted_iota(jnp.int32, (TAIL, LANES), 1) % ROWS < ROWS // 2
        tails = (tails[0][:TAIL], tails[0][HALF : HALF + TAIL], jnp.where(early, tails[1][:TAIL], tails[1][HALF : HALF + TAIL]))
        for f, (ref, out) in enumerate(((u_ref, u_out), (v_ref, v_out), (h_ref, h_out))):
            here = pl.ds(level, LANES, 2)
            out[here, :] = ref[here, :] + tile_ref[f].T
            here = pl.ds(2 * LANES + level, TAIL, 2)
            out[here, :] = ref[here, :] + tails[f]


def halves(x):
    high = x.astype(jnp.bfloat16)
    return high, (x - high.astype(jnp.float32)).astype(jnp.bfloat16)


def dot(x, table, contract):
    def product(a, b):
        return lax.dot_general(a, b, (((1,), (contract,)), ((), ())), preferred_element_type=jnp.float32)

    (high, low), (table_high, table_low) = halves(x), halves(table)
    return product(high, table_high) + (product(high, table_low) + product(low, table_high))


BLOCK = WAVES * ROWS


def padded(fields):
    return -(-fields * BLOCK // 16) * 16


def transform(x_ref, table_ref, twiddle_ref, spec_ref, left_ref, columns):
    first = first_half((ROWS, LANES))
    for get, part, fields in columns:
        lanes = slice(part * LANES, (part + 1) * LANES)
        late = slice(WIDE + part * LANES, WIDE + (part + 1) * LANES)
        for k1, (re, im) in enumerate(real_fft([get(x_ref, a) for a in range(PARTS)])):
            cos = twiddle_ref[k1 : k1 + 1, lanes]
            sin = twiddle_ref[WAVES + k1 : WAVES + k1 + 1, lanes]
            if im is None:
                new_re, new_im = re * cos, -re * sin
            else:
                new_re, new_im = re * cos + im * sin, im * cos - re * sin
            for f, half in fields:
                rows = slice(f * BLOCK + k1 * ROWS, f * BLOCK + (k1 + 1) * ROWS)
                if part == 0:
                    left_ref[rows, lanes], left_ref[rows, late] = new_re, new_im
                else:
                    mine = jnp.logical_not(first) if half else first
                    left_ref[rows, lanes] = jnp.where(mine, new_re, 0.0)
                    left_ref[rows, late] = jnp.where(mine, new_im, 0.0)
    spec_ref[...] = dot(left_ref[...], table_ref[...], 0)


def tile(f):
    def get(x_ref, a):
        at = a * CHUNK + f * ROWS
        return x_ref[at : at + ROWS, :]

    return get


def tail(x_ref, a):
    here = x_ref[a * CHUNK + 4 * ROWS : (a + 1) * CHUNK, :]
    there = pltpu.roll(here, HALF, 1)
    first = first_half(here.shape)
    return jnp.concatenate([jnp.where(first, here, there), jnp.where(first, there, here)], axis=0)


def times_h(get, h):
    return lambda x_ref, a: get(x_ref, a) * h(x_ref, a)


H, UH, VH = range(3)
U, V = range(2)
MASS_COLUMNS = (
    (tile(2), 0, ((H, 0),)),
    (times_h(tile(0), tile(2)), 0, ((UH, 0),)),
    (times_h(tile(1), tile(2)), 0, ((VH, 0),)),
    (tail, 1, ((H, 0),)),
    (times_h(tile(3), tail), 1, ((UH, 0), (VH, 1))),
)
WIND_COLUMNS = ((tile(0), 0, ((U, 0),)), (tile(1), 0, ((V, 0),)), (tile(3), 1, ((U, 0), (V, 1))))


def wind_kernel(x_ref, table_ref, twiddle_ref, spec_ref, left_ref):
    transform(x_ref, table_ref, twiddle_ref, spec_ref, left_ref, WIND_COLUMNS)


def mass_kernel(x_ref, table_ref, twiddle_ref, wave_ref, row_ref, spec_ref, up_ref, down_ref, left_ref):
    transform(x_ref, table_ref, twiddle_ref, spec_ref, left_ref, MASS_COLUMNS)
    row = row_ref[0]
    ratio2, x_coef, coslat = row[:, 0:1], row[:, 1:2], row[:, 4:5]
    real, imag = slice(0, WIDE), slice(WIDE, 2 * WIDE)
    zeros = jnp.zeros((2, WIDE), jnp.float32)
    for k1 in range(WAVES):
        here, there, slope = (wave_ref[i * WAVES + k1 : i * WAVES + k1 + 1, :] for i in range(3))
        damp = 0.5 * (ratio2 / jnp.maximum(here, ratio2) + ratio2 / jnp.maximum(there, ratio2))

        def rows(f):
            return slice(f * BLOCK + k1 * ROWS, f * BLOCK + (k1 + 1) * ROWS)

        across = x_coef * slope * damp
        gain_re = across * spec_ref[rows(UH), imag]
        gain_im = -across * spec_ref[rows(UH), real]
        spec_ref[rows(UH), real] = gain_re
        spec_ref[rows(UH), imag] = gain_im
        mass_re = spec_ref[rows(H), real] + gain_re
        mass_im = spec_ref[rows(H), imag] + gain_im
        scale = damp * coslat
        flux_re = scale * spec_ref[rows(VH), real]
        flux_im = scale * spec_ref[rows(VH), imag]
        spec_ref[rows(VH), real] = flux_re
        spec_ref[rows(VH), imag] = flux_im
        up_ref[k1] = jnp.concatenate([mass_re[7:8], mass_im[7:8], flux_re[6:8], flux_im[6:8], zeros], axis=0)
        down_ref[k1] = jnp.concatenate([mass_re[0:1], mass_im[0:1], flux_re[0:2], flux_im[0:2], zeros], axis=0)


def inverse_kernel(
    spec_ref, wind_ref, below_ref, above_ref, table_ref, twiddle_ref, wave_ref, row_ref, out_ref, left_ref, right_ref
):
    row = row_ref[0]
    ratio2, x_coef, y_coef, rotation = (row[:, i : i + 1] for i in range(4))
    y_below, y_above = row[0:1, 5:6], row[0:1, 6:7]
    spans = (slice(0, WIDE), slice(WIDE, 2 * WIDE))
    for k1 in range(WAVES):
        here, there, slope = (wave_ref[i * WAVES + k1 : i * WAVES + k1 + 1, :] for i in range(3))
        damp = (0.5 * SCALE) * (ratio2 / jnp.maximum(here, ratio2) + ratio2 / jnp.maximum(there, ratio2))

        def rows(f):
            return slice(f * BLOCK + k1 * ROWS, f * BLOCK + (k1 + 1) * ROWS)

        mass = []
        for part, span in enumerate(spans):
            flux = spec_ref[rows(VH), span]
            gain = spec_ref[rows(UH), span]
            mass_below, mass_above = below_ref[k1, part : part + 1, :], above_ref[k1, part : part + 1, :]
            fluxes_below = below_ref[k1, 2 + 2 * part : 4 + 2 * part, :]
            fluxes_above = above_ref[k1, 2 + 2 * part : 4 + 2 * part, :]
            prev = jnp.concatenate([fluxes_below[1:2], flux[:-1]], axis=0)
            following = jnp.concatenate([flux[1:], fluxes_above[0:1]], axis=0)
            change = gain - y_coef * (following - prev)
            new = spec_ref[rows(H), span] + change
            new_below = mass_below - y_below * (flux[0:1] - fluxes_below[0:1])
            new_above = mass_above - y_above * (fluxes_above[1:2] - flux[7:8])
            mass.append(new)
            prev = jnp.concatenate([new_below, new[:-1]], axis=0)
            following = jnp.concatenate([new[1:], new_above], axis=0)
            push = -PUSH_COEF * (following - prev) - rotation * wind_ref[rows(U), span]
            left_ref[rows(2), span] = damp * push
            left_ref[rows(0), span] = SCALE * change
        across = x_coef * slope
        left_ref[rows(1), spans[0]] = damp * (across * mass[1] + rotation * wind_ref[rows(V), spans[0]])
        left_ref[rows(1), spans[1]] = damp * (rotation * wind_ref[rows(V), spans[1]] - across * mass[0])
    right_ref[...] = dot(left_ref[...], table_ref[...], 1)
    first = first_half((ROWS, LANES))
    for f, part, fields in ((0, 0, (1,)), (1, 0, (2,)), (2, 0, (0,)), (3, 1, (1, 2)), (4, 1, (0,))):
        lanes = slice(part * LANES, (part + 1) * LANES)
        late = slice(WIDE + part * LANES, WIDE + (part + 1) * LANES)
        waves = []
        for k1 in range(WAVES):
            cos = twiddle_ref[k1 : k1 + 1, lanes]
            sin = twiddle_ref[WAVES + k1 : WAVES + k1 + 1, lanes]
            spots = [slice(g * BLOCK + k1 * ROWS, g * BLOCK + (k1 + 1) * ROWS) for g in fields]
            re, im = right_ref[spots[0], lanes], right_ref[spots[0], late]
            if len(spots) == 2:
                re = jnp.where(first, re, right_ref[spots[1], lanes])
                im = jnp.where(first, im, right_ref[spots[1], late])
            waves.append((re * cos - im * sin, None if k1 in (0, WAVES - 1) else im * cos + re * sin))
        for a, value in enumerate(real_ifft(waves)):
            at = a * CHUNK + f * ROWS
            if f == 4:
                half = ROWS // 2
                value = jnp.where(first_half((half, LANES)), value[:half], value[half:])
            out_ref[at : at + value.shape[0], :] = value


def in_vmem():
    return pl.BlockSpec(memory_space=pltpu.VMEM)


PARAMS = pltpu.CompilerParams(vmem_limit_bytes=40 * 2**20)


def like(*shape):
    return jax.ShapeDtypeStruct(shape, jnp.float32)


def place(level, r, lat):
    return (level * 16 + (15 - r if lat % 2 else r)) * 16 + lat


def neighbour_pairs(up):
    pairs = []
    for level in range(2):
        for lat in range(16):
            pairs += [(place(level, r, lat), place(level, r + 1, lat)) for r in range(15)]
        pairs += [(place(level, 15, lat), place(level, 0, lat + 1)) for lat in range(15)]
    return pairs if up else [(b, a) for a, b in pairs]


def in_smem():
    return pl.BlockSpec(memory_space=pltpu.SMEM)


def pack(turned, u, v, h):
    return pl.pallas_call(
        pack_kernel,
        out_shape=like(PARTS * CHUNK, LANES),
        in_specs=[in_smem()] + [pl.BlockSpec(memory_space=pltpu.HBM)] * 3,
        out_specs=in_vmem(),
        scratch_shapes=[pltpu.VMEM((2 * SEG, LANES), jnp.float32)] * 3
        + [pltpu.VMEM((LANES, LANES), jnp.float32), pltpu.SemaphoreType.DMA((3,))],
        compiler_params=pltpu.CompilerParams(vmem_limit_bytes=56 * 2**20),
        name="pack",
    )(turned, u, v, h)


def cost(fields):
    size = padded(fields) * 2 * WIDE
    return pl.CostEstimate(flops=6 * size * 2 * WIDE, bytes_accessed=8 * size, transcendentals=0)


def forward_mass(whole, row):
    return pl.pallas_call(
        mass_kernel,
        out_shape=(like(padded(3), 2 * WIDE), like(WAVES, ROWS, WIDE), like(WAVES, ROWS, WIDE)),
        in_specs=[in_vmem()] * 5,
        out_specs=(in_vmem(),) * 3,
        scratch_shapes=[pltpu.VMEM((padded(3), 2 * WIDE), jnp.float32)],
        compiler_params=PARAMS,
        cost_estimate=cost(3),
        name="forward_mass",
    )(whole, dft_table(), twiddle_table(), wave_table(), row)


def forward_wind(whole):
    return pl.pallas_call(
        wind_kernel,
        out_shape=like(padded(2), 2 * WIDE),
        in_specs=[in_vmem()] * 3,
        out_specs=in_vmem(),
        scratch_shapes=[pltpu.VMEM((padded(2), 2 * WIDE), jnp.float32)],
        compiler_params=PARAMS,
        cost_estimate=cost(2),
        name="forward_wind",
    )(whole, dft_table(), twiddle_table())


def inverse(spec, wind, below, above, row):
    return pl.pallas_call(
        inverse_kernel,
        out_shape=like(PARTS * CHUNK, LANES),
        in_specs=[in_vmem()] * 8,
        out_specs=in_vmem(),
        scratch_shapes=[pltpu.VMEM((padded(3), 2 * WIDE), jnp.float32)] * 2,
        compiler_params=PARAMS,
        cost_estimate=cost(3),
        name="inverse",
    )(spec, wind, below, above, dft_table(), twiddle_table(), wave_table(), row)


def unpack(turned, back, u, v, h):
    return pl.pallas_call(
        unpack_kernel,
        out_shape=(like(2 * SEG, LANES),) * 3,
        in_specs=[in_smem()] + [in_vmem()] * 4,
        out_specs=(in_vmem(),) * 3,
        scratch_shapes=[pltpu.VMEM((5, LANES, LANES), jnp.float32)],
        compiler_params=PARAMS,
        name="unpack",
    )(turned, back, u, v, h)


def row_of(group):
    return lax.dynamic_slice_in_dim(jnp.asarray(row_table()), group, 1, axis=0)


def exchange(chunks):
    moved = lax.all_to_all(chunks.reshape(PARTS, CHUNK, 1, LANES), "lon", 0, 0, tiled=True)
    return moved.reshape(PARTS * CHUNK, LANES)


def step(u, v, h):
    lat = lax.axis_index("lat")
    turned = lat % 2
    r = lax.axis_index("lon") % 16
    row = row_of(lat * 16 + jnp.where(turned == 1, 15 - r, r))
    turned = turned.reshape(1)
    u, v, h = (jnp.swapaxes(x, 0, 1).reshape(2 * SEG, LANES) for x in (u, v, h))
    whole = exchange(pack(turned, u, v, h))
    spec, up, down = forward_mass(whole, row)
    below = lax.ppermute(up, ("lon", "lat"), neighbour_pairs(True))
    above = lax.ppermute(down, ("lon", "lat"), neighbour_pairs(False))
    wind = forward_wind(whole)
    outs = unpack(turned, exchange(inverse(spec, wind, below, above, row)), u, v, h)
    return tuple(jnp.swapaxes(x.reshape(SEG, 2, LANES), 0, 1) for x in outs)


def solution(mesh):
    spec = P(None, "lon", "lat")
    return jax.shard_map(step, mesh=mesh, in_specs=(spec,) * 3, out_specs=(spec,) * 3, check_vma=False)
```

```python
import functools
import math

import jax
import jax.numpy as jnp
import numpy as np
from jax import lax
from jax.experimental import pallas as pl
from jax.experimental.pallas import tpu as pltpu
from jax.sharding import PartitionSpec as P

NLON = 5760
NLAT = 2048
PARTS = 32
SEG = 180
LANES = 128
TAIL = SEG - LANES
HALF = 64
ROWS = 8
WAVES = PARTS // 2 + 1
WIDE = 2 * LANES
SCALE = 1.0 / NLON
CHUNK = 4 * ROWS + ROWS // 2


def places(half):
    b = np.arange(SEG)
    return np.where(b < LANES, b, b + half * HALF)


def dft_table():
    b = np.arange(SEG)
    angle = (np.outer(b, b) % SEG) * (2.0 * math.pi / SEG)
    cos, sin = np.cos(angle), np.sin(angle)
    table = np.zeros((2 * WIDE, 2 * WIDE))
    for half in (0, 1):
        at = places(half)
        table[np.ix_(at, b)] = cos
        table[np.ix_(at, WIDE + b)] = -sin
        table[np.ix_(WIDE + at, b)] = sin
        table[np.ix_(WIDE + at, WIDE + b)] = cos
    return table.astype(np.float32)


def twiddle_table():
    angle = np.zeros((WAVES, WIDE))
    turn = np.outer(np.arange(WAVES), np.arange(SEG)) * (2.0 * math.pi / NLON)
    for half in (0, 1):
        angle[:, places(half)] = turn
    return np.concatenate([np.cos(angle), np.sin(angle)]).astype(np.float32)


def wave_table():
    k = np.arange(WAVES)[:, None] + PARTS * np.arange(SEG)[None, :]
    step = np.float32(math.pi / NLON)
    here = np.sin(k.astype(np.float32) * step) ** 2
    there = np.sin(((NLON - k) % NLON).astype(np.float32) * step) ** 2
    slope = 2.0 * np.sin(2.0 * math.pi * k / NLON)
    table = np.zeros((3 * WAVES, WIDE), np.float32)
    table[:, :SEG] = np.concatenate([here, there, slope])
    return table


def row_table():
    j = np.arange(-1, NLAT + 1)
    phi = np.float32(-0.5 * math.pi) + (j.astype(np.float32) + np.float32(0.5)) * np.float32(math.pi / NLAT)
    phi = phi.astype(np.float64)
    lat_step, lon_step = math.pi / NLAT, 2.0 * math.pi / NLON
    time_step = 0.25 * lat_step
    cos = np.cos(phi)
    y_coef = time_step / (2.0 * lat_step * cos)
    y_coef[0] = y_coef[-1] = 0.0
    table = np.zeros((NLAT, LANES))
    table[:, 0] = (cos / math.cos(0.25 * math.pi))[1:-1] ** 2
    table[:, 1] = (time_step / (2.0 * lon_step * cos))[1:-1]
    table[:, 2] = y_coef[1:-1]
    table[:, 3] = 0.3 * np.sin(phi)[1:-1]
    table[:, 4] = cos[1:-1]
    table[:, 5] = np.repeat(y_coef[0:NLAT:ROWS], ROWS)
    table[:, 6] = np.repeat(y_coef[ROWS + 1 :: ROWS], ROWS)
    table[:, 7] = np.arange(NLAT) // ROWS % 2
    return table.reshape(NLAT // ROWS, ROWS, LANES).astype(np.float32)


PUSH_COEF = 0.25 / 2.0


def add(x, y):
    if x is None:
        return y
    return x if y is None else x + y


def sub(x, y):
    if y is None:
        return x
    return -y if x is None else x - y


def times(z, cos, sin):
    re, im = z
    if abs(sin) < 1e-15:
        return (re * cos, None if im is None else im * cos)
    if im is None:
        return (re * cos, re * sin)
    return (re * cos - im * sin, re * sin + im * cos)


def real_fft(values):
    n = len(values)
    if n == 2:
        return [(values[0] + values[1], None), (values[0] - values[1], None)]
    even, odd = real_fft(values[0::2]), real_fft(values[1::2])
    out = [None] * (n // 2 + 1)
    out[0] = (even[0][0] + odd[0][0], None)
    out[n // 2] = (even[0][0] - odd[0][0], None)
    for k in range(1, n // 4):
        re, im = times(odd[k], math.cos(2 * math.pi * k / n), -math.sin(2 * math.pi * k / n))
        out[k] = (add(even[k][0], re), add(even[k][1], im))
        out[n // 2 - k] = (sub(even[k][0], re), sub(im, even[k][1]))
    out[n // 4] = (even[n // 4][0], -odd[n // 4][0])
    return out


def real_ifft(waves):
    n = 2 * (len(waves) - 1)
    if n == 2:
        return [waves[0][0] + waves[1][0], waves[0][0] - waves[1][0]]
    even, odd = [None] * (n // 4 + 1), [None] * (n // 4 + 1)
    even[0] = (waves[0][0] + waves[n // 2][0], None)
    odd[0] = (waves[0][0] - waves[n // 2][0], None)
    for k in range(1, n // 4):
        (re, im), (far_re, far_im) = waves[k], waves[n // 2 - k]
        even[k] = (re + far_re, im - far_im)
        odd[k] = times((re - far_re, im + far_im), math.cos(2 * math.pi * k / n), math.sin(2 * math.pi * k / n))
    even[n // 4] = (2.0 * waves[n // 4][0], None)
    odd[n // 4] = (-2.0 * waves[n // 4][1], None)
    out = [None] * n
    out[0::2], out[1::2] = real_ifft(even), real_ifft(odd)
    return out


def first_half(shape):
    return lax.broadcasted_iota(jnp.int32, shape, 1) < HALF


def spot(level, r, turned):
    return CHUNK * (level * 16 + (15 - r if turned else r))


def pack_kernel(turn_ref, u_hbm, v_hbm, h_hbm, out_ref, u_ref, v_ref, h_ref, tail_ref, sems):
    moves = [
        pltpu.make_async_copy(src, dst, sems.at[i])
        for i, (src, dst) in enumerate(((u_hbm, u_ref), (v_hbm, v_ref), (h_hbm, h_ref)))
    ]
    for move in moves:
        move.start()
    tail_ref[...] = jnp.zeros_like(tail_ref)
    for move in moves:
        move.wait()
    for level in range(2):
        tiles = [ref[pl.ds(level, LANES, 2), :].T for ref in (u_ref, v_ref, h_ref)]
        for pair in ((u_ref, v_ref), (h_ref, h_ref)):
            for half, ref in enumerate(pair):
                tail_ref[half * HALF : half * HALF + TAIL, :] = ref[pl.ds(2 * LANES + level, TAIL, 2), :]
            tiles.append(tail_ref[...].T)
        for turned in (False, True):

            @pl.when(turn_ref[0] == int(turned))
            def _():
                for r in range(16):
                    at = spot(level, r, turned)
                    for f in range(4):
                        out_ref[at + f * ROWS : at + (f + 1) * ROWS, :] = tiles[f][r * ROWS : (r + 1) * ROWS]
                    low, high = tiles[4][r * ROWS : r * ROWS + 4], tiles[4][r * ROWS + 4 : (r + 1) * ROWS]
                    out_ref[at + 4 * ROWS : at + CHUNK, :] = jnp.where(first_half(low.shape), low, high)


def unpack_kernel(turn_ref, in_ref, u_ref, v_ref, h_ref, u_out, v_out, h_out, tile_ref):
    for level in range(2):
        for turned in (False, True):

            @pl.when(turn_ref[0] == int(turned))
            def _():
                for r in range(16):
                    at = spot(level, r, turned)
                    for f in range(4):
                        tile_ref[f, r * ROWS : (r + 1) * ROWS, :] = in_ref[at + f * ROWS : at + (f + 1) * ROWS, :]
                    tail = in_ref[at + 4 * ROWS : at + CHUNK, :]
                    tile_ref[4, r * ROWS : (r + 1) * ROWS, :] = jnp.concatenate([tail, tail], axis=0)

        tails = tile_ref[3].T, tile_ref[4].T
        early = lax.broadcasted_iota(jnp.int32, (TAIL, LANES), 1) % ROWS < ROWS // 2
        tails = (tails[0][:TAIL], tails[0][HALF : HALF + TAIL], jnp.where(early, tails[1][:TAIL], tails[1][HALF : HALF + TAIL]))
        for f, (ref, out) in enumerate(((u_ref, u_out), (v_ref, v_out), (h_ref, h_out))):
            here = pl.ds(level, LANES, 2)
            out[here, :] = ref[here, :] + tile_ref[f].T
            here = pl.ds(2 * LANES + level, TAIL, 2)
            out[here, :] = ref[here, :] + tails[f]


def halves(x):
    high = x.astype(jnp.bfloat16)
    return high, (x - high.astype(jnp.float32)).astype(jnp.bfloat16)


def dot(x, table, contract):
    def product(a, b):
        return lax.dot_general(a, b, (((1,), (contract,)), ((), ())), preferred_element_type=jnp.float32)

    (high, low), (table_high, table_low) = halves(x), halves(table)
    return product(high, table_high) + (product(high, table_low) + product(low, table_high))


BLOCK = WAVES * ROWS


def padded(fields):
    return -(-fields * BLOCK // 16) * 16


def transform(x_ref, table_ref, twiddle_ref, spec_ref, left_ref, columns):
    first = first_half((ROWS, LANES))
    for get, part, fields in columns:
        lanes = slice(part * LANES, (part + 1) * LANES)
        late = slice(WIDE + part * LANES, WIDE + (part + 1) * LANES)
        for k1, (re, im) in enumerate(real_fft([get(x_ref, a) for a in range(PARTS)])):
            cos = twiddle_ref[k1 : k1 + 1, lanes]
            sin = twiddle_ref[WAVES + k1 : WAVES + k1 + 1, lanes]
            if im is None:
                new_re, new_im = re * cos, -re * sin
            else:
                new_re, new_im = re * cos + im * sin, im * cos - re * sin
            for f, half in fields:
                rows = slice(f * BLOCK + k1 * ROWS, f * BLOCK + (k1 + 1) * ROWS)
                if part == 0:
                    left_ref[rows, lanes], left_ref[rows, late] = new_re, new_im
                else:
                    mine = jnp.logical_not(first) if half else first
                    left_ref[rows, lanes] = jnp.where(mine, new_re, 0.0)
                    left_ref[rows, late] = jnp.where(mine, new_im, 0.0)
    spec_ref[...] = dot(left_ref[...], table_ref[...], 0)


def tile(f):
    def get(x_ref, a):
        at = a * CHUNK + f * ROWS
        return x_ref[at : at + ROWS, :]

    return get


def tail(x_ref, a):
    here = x_ref[a * CHUNK + 4 * ROWS : (a + 1) * CHUNK, :]
    there = pltpu.roll(here, HALF, 1)
    first = first_half(here.shape)
    return jnp.concatenate([jnp.where(first, here, there), jnp.where(first, there, here)], axis=0)


def times_h(get, h):
    return lambda x_ref, a: get(x_ref, a) * h(x_ref, a)


H, UH, VH = range(3)
U, V = range(2)
MASS_COLUMNS = (
    (tile(2), 0, ((H, 0),)),
    (times_h(tile(0), tile(2)), 0, ((UH, 0),)),
    (times_h(tile(1), tile(2)), 0, ((VH, 0),)),
    (tail, 1, ((H, 0),)),
    (times_h(tile(3), tail), 1, ((UH, 0), (VH, 1))),
)
WIND_COLUMNS = ((tile(0), 0, ((U, 0),)), (tile(1), 0, ((V, 0),)), (tile(3), 1, ((U, 0), (V, 1))))


def wind_kernel(x_ref, table_ref, twiddle_ref, spec_ref, left_ref):
    transform(x_ref, table_ref, twiddle_ref, spec_ref, left_ref, WIND_COLUMNS)


def mass_kernel(x_ref, table_ref, twiddle_ref, wave_ref, row_ref, spec_ref, near_ref, far_ref, left_ref):
    transform(x_ref, table_ref, twiddle_ref, spec_ref, left_ref, MASS_COLUMNS)
    row = row_ref[0]
    ratio2, x_coef, coslat = row[:, 0:1], row[:, 1:2], row[:, 4:5]
    real, imag = slice(0, WIDE), slice(WIDE, 2 * WIDE)
    zeros = jnp.zeros((2, WIDE), jnp.float32)
    odd = row[:, 7:8] > 0.5
    for k1 in range(WAVES):
        here, there, slope = (wave_ref[i * WAVES + k1 : i * WAVES + k1 + 1, :] for i in range(3))
        damp = 0.5 * (ratio2 / jnp.maximum(here, ratio2) + ratio2 / jnp.maximum(there, ratio2))

        def rows(f):
            return slice(f * BLOCK + k1 * ROWS, f * BLOCK + (k1 + 1) * ROWS)

        across = x_coef * slope * damp
        gain_re = across * spec_ref[rows(UH), imag]
        gain_im = -across * spec_ref[rows(UH), real]
        spec_ref[rows(UH), real] = gain_re
        spec_ref[rows(UH), imag] = gain_im
        mass_re = spec_ref[rows(H), real] + gain_re
        mass_im = spec_ref[rows(H), imag] + gain_im
        scale = damp * coslat
        flux_re = scale * spec_ref[rows(VH), real]
        flux_im = scale * spec_ref[rows(VH), imag]
        spec_ref[rows(VH), real] = flux_re
        spec_ref[rows(VH), imag] = flux_im
        up = jnp.concatenate([mass_re[7:8], mass_im[7:8], flux_re[6:8], flux_im[6:8], zeros], axis=0)
        down = jnp.concatenate([mass_re[0:1], mass_im[0:1], flux_re[0:2], flux_im[0:2], zeros], axis=0)
        near_ref[k1] = jnp.where(odd, down, up)
        far_ref[k1] = jnp.where(odd, up, down)


def inverse_kernel(
    spec_ref, wind_ref, near_ref, far_ref, table_ref, twiddle_ref, wave_ref, row_ref, out_ref, left_ref, right_ref
):
    row = row_ref[0]
    ratio2, x_coef, y_coef, rotation = (row[:, i : i + 1] for i in range(4))
    y_below, y_above = row[0:1, 5:6], row[0:1, 6:7]
    odd = row[:, 7:8] > 0.5
    spans = (slice(0, WIDE), slice(WIDE, 2 * WIDE))
    for k1 in range(WAVES):
        here, there, slope = (wave_ref[i * WAVES + k1 : i * WAVES + k1 + 1, :] for i in range(3))
        damp = (0.5 * SCALE) * (ratio2 / jnp.maximum(here, ratio2) + ratio2 / jnp.maximum(there, ratio2))

        def rows(f):
            return slice(f * BLOCK + k1 * ROWS, f * BLOCK + (k1 + 1) * ROWS)

        mass = []
        below = jnp.where(odd, near_ref[k1], far_ref[k1])
        above = jnp.where(odd, far_ref[k1], near_ref[k1])
        for part, span in enumerate(spans):
            flux = spec_ref[rows(VH), span]
            gain = spec_ref[rows(UH), span]
            mass_below, mass_above = below[part : part + 1], above[part : part + 1]
            fluxes_below, fluxes_above = below[2 + 2 * part : 4 + 2 * part], above[2 + 2 * part : 4 + 2 * part]
            prev = jnp.concatenate([fluxes_below[1:2], flux[:-1]], axis=0)
            following = jnp.concatenate([flux[1:], fluxes_above[0:1]], axis=0)
            change = gain - y_coef * (following - prev)
            new = spec_ref[rows(H), span] + change
            new_below = mass_below - y_below * (flux[0:1] - fluxes_below[0:1])
            new_above = mass_above - y_above * (fluxes_above[1:2] - flux[7:8])
            mass.append(new)
            prev = jnp.concatenate([new_below, new[:-1]], axis=0)
            following = jnp.concatenate([new[1:], new_above], axis=0)
            push = -PUSH_COEF * (following - prev) - rotation * wind_ref[rows(U), span]
            left_ref[rows(2), span] = damp * push
            left_ref[rows(0), span] = SCALE * change
        across = x_coef * slope
        left_ref[rows(1), spans[0]] = damp * (across * mass[1] + rotation * wind_ref[rows(V), spans[0]])
        left_ref[rows(1), spans[1]] = damp * (rotation * wind_ref[rows(V), spans[1]] - across * mass[0])
    right_ref[...] = dot(left_ref[...], table_ref[...], 1)
    first = first_half((ROWS, LANES))
    for f, part, fields in ((0, 0, (1,)), (1, 0, (2,)), (2, 0, (0,)), (3, 1, (1, 2)), (4, 1, (0,))):
        lanes = slice(part * LANES, (part + 1) * LANES)
        late = slice(WIDE + part * LANES, WIDE + (part + 1) * LANES)
        waves = []
        for k1 in range(WAVES):
            cos = twiddle_ref[k1 : k1 + 1, lanes]
            sin = twiddle_ref[WAVES + k1 : WAVES + k1 + 1, lanes]
            spots = [slice(g * BLOCK + k1 * ROWS, g * BLOCK + (k1 + 1) * ROWS) for g in fields]
            re, im = right_ref[spots[0], lanes], right_ref[spots[0], late]
            if len(spots) == 2:
                re = jnp.where(first, re, right_ref[spots[1], lanes])
                im = jnp.where(first, im, right_ref[spots[1], late])
            waves.append((re * cos - im * sin, None if k1 in (0, WAVES - 1) else im * cos + re * sin))
        for a, value in enumerate(real_ifft(waves)):
            at = a * CHUNK + f * ROWS
            if f == 4:
                half = ROWS // 2
                value = jnp.where(first_half((half, LANES)), value[:half], value[half:])
            out_ref[at : at + value.shape[0], :] = value


def in_vmem():
    return pl.BlockSpec(memory_space=pltpu.VMEM)


PARAMS = pltpu.CompilerParams(vmem_limit_bytes=40 * 2**20)


def like(*shape):
    return jax.ShapeDtypeStruct(shape, jnp.float32)


def place(level, r, lat):
    return (level * 16 + (15 - r if lat % 2 else r)) * 16 + lat


def swaps(odd):
    pairs = []
    for level in range(2):
        for lat in range(16):
            pairs += [(place(level, r, lat), place(level, r + 1, lat)) for r in range(odd, 15, 2)]
            if odd and lat < 15:
                pairs.append((place(level, 15, lat), place(level, 0, lat + 1)))
    return pairs + [(b, a) for a, b in pairs]


def in_smem():
    return pl.BlockSpec(memory_space=pltpu.SMEM)


def pack(turned, u, v, h):
    return pl.pallas_call(
        pack_kernel,
        out_shape=like(PARTS * CHUNK, LANES),
        in_specs=[in_smem()] + [pl.BlockSpec(memory_space=pltpu.HBM)] * 3,
        out_specs=in_vmem(),
        scratch_shapes=[pltpu.VMEM((2 * SEG, LANES), jnp.float32)] * 3
        + [pltpu.VMEM((LANES, LANES), jnp.float32), pltpu.SemaphoreType.DMA((3,))],
        compiler_params=pltpu.CompilerParams(vmem_limit_bytes=56 * 2**20),
        name="pack",
    )(turned, u, v, h)


def cost(fields):
    size = padded(fields) * 2 * WIDE
    return pl.CostEstimate(flops=6 * size * 2 * WIDE, bytes_accessed=8 * size, transcendentals=0)


def forward_mass(whole, row):
    return pl.pallas_call(
        mass_kernel,
        out_shape=(like(padded(3), 2 * WIDE), like(WAVES, ROWS, WIDE), like(WAVES, ROWS, WIDE)),
        in_specs=[in_vmem()] * 5,
        out_specs=(in_vmem(),) * 3,
        scratch_shapes=[pltpu.VMEM((padded(3), 2 * WIDE), jnp.float32)],
        compiler_params=PARAMS,
        cost_estimate=cost(3),
        name="forward_mass",
    )(whole, dft_table(), twiddle_table(), wave_table(), row)


def forward_wind(whole):
    return pl.pallas_call(
        wind_kernel,
        out_shape=like(padded(2), 2 * WIDE),
        in_specs=[in_vmem()] * 3,
        out_specs=in_vmem(),
        scratch_shapes=[pltpu.VMEM((padded(2), 2 * WIDE), jnp.float32)],
        compiler_params=PARAMS,
        cost_estimate=cost(2),
        name="forward_wind",
    )(whole, dft_table(), twiddle_table())


def inverse(spec, wind, near, far, row):
    return pl.pallas_call(
        inverse_kernel,
        out_shape=like(PARTS * CHUNK, LANES),
        in_specs=[in_vmem()] * 8,
        out_specs=in_vmem(),
        scratch_shapes=[pltpu.VMEM((padded(3), 2 * WIDE), jnp.float32)] * 2,
        compiler_params=PARAMS,
        cost_estimate=cost(3),
        name="inverse",
    )(spec, wind, near, far, dft_table(), twiddle_table(), wave_table(), row)


def unpack(turned, back, u, v, h):
    return pl.pallas_call(
        unpack_kernel,
        out_shape=(like(2 * SEG, LANES),) * 3,
        in_specs=[in_smem()] + [in_vmem()] * 4,
        out_specs=(in_vmem(),) * 3,
        scratch_shapes=[pltpu.VMEM((5, LANES, LANES), jnp.float32)],
        compiler_params=PARAMS,
        name="unpack",
    )(turned, back, u, v, h)


def row_of(group):
    return lax.dynamic_slice_in_dim(jnp.asarray(row_table()), group, 1, axis=0)


def exchange(chunks):
    moved = lax.all_to_all(chunks.reshape(PARTS, CHUNK, 1, LANES), "lon", 0, 0, tiled=True)
    return moved.reshape(PARTS * CHUNK, LANES)


def step(u, v, h):
    lat = lax.axis_index("lat")
    turned = lat % 2
    r = lax.axis_index("lon") % 16
    row = row_of(lat * 16 + jnp.where(turned == 1, 15 - r, r))
    turned = turned.reshape(1)
    u, v, h = (jnp.swapaxes(x, 0, 1).reshape(2 * SEG, LANES) for x in (u, v, h))
    whole = exchange(pack(turned, u, v, h))
    spec, near, far = forward_mass(whole, row)
    near = lax.ppermute(near, ("lon", "lat"), swaps(0))
    far = lax.ppermute(far, ("lon", "lat"), swaps(1))
    wind = forward_wind(whole)
    outs = unpack(turned, exchange(inverse(spec, wind, near, far, row)), u, v, h)
    return tuple(jnp.swapaxes(x.reshape(SEG, 2, LANES), 0, 1) for x in outs)


def solution(mesh):
    spec = P(None, "lon", "lat")
    return jax.shard_map(step, mesh=mesh, in_specs=(spec,) * 3, out_specs=(spec,) * 3, check_vma=False)
```

```python
import functools
import math

import jax
import jax.numpy as jnp
import numpy as np
from jax import lax
from jax.experimental import pallas as pl
from jax.experimental.pallas import tpu as pltpu
from jax.sharding import PartitionSpec as P

NLON = 5760
NLAT = 2048
PARTS = 32
SEG = 180
LANES = 128
TAIL = SEG - LANES
HALF = 64
ROWS = 8
WAVES = PARTS // 2 + 1
WIDE = 2 * LANES
SCALE = 1.0 / NLON
SIDE = HALF - TAIL
LAST = TAIL - 2 * SIDE
QUARTER = 32
CHUNK = 4 * ROWS + 2


def placed():
    b = np.arange(SEG)
    tail, side = b[LANES:], LANES + SIDE
    last = np.concatenate([b[-LAST:], np.full(QUARTER - LAST, -1)])
    return np.concatenate([b[:LANES], tail, b[LANES:side], tail, b[side : side + SIDE], np.tile(last, 4)])


def dft_table():
    b = placed()
    angle = (np.outer(b, np.arange(SEG)) % SEG) * (2.0 * math.pi / SEG)
    cos, sin = np.cos(angle) * (b >= 0)[:, None], np.sin(angle) * (b >= 0)[:, None]
    table = np.zeros((6 * LANES, 2 * WIDE))
    for to, (re, im) in ((slice(0, SEG), (cos, sin)), (slice(WIDE, WIDE + SEG), (-sin, cos))):
        table[:WIDE, to], table[WIDE : 2 * WIDE, to] = re[:WIDE], im[:WIDE]
        table[2 * WIDE : 2 * WIDE + LANES, to], table[2 * WIDE + LANES :, to] = re[WIDE:], im[WIDE:]
    return table.astype(np.float32)


def twiddle_table():
    angle = np.outer(np.arange(WAVES), placed()) * (2.0 * math.pi / NLON)
    return np.concatenate([np.cos(angle), np.sin(angle)]).astype(np.float32)


def wave_table():
    k = np.arange(WAVES)[:, None] + PARTS * np.arange(SEG)[None, :]
    step = np.float32(math.pi / NLON)
    here = np.sin(k.astype(np.float32) * step) ** 2
    there = np.sin(((NLON - k) % NLON).astype(np.float32) * step) ** 2
    slope = 2.0 * np.sin(2.0 * math.pi * k / NLON)
    table = np.zeros((3 * WAVES, WIDE), np.float32)
    table[:, :SEG] = np.concatenate([here, there, slope])
    return table


def row_table():
    j = np.arange(-1, NLAT + 1)
    phi = np.float32(-0.5 * math.pi) + (j.astype(np.float32) + np.float32(0.5)) * np.float32(math.pi / NLAT)
    phi = phi.astype(np.float64)
    lat_step, lon_step = math.pi / NLAT, 2.0 * math.pi / NLON
    time_step = 0.25 * lat_step
    cos = np.cos(phi)
    y_coef = time_step / (2.0 * lat_step * cos)
    y_coef[0] = y_coef[-1] = 0.0
    table = np.zeros((NLAT, LANES))
    table[:, 0] = (cos / math.cos(0.25 * math.pi))[1:-1] ** 2
    table[:, 1] = (time_step / (2.0 * lon_step * cos))[1:-1]
    table[:, 2] = y_coef[1:-1]
    table[:, 3] = 0.3 * np.sin(phi)[1:-1]
    table[:, 4] = cos[1:-1]
    table[:, 5] = np.repeat(y_coef[0:NLAT:ROWS], ROWS)
    table[:, 6] = np.repeat(y_coef[ROWS + 1 :: ROWS], ROWS)
    table[:, 7] = np.arange(NLAT) // ROWS % 2
    return table.reshape(NLAT // ROWS, ROWS, LANES).astype(np.float32)


PUSH_COEF = 0.25 / 2.0


def add(x, y):
    if x is None:
        return y
    return x if y is None else x + y


def sub(x, y):
    if y is None:
        return x
    return -y if x is None else x - y


def times(z, cos, sin):
    re, im = z
    if abs(sin) < 1e-15:
        return (re * cos, None if im is None else im * cos)
    if im is None:
        return (re * cos, re * sin)
    return (re * cos - im * sin, re * sin + im * cos)


def real_fft(values):
    n = len(values)
    if n == 2:
        return [(values[0] + values[1], None), (values[0] - values[1], None)]
    even, odd = real_fft(values[0::2]), real_fft(values[1::2])
    out = [None] * (n // 2 + 1)
    out[0] = (even[0][0] + odd[0][0], None)
    out[n // 2] = (even[0][0] - odd[0][0], None)
    for k in range(1, n // 4):
        re, im = times(odd[k], math.cos(2 * math.pi * k / n), -math.sin(2 * math.pi * k / n))
        out[k] = (add(even[k][0], re), add(even[k][1], im))
        out[n // 2 - k] = (sub(even[k][0], re), sub(im, even[k][1]))
    out[n // 4] = (even[n // 4][0], -odd[n // 4][0])
    return out


def real_ifft(waves):
    n = 2 * (len(waves) - 1)
    if n == 2:
        return [waves[0][0] + waves[1][0], waves[0][0] - waves[1][0]]
    even, odd = [None] * (n // 4 + 1), [None] * (n // 4 + 1)
    even[0] = (waves[0][0] + waves[n // 2][0], None)
    odd[0] = (waves[0][0] - waves[n // 2][0], None)
    for k in range(1, n // 4):
        (re, im), (far_re, far_im) = waves[k], waves[n // 2 - k]
        even[k] = (re + far_re, im - far_im)
        odd[k] = times((re - far_re, im + far_im), math.cos(2 * math.pi * k / n), math.sin(2 * math.pi * k / n))
    even[n // 4] = (2.0 * waves[n // 4][0], None)
    odd[n // 4] = (-2.0 * waves[n // 4][1], None)
    out = [None] * n
    out[0::2], out[1::2] = real_ifft(even), real_ifft(odd)
    return out


def lane(shape):
    return lax.broadcasted_iota(jnp.int32, shape, 1)


def own_quarter(shape):
    return lane(shape) // QUARTER == lax.broadcasted_iota(jnp.int32, shape, 0) % 4


def fold(tile):
    size = tile.shape[0]
    mine = jnp.where(own_quarter(tile.shape), tile, 0.0)
    pairs = mine + pltpu.roll(mine, size - 1, 0)
    return pairs + pltpu.roll(pairs, size - 2, 0)


def spot(level, r, turned):
    return CHUNK * (level * 16 + (15 - r if turned else r))


def east(level, start, count):
    return pl.ds(2 * start + level, count, 2)


def pack_kernel(turn_ref, u_hbm, v_hbm, h_hbm, out_ref, u_ref, v_ref, h_ref, tail_ref, last_ref, sems):
    moves = [
        pltpu.make_async_copy(src, dst, sems.at[i])
        for i, (src, dst) in enumerate(((u_hbm, u_ref), (v_hbm, v_ref), (h_hbm, h_ref)))
    ]
    for move in moves:
        move.start()
    last_ref[...] = jnp.zeros_like(last_ref)
    for move in moves:
        move.wait()
    for level in range(2):
        tiles = [ref[east(level, 0, LANES), :].T for ref in (u_ref, v_ref, h_ref)]
        tail_ref[:TAIL, :] = u_ref[east(level, LANES, TAIL), :]
        tail_ref[TAIL:HALF, :] = h_ref[east(level, LANES, SIDE), :]
        tail_ref[HALF : HALF + TAIL, :] = v_ref[east(level, LANES, TAIL), :]
        tail_ref[HALF + TAIL :, :] = h_ref[east(level, LANES + SIDE, SIDE), :]
        tiles.append(tail_ref[...].T)
        last = h_ref[east(level, SEG - LAST, LAST), :]
        for g in range(4):
            last_ref[g * QUARTER : g * QUARTER + LAST, :] = last
        tail_ref[...] = fold(last_ref[...].T)
        folded = tail_ref[pl.ds(0, 32, 4), :]
        for turned in (False, True):

            @pl.when(turn_ref[0] == int(turned))
            def _():
                for r in range(16):
                    at = spot(level, r, turned)
                    for f in range(4):
                        out_ref[at + f * ROWS : at + (f + 1) * ROWS, :] = tiles[f][r * ROWS : (r + 1) * ROWS]
                    out_ref[at + 4 * ROWS : at + CHUNK, :] = folded[2 * r : 2 * r + 2]


def unpack_kernel(turn_ref, in_ref, u_ref, v_ref, h_ref, u_out, v_out, h_out, tile_ref):
    for level in range(2):
        for turned in (False, True):

            @pl.when(turn_ref[0] == int(turned))
            def _():
                for r in range(16):
                    at = spot(level, r, turned)
                    for f in range(4):
                        tile_ref[f, r * ROWS : (r + 1) * ROWS, :] = in_ref[at + f * ROWS : at + (f + 1) * ROWS, :]
                    for t in range(2):
                        row = in_ref[at + 4 * ROWS + t : at + 4 * ROWS + t + 1, :]
                        tile_ref[4, r * ROWS + 4 * t : r * ROWS + 4 * t + 4, :] = jnp.broadcast_to(row, (4, LANES))

        for f, (ref, out) in enumerate(((u_ref, u_out), (v_ref, v_out), (h_ref, h_out))):
            here = east(level, 0, LANES)
            out[here, :] = ref[here, :] + tile_ref[f].T
        mixed, quarters = tile_ref[3].T, tile_ref[4].T
        group = lane((LAST, LANES)) % 4
        last = quarters[:LAST]
        for g in range(1, 4):
            last = jnp.where(group == g, quarters[g * QUARTER : g * QUARTER + LAST], last)
        for ref, out, start, change in (
            (u_ref, u_out, LANES, mixed[:TAIL]),
            (h_ref, h_out, LANES, mixed[TAIL:HALF]),
            (v_ref, v_out, LANES, mixed[HALF : HALF + TAIL]),
            (h_ref, h_out, LANES + SIDE, mixed[HALF + TAIL :]),
            (h_ref, h_out, SEG - LAST, last),
        ):
            here = east(level, start, change.shape[0])
            out[here, :] = ref[here, :] + change


def halves(x):
    high = x.astype(jnp.bfloat16)
    return high, (x - high.astype(jnp.float32)).astype(jnp.bfloat16)


def dot(x, table, contract):
    def product(a, b):
        return lax.dot_general(a, b, (((1,), (contract,)), ((), ())), preferred_element_type=jnp.float32)

    (high, low), (table_high, table_low) = halves(x), halves(table)
    return product(high, table_high) + (product(high, table_low) + product(low, table_high))


BLOCK = WAVES * ROWS


def padded(fields):
    return -(-fields * BLOCK // 16) * 16


def transform(columns, table_ref, twiddle_ref, spec_ref, left_ref):
    at = lane((ROWS, LANES))
    own = (at < TAIL, (at >= HALF) & (at < HALF + TAIL))
    for get, part, fields in columns:
        lanes = slice(part * LANES, (part + 1) * LANES)
        late = slice(WIDE + part * LANES, WIDE + (part + 1) * LANES)
        for k1, (re, im) in enumerate(real_fft([get(a) for a in range(PARTS)])):
            cos = twiddle_ref[k1 : k1 + 1, lanes]
            sin = twiddle_ref[WAVES + k1 : WAVES + k1 + 1, lanes]
            if im is None:
                new_re, new_im = re * cos, -re * sin
            else:
                new_re, new_im = re * cos + im * sin, im * cos - re * sin
            for f, half in fields:
                rows = slice(f * BLOCK + k1 * ROWS, f * BLOCK + (k1 + 1) * ROWS)
                if part == 0:
                    left_ref[rows, lanes], left_ref[rows, late] = new_re, new_im
                else:
                    left_ref[rows, lanes] = jnp.where(own[half], new_re, 0.0)
                    left_ref[rows, late] = jnp.where(own[half], new_im, 0.0)
    spec_ref[...] = dot(left_ref[...], table_ref[: 2 * WIDE, :], 0)


def tiles_of(x_ref):
    def tile(f):
        return lambda a: x_ref[a * CHUNK + f * ROWS : a * CHUNK + (f + 1) * ROWS, :]

    return tile


def gather_tails(x_ref, tails_ref):
    at = lane((ROWS, LANES))
    place_of_four = lax.broadcasted_iota(jnp.int32, at.shape, 0) % 4
    for a in range(PARTS):
        base = a * CHUNK + 3 * ROWS
        mixed = x_ref[base : base + ROWS, :]
        rows = [jnp.broadcast_to(x_ref[base + ROWS + t : base + ROWS + t + 1, :], (4, LANES)) for t in range(2)]
        quarters, last = jnp.concatenate(rows, axis=0), None
        for g in range(4):
            moved = pltpu.roll(quarters, (2 * SIDE - g * QUARTER) % LANES, 1)
            last = moved if last is None else jnp.where(place_of_four == g, moved, last)
        beside_u, beside_v = pltpu.roll(mixed, LANES - TAIL, 1), pltpu.roll(mixed, HALF - TAIL + SIDE, 1)
        whole = jnp.where(at < SIDE, beside_u, jnp.where(at < 2 * SIDE, beside_v, last))
        tails_ref[a * ROWS : (a + 1) * ROWS, :] = jnp.where(at < HALF, whole, pltpu.roll(whole, HALF, 1))


H, UH, VH = range(3)
U, V = range(2)


def damping(row, wave_ref, k1):
    ratio2 = row[:, 0:1]
    here, there = wave_ref[k1 : k1 + 1, :], wave_ref[WAVES + k1 : WAVES + k1 + 1, :]
    return 0.5 * (ratio2 / jnp.maximum(here, ratio2) + ratio2 / jnp.maximum(there, ratio2))


REAL, IMAG = slice(0, WIDE), slice(WIDE, 2 * WIDE)


def rows_of(f, k1):
    return slice(f * BLOCK + k1 * ROWS, f * BLOCK + (k1 + 1) * ROWS)


def wind_kernel(x_ref, table_ref, twiddle_ref, wave_ref, row_ref, spec_ref, damp_ref, left_ref):
    tile = tiles_of(x_ref)
    columns = ((tile(0), 0, ((U, 0),)), (tile(1), 0, ((V, 0),)), (tile(3), 1, ((U, 0), (V, 1))))
    transform(columns, table_ref, twiddle_ref, spec_ref, left_ref)
    row = row_ref[0]
    rotation = row[:, 3:4]
    for k1 in range(WAVES):
        damp = SCALE * damping(row, wave_ref, k1)
        damp_ref[rows_of(0, k1), :] = damp
        turn = damp * rotation
        for span in (REAL, IMAG):
            spec_ref[rows_of(U, k1), span] = -turn * spec_ref[rows_of(U, k1), span]
            spec_ref[rows_of(V, k1), span] = turn * spec_ref[rows_of(V, k1), span]


def to_message(rows):
    tails = rows[:, LANES:]
    tails = jnp.where(lane((2, LANES)) < HALF, tails[:2], pltpu.roll(tails[2:], HALF, 1))
    return jnp.concatenate([rows[:, :LANES], tails, jnp.zeros((2, LANES), jnp.float32)], axis=0)


def from_message(message):
    tails = message[4:6]
    tails = jnp.concatenate([tails, pltpu.roll(tails, HALF, 1)], axis=0)
    return jnp.concatenate([message[:4], tails], axis=1)


def mass_kernel(
    x_ref, table_ref, twiddle_ref, wave_ref, row_ref, spec_ref, near_ref, far_ref, left_ref, tails_ref
):
    gather_tails(x_ref, tails_ref)
    tile = tiles_of(x_ref)

    def tail(a):
        return tails_ref[a * ROWS : (a + 1) * ROWS, :]

    def product(f, h):
        return lambda a: tile(f)(a) * h(a)

    columns = (
        (tile(2), 0, ((H, 0),)),
        (product(0, tile(2)), 0, ((UH, 0),)),
        (product(1, tile(2)), 0, ((VH, 0),)),
        (tail, 1, ((H, 0),)),
        (product(3, tail), 1, ((UH, 0), (VH, 1))),
    )
    transform(columns, table_ref, twiddle_ref, spec_ref, left_ref)
    row = row_ref[0]
    x_coef, y_coef, coslat, odd = row[:, 1:2], row[:, 2:3], row[:, 4:5], row[:4, 7:8] > 0.5
    for k1 in range(WAVES):
        damp = damping(row, wave_ref, k1)
        across = x_coef * wave_ref[2 * WAVES + k1 : 2 * WAVES + k1 + 1, :] * damp
        gain_re = across * spec_ref[rows_of(UH, k1), IMAG]
        gain_im = -across * spec_ref[rows_of(UH, k1), REAL]
        scale = damp * coslat
        up, down = [], []
        for span, gain in ((REAL, gain_re), (IMAG, gain_im)):
            spec_ref[rows_of(UH, k1), span] = gain
            mass = spec_ref[rows_of(H, k1), span] + gain
            flux = scale * spec_ref[rows_of(VH, k1), span]
            spec_ref[rows_of(VH, k1), span] = flux
            up += [flux[7:8], mass[7:8] + y_coef[7:8] * flux[6:7]]
            down += [flux[0:1], mass[0:1] - y_coef[0:1] * flux[1:2]]
        up, down = jnp.concatenate(up, axis=0), jnp.concatenate(down, axis=0)
        near_ref[rows_of(0, k1), :] = to_message(jnp.where(odd, down, up))
        far_ref[rows_of(0, k1), :] = to_message(jnp.where(odd, up, down))


def inverse_kernel(
    spec_ref, wind_ref, damp_ref, near_ref, far_ref, table_ref, twiddle_ref, wave_ref, row_ref, out_ref, left_ref,
    right_ref, last_ref
):
    row = row_ref[0]
    x_coef, y_coef = row[:, 1:2], row[:, 2:3]
    y_below, y_above = row[0:1, 5:6], row[0:1, 6:7]
    odd = row[:, 7:8] > 0.5
    for k1 in range(WAVES):
        near, far = near_ref[rows_of(0, k1), :], far_ref[rows_of(0, k1), :]
        below, above = from_message(jnp.where(odd, near, far)), from_message(jnp.where(odd, far, near))
        damp = damp_ref[rows_of(0, k1), :]
        across = damp * x_coef * wave_ref[2 * WAVES + k1 : 2 * WAVES + k1 + 1, :]
        along = -PUSH_COEF * damp
        mass = []
        for part, span in enumerate((REAL, IMAG)):
            flux = spec_ref[rows_of(VH, k1), span]
            flux_below, flux_above = below[2 * part : 2 * part + 1], above[2 * part : 2 * part + 1]
            prev = jnp.concatenate([flux_below, flux[:-1]], axis=0)
            following = jnp.concatenate([flux[1:], flux_above], axis=0)
            change = spec_ref[rows_of(UH, k1), span] - y_coef * (following - prev)
            new = spec_ref[rows_of(H, k1), span] + change
            new_below = below[2 * part + 1 : 2 * part + 2] - y_below * flux[0:1]
            new_above = above[2 * part + 1 : 2 * part + 2] + y_above * flux[7:8]
            mass.append(new)
            prev = jnp.concatenate([new_below, new[:-1]], axis=0)
            following = jnp.concatenate([new[1:], new_above], axis=0)
            left_ref[rows_of(2, k1), span] = along * (following - prev) + wind_ref[rows_of(U, k1), span]
            left_ref[rows_of(0, k1), span] = SCALE * change
        left_ref[rows_of(1, k1), REAL] = across * mass[1] + wind_ref[rows_of(V, k1), REAL]
        left_ref[rows_of(1, k1), IMAG] = wind_ref[rows_of(V, k1), IMAG] - across * mass[0]
    right_ref[...] = dot(left_ref[...], table_ref[: 2 * WIDE, :], 1)
    last_ref[...] = dot(left_ref[:BLOCK, :], table_ref[2 * WIDE :, :], 1)
    at = lane((ROWS, LANES))
    for f, part, fields in ((0, 0, (1,)), (1, 0, (2,)), (2, 0, (0,)), (3, 1, (0, 1, 2)), (4, 2, (0,))):
        lanes = slice(part * LANES, (part + 1) * LANES)
        source, start, late = (last_ref, 0, LANES) if part == 2 else (right_ref, part * LANES, WIDE + part * LANES)
        waves = []
        for k1 in range(WAVES):
            cos = twiddle_ref[k1 : k1 + 1, lanes]
            sin = twiddle_ref[WAVES + k1 : WAVES + k1 + 1, lanes]
            re = [source[rows_of(g, k1), start : start + LANES] for g in fields]
            im = [source[rows_of(g, k1), late : late + LANES] for g in fields]
            if len(fields) == 3:
                own = (at < TAIL, (at >= HALF) & (at < HALF + TAIL))
                re = [jnp.where(own[0], re[1], jnp.where(own[1], re[2], re[0]))]
                im = [jnp.where(own[0], im[1], jnp.where(own[1], im[2], im[0]))]
            re, im = re[0], im[0]
            waves.append((re * cos - im * sin, None if k1 in (0, WAVES - 1) else im * cos + re * sin))
        for a, value in enumerate(real_ifft(waves)):
            start = a * CHUNK + f * ROWS
            if f == 4:
                value = fold(value)
                value = jnp.concatenate([value[0:1], value[4:5]], axis=0)
            out_ref[start : start + value.shape[0], :] = value


def in_vmem():
    return pl.BlockSpec(memory_space=pltpu.VMEM)


PARAMS = pltpu.CompilerParams(vmem_limit_bytes=40 * 2**20)


def like(*shape):
    return jax.ShapeDtypeStruct(shape, jnp.float32)


def place(level, r, lat):
    return (level * 16 + (15 - r if lat % 2 else r)) * 16 + lat


def swaps(odd):
    pairs = []
    for level in range(2):
        for lat in range(16):
            pairs += [(place(level, r, lat), place(level, r + 1, lat)) for r in range(odd, 15, 2)]
            if odd and lat < 15:
                pairs.append((place(level, 15, lat), place(level, 0, lat + 1)))
    return pairs + [(b, a) for a, b in pairs]


def in_smem():
    return pl.BlockSpec(memory_space=pltpu.SMEM)


def pack(turned, u, v, h):
    return pl.pallas_call(
        pack_kernel,
        out_shape=like(PARTS * CHUNK, LANES),
        in_specs=[in_smem()] + [pl.BlockSpec(memory_space=pltpu.HBM)] * 3,
        out_specs=in_vmem(),
        scratch_shapes=[pltpu.VMEM((2 * SEG, LANES), jnp.float32)] * 3
        + [pltpu.VMEM((LANES, LANES), jnp.float32)] * 2
        + [pltpu.SemaphoreType.DMA((3,))],
        compiler_params=pltpu.CompilerParams(vmem_limit_bytes=56 * 2**20),
        name="pack",
    )(turned, u, v, h)


def cost(fields):
    size = padded(fields) * 2 * WIDE
    return pl.CostEstimate(flops=6 * size * 2 * WIDE, bytes_accessed=8 * size, transcendentals=0)


def forward_mass(whole, row):
    return pl.pallas_call(
        mass_kernel,
        out_shape=(like(padded(3), 2 * WIDE), like(BLOCK, LANES), like(BLOCK, LANES)),
        in_specs=[in_vmem()] * 5,
        out_specs=(in_vmem(),) * 3,
        scratch_shapes=[pltpu.VMEM((padded(3), 2 * WIDE), jnp.float32), pltpu.VMEM((PARTS * ROWS, LANES), jnp.float32)],
        compiler_params=PARAMS,
        cost_estimate=cost(3),
        name="forward_mass",
    )(whole, dft_table(), twiddle_table(), wave_table(), row)


def forward_wind(whole, row):
    return pl.pallas_call(
        wind_kernel,
        out_shape=(like(padded(2), 2 * WIDE), like(BLOCK, WIDE)),
        in_specs=[in_vmem()] * 5,
        out_specs=(in_vmem(),) * 2,
        scratch_shapes=[pltpu.VMEM((padded(2), 2 * WIDE), jnp.float32)],
        compiler_params=PARAMS,
        cost_estimate=cost(2),
        name="forward_wind",
    )(whole, dft_table(), twiddle_table(), wave_table(), row)


def inverse(spec, wind, damp, near, far, row):
    return pl.pallas_call(
        inverse_kernel,
        out_shape=like(PARTS * CHUNK, LANES),
        in_specs=[in_vmem()] * 9,
        out_specs=in_vmem(),
        scratch_shapes=[pltpu.VMEM((padded(3), 2 * WIDE), jnp.float32)] * 2 + [pltpu.VMEM((BLOCK, WIDE), jnp.float32)],
        compiler_params=PARAMS,
        cost_estimate=cost(3),
        name="inverse",
    )(spec, wind, damp, near, far, dft_table(), twiddle_table(), wave_table(), row)


def unpack(turned, back, u, v, h):
    return pl.pallas_call(
        unpack_kernel,
        out_shape=(like(2 * SEG, LANES),) * 3,
        in_specs=[in_smem()] + [in_vmem()] * 4,
        out_specs=(in_vmem(),) * 3,
        scratch_shapes=[pltpu.VMEM((5, LANES, LANES), jnp.float32)],
        compiler_params=PARAMS,
        name="unpack",
    )(turned, back, u, v, h)


def row_of(group):
    return lax.dynamic_slice_in_dim(jnp.asarray(row_table()), group, 1, axis=0)


def exchange(chunks):
    moved = lax.all_to_all(chunks.reshape(PARTS, CHUNK, 1, LANES), "lon", 0, 0, tiled=True)
    return moved.reshape(PARTS * CHUNK, LANES)


def step(u, v, h):
    lat = lax.axis_index("lat")
    turned = lat % 2
    r = lax.axis_index("lon") % 16
    row = row_of(lat * 16 + jnp.where(turned == 1, 15 - r, r))
    turned = turned.reshape(1)
    u, v, h = (jnp.swapaxes(x, 0, 1).reshape(2 * SEG, LANES) for x in (u, v, h))
    whole = exchange(pack(turned, u, v, h))
    spec, near, far = forward_mass(whole, row)
    near = lax.ppermute(near, ("lon", "lat"), swaps(0))
    far = lax.ppermute(far, ("lon", "lat"), swaps(1))
    wind, damp = forward_wind(whole, row)
    outs = unpack(turned, exchange(inverse(spec, wind, damp, near, far, row)), u, v, h)
    return tuple(jnp.swapaxes(x.reshape(SEG, 2, LANES), 0, 1) for x in outs)


def solution(mesh):
    spec = P(None, "lon", "lat")
    return jax.shard_map(step, mesh=mesh, in_specs=(spec,) * 3, out_specs=(spec,) * 3, check_vma=False)
```

```python
import functools
import math

import jax
import jax.numpy as jnp
import numpy as np
from jax import lax
from jax.experimental import pallas as pl
from jax.experimental.pallas import tpu as pltpu
from jax.sharding import PartitionSpec as P

NLON = 5760
NLAT = 2048
PARTS = 32
SEG = 180
LANES = 128
TAIL = SEG - LANES
HALF = 64
ROWS = 8
WAVES = PARTS // 2 + 1
WIDE = 2 * LANES
SCALE = 1.0 / NLON
SIDE = HALF - TAIL
LAST = TAIL - 2 * SIDE
QUARTER = 32
CHUNK = 4 * ROWS + 2


def placed():
    b = np.arange(SEG)
    tail, side = b[LANES:], LANES + SIDE
    last = np.concatenate([b[-LAST:], np.full(QUARTER - LAST, -1)])
    return np.concatenate([b[:LANES], tail, b[LANES:side], tail, b[side : side + SIDE], np.tile(last, 4)])


def dft_table():
    b = placed()
    angle = (np.outer(b, np.arange(SEG)) % SEG) * (2.0 * math.pi / SEG)
    cos, sin = np.cos(angle) * (b >= 0)[:, None], np.sin(angle) * (b >= 0)[:, None]
    table = np.zeros((6 * LANES, 2 * WIDE))
    for to, (re, im) in ((slice(0, SEG), (cos, sin)), (slice(WIDE, WIDE + SEG), (-sin, cos))):
        table[:WIDE, to], table[WIDE : 2 * WIDE, to] = re[:WIDE], im[:WIDE]
        table[2 * WIDE : 2 * WIDE + LANES, to], table[2 * WIDE + LANES :, to] = re[WIDE:], im[WIDE:]
    return table.astype(np.float32)


def twiddle_table():
    angle = np.outer(np.arange(WAVES), placed()) * (2.0 * math.pi / NLON)
    return np.concatenate([np.cos(angle), np.sin(angle)]).astype(np.float32)


def wave_table():
    k = np.arange(WAVES)[:, None] + PARTS * np.arange(SEG)[None, :]
    step = np.float32(math.pi / NLON)
    here = np.sin(k.astype(np.float32) * step) ** 2
    there = np.sin(((NLON - k) % NLON).astype(np.float32) * step) ** 2
    slope = 2.0 * np.sin(2.0 * math.pi * k / NLON)
    table = np.zeros((3 * WAVES, WIDE), np.float32)
    table[:, :SEG] = np.concatenate([here, there, slope])
    return table


def row_table():
    j = np.arange(-1, NLAT + 1)
    phi = np.float32(-0.5 * math.pi) + (j.astype(np.float32) + np.float32(0.5)) * np.float32(math.pi / NLAT)
    phi = phi.astype(np.float64)
    lat_step, lon_step = math.pi / NLAT, 2.0 * math.pi / NLON
    time_step = 0.25 * lat_step
    cos = np.cos(phi)
    y_coef = time_step / (2.0 * lat_step * cos)
    y_coef[0] = y_coef[-1] = 0.0
    table = np.zeros((NLAT, LANES))
    table[:, 0] = (cos / math.cos(0.25 * math.pi))[1:-1] ** 2
    table[:, 1] = (time_step / (2.0 * lon_step * cos))[1:-1]
    table[:, 2] = y_coef[1:-1]
    table[:, 3] = 0.3 * np.sin(phi)[1:-1]
    table[:, 4] = cos[1:-1]
    table[:, 5] = np.repeat(y_coef[0:NLAT:ROWS], ROWS)
    table[:, 6] = np.repeat(y_coef[ROWS + 1 :: ROWS], ROWS)
    table[:, 7] = np.arange(NLAT) // ROWS % 2
    return table.reshape(NLAT // ROWS, ROWS, LANES).astype(np.float32)


PUSH_COEF = 0.25 / 2.0


def add(x, y):
    if x is None:
        return y
    return x if y is None else x + y


def sub(x, y):
    if y is None:
        return x
    return -y if x is None else x - y


def times(z, cos, sin):
    re, im = z
    if abs(sin) < 1e-15:
        return (re * cos, None if im is None else im * cos)
    if im is None:
        return (re * cos, re * sin)
    return (re * cos - im * sin, re * sin + im * cos)


def real_fft(values):
    n = len(values)
    if n == 2:
        return [(values[0] + values[1], None), (values[0] - values[1], None)]
    even, odd = real_fft(values[0::2]), real_fft(values[1::2])
    out = [None] * (n // 2 + 1)
    out[0] = (even[0][0] + odd[0][0], None)
    out[n // 2] = (even[0][0] - odd[0][0], None)
    for k in range(1, n // 4):
        re, im = times(odd[k], math.cos(2 * math.pi * k / n), -math.sin(2 * math.pi * k / n))
        out[k] = (add(even[k][0], re), add(even[k][1], im))
        out[n // 2 - k] = (sub(even[k][0], re), sub(im, even[k][1]))
    out[n // 4] = (even[n // 4][0], -odd[n // 4][0])
    return out


def real_ifft(waves):
    n = 2 * (len(waves) - 1)
    if n == 2:
        return [waves[0][0] + waves[1][0], waves[0][0] - waves[1][0]]
    even, odd = [None] * (n // 4 + 1), [None] * (n // 4 + 1)
    even[0] = (waves[0][0] + waves[n // 2][0], None)
    odd[0] = (waves[0][0] - waves[n // 2][0], None)
    for k in range(1, n // 4):
        (re, im), (far_re, far_im) = waves[k], waves[n // 2 - k]
        even[k] = (re + far_re, im - far_im)
        odd[k] = times((re - far_re, im + far_im), math.cos(2 * math.pi * k / n), math.sin(2 * math.pi * k / n))
    even[n // 4] = (2.0 * waves[n // 4][0], None)
    odd[n // 4] = (-2.0 * waves[n // 4][1], None)
    out = [None] * n
    out[0::2], out[1::2] = real_ifft(even), real_ifft(odd)
    return out


def lane(shape):
    return lax.broadcasted_iota(jnp.int32, shape, 1)


def own_quarter(shape):
    return lane(shape) // QUARTER == lax.broadcasted_iota(jnp.int32, shape, 0) % 4


def fold(tile):
    size = tile.shape[0]
    mine = jnp.where(own_quarter(tile.shape), tile, 0.0)
    pairs = mine + pltpu.roll(mine, size - 1, 0)
    return pairs + pltpu.roll(pairs, size - 2, 0)


def spot(level, r, turned):
    return CHUNK * (level * 16 + (15 - r if turned else r))


def east(level, start, count):
    return pl.ds(2 * start + level, count, 2)


def pack_kernel(turn_ref, u_hbm, v_hbm, h_hbm, out_ref, u_ref, v_ref, h_ref, tail_ref, last_ref, sems):
    moves = [
        pltpu.make_async_copy(src, dst, sems.at[i])
        for i, (src, dst) in enumerate(((u_hbm, u_ref), (v_hbm, v_ref), (h_hbm, h_ref)))
    ]
    for move in moves:
        move.start()
    last_ref[...] = jnp.zeros_like(last_ref)
    for move in moves:
        move.wait()
    for level in range(2):
        tiles = [ref[east(level, 0, LANES), :].T for ref in (u_ref, v_ref, h_ref)]
        tail_ref[:TAIL, :] = u_ref[east(level, LANES, TAIL), :]
        tail_ref[TAIL:HALF, :] = h_ref[east(level, LANES, SIDE), :]
        tail_ref[HALF : HALF + TAIL, :] = v_ref[east(level, LANES, TAIL), :]
        tail_ref[HALF + TAIL :, :] = h_ref[east(level, LANES + SIDE, SIDE), :]
        tiles.append(tail_ref[...].T)
        last = h_ref[east(level, SEG - LAST, LAST), :]
        for g in range(4):
            last_ref[g * QUARTER : g * QUARTER + LAST, :] = last
        tail_ref[...] = fold(last_ref[...].T)
        folded = tail_ref[pl.ds(0, 32, 4), :]
        for turned in (False, True):

            @pl.when(turn_ref[0] == int(turned))
            def _():
                for r in range(16):
                    at = spot(level, r, turned)
                    for f in range(4):
                        out_ref[at + f * ROWS : at + (f + 1) * ROWS, :] = tiles[f][r * ROWS : (r + 1) * ROWS]
                    out_ref[at + 4 * ROWS : at + CHUNK, :] = folded[2 * r : 2 * r + 2]


def unpack_kernel(turn_ref, in_ref, u_ref, v_ref, h_ref, u_out, v_out, h_out, tile_ref):
    for level in range(2):
        for turned in (False, True):

            @pl.when(turn_ref[0] == int(turned))
            def _():
                for r in range(16):
                    at = spot(level, r, turned)
                    for f in range(4):
                        tile_ref[f, r * ROWS : (r + 1) * ROWS, :] = in_ref[at + f * ROWS : at + (f + 1) * ROWS, :]
                    for t in range(2):
                        row = in_ref[at + 4 * ROWS + t : at + 4 * ROWS + t + 1, :]
                        tile_ref[4, r * ROWS + 4 * t : r * ROWS + 4 * t + 4, :] = jnp.broadcast_to(row, (4, LANES))

        for f, (ref, out) in enumerate(((u_ref, u_out), (v_ref, v_out), (h_ref, h_out))):
            here = east(level, 0, LANES)
            out[here, :] = ref[here, :] + tile_ref[f].T
        mixed, quarters = tile_ref[3].T, tile_ref[4].T
        group = lane((LAST, LANES)) % 4
        last = quarters[:LAST]
        for g in range(1, 4):
            last = jnp.where(group == g, quarters[g * QUARTER : g * QUARTER + LAST], last)
        for ref, out, start, change in (
            (u_ref, u_out, LANES, mixed[:TAIL]),
            (h_ref, h_out, LANES, mixed[TAIL:HALF]),
            (v_ref, v_out, LANES, mixed[HALF : HALF + TAIL]),
            (h_ref, h_out, LANES + SIDE, mixed[HALF + TAIL :]),
            (h_ref, h_out, SEG - LAST, last),
        ):
            here = east(level, start, change.shape[0])
            out[here, :] = ref[here, :] + change


def halves(x):
    high = x.astype(jnp.bfloat16)
    return high, (x - high.astype(jnp.float32)).astype(jnp.bfloat16)


def dot(x, table, contract):
    def product(a, b):
        return lax.dot_general(a, b, (((1,), (contract,)), ((), ())), preferred_element_type=jnp.float32)

    (high, low), (table_high, table_low) = halves(x), halves(table)
    return product(high, table_high) + (product(high, table_low) + product(low, table_high))


BLOCK = WAVES * ROWS


def padded(fields):
    return -(-fields * BLOCK // 16) * 16


def transform(columns, table_ref, twiddle_ref, spec_ref, left_ref):
    at = lane((ROWS, LANES))
    own = (at < TAIL, (at >= HALF) & (at < HALF + TAIL))
    for get, part, fields in columns:
        lanes = slice(part * LANES, (part + 1) * LANES)
        late = slice(WIDE + part * LANES, WIDE + (part + 1) * LANES)
        for k1, (re, im) in enumerate(real_fft([get(a) for a in range(PARTS)])):
            cos = twiddle_ref[k1 : k1 + 1, lanes]
            sin = twiddle_ref[WAVES + k1 : WAVES + k1 + 1, lanes]
            if im is None:
                new_re, new_im = re * cos, -re * sin
            else:
                new_re, new_im = re * cos + im * sin, im * cos - re * sin
            for f, half in fields:
                rows = slice(f * BLOCK + k1 * ROWS, f * BLOCK + (k1 + 1) * ROWS)
                if part == 0:
                    left_ref[rows, lanes], left_ref[rows, late] = new_re, new_im
                else:
                    left_ref[rows, lanes] = jnp.where(own[half], new_re, 0.0)
                    left_ref[rows, late] = jnp.where(own[half], new_im, 0.0)
    spec_ref[...] = dot(left_ref[...], table_ref[: 2 * WIDE, :], 0)


def tiles_of(x_ref):
    def tile(f):
        return lambda a: x_ref[a * CHUNK + f * ROWS : a * CHUNK + (f + 1) * ROWS, :]

    return tile


def gather_tails(x_ref, tails_ref):
    at = lane((ROWS, LANES))
    place_of_four = lax.broadcasted_iota(jnp.int32, at.shape, 0) % 4
    for a in range(PARTS):
        base = a * CHUNK + 3 * ROWS
        mixed = x_ref[base : base + ROWS, :]
        rows = [jnp.broadcast_to(x_ref[base + ROWS + t : base + ROWS + t + 1, :], (4, LANES)) for t in range(2)]
        quarters, last = jnp.concatenate(rows, axis=0), None
        for g in range(4):
            moved = pltpu.roll(quarters, (2 * SIDE - g * QUARTER) % LANES, 1)
            last = moved if last is None else jnp.where(place_of_four == g, moved, last)
        beside_u, beside_v = pltpu.roll(mixed, LANES - TAIL, 1), pltpu.roll(mixed, HALF - TAIL + SIDE, 1)
        whole = jnp.where(at < SIDE, beside_u, jnp.where(at < 2 * SIDE, beside_v, last))
        tails_ref[a * ROWS : (a + 1) * ROWS, :] = jnp.where(at < HALF, whole, pltpu.roll(whole, HALF, 1))


H, UH, VH = range(3)
U, V = range(2)


def damping(row, wave_ref, k1):
    ratio2 = row[:, 0:1]
    here, there = wave_ref[k1 : k1 + 1, :], wave_ref[WAVES + k1 : WAVES + k1 + 1, :]
    return 0.5 * (ratio2 / jnp.maximum(here, ratio2) + ratio2 / jnp.maximum(there, ratio2))


REAL, IMAG = slice(0, WIDE), slice(WIDE, 2 * WIDE)


def rows_of(f, k1):
    return slice(f * BLOCK + k1 * ROWS, f * BLOCK + (k1 + 1) * ROWS)


def wind_kernel(x_ref, table_ref, twiddle_ref, wave_ref, row_ref, spec_ref, damp_ref, left_ref):
    tile = tiles_of(x_ref)
    columns = ((tile(0), 0, ((U, 0),)), (tile(1), 0, ((V, 0),)), (tile(3), 1, ((U, 0), (V, 1))))
    transform(columns, table_ref, twiddle_ref, spec_ref, left_ref)
    row = row_ref[0]
    rotation = row[:, 3:4]
    for k1 in range(WAVES):
        damp = SCALE * damping(row, wave_ref, k1)
        damp_ref[rows_of(0, k1), :] = damp
        turn = damp * rotation
        for span in (REAL, IMAG):
            spec_ref[rows_of(U, k1), span] = -turn * spec_ref[rows_of(U, k1), span]
            spec_ref[rows_of(V, k1), span] = turn * spec_ref[rows_of(V, k1), span]


def to_message(rows):
    tails = rows[:, LANES:]
    tails = jnp.where(lane((2, LANES)) < HALF, tails[:2], pltpu.roll(tails[2:], HALF, 1))
    return jnp.concatenate([rows[:, :LANES], tails, jnp.zeros((2, LANES), jnp.float32)], axis=0)


def from_message(message):
    tails = message[4:6]
    tails = jnp.concatenate([tails, pltpu.roll(tails, HALF, 1)], axis=0)
    return jnp.concatenate([message[:4], tails], axis=1)


def mass_kernel(
    x_ref, table_ref, twiddle_ref, wave_ref, row_ref, spec_ref, far_ref, near_ref, left_ref, tails_ref
):
    gather_tails(x_ref, tails_ref)
    tile = tiles_of(x_ref)

    def tail(a):
        return tails_ref[a * ROWS : (a + 1) * ROWS, :]

    def product(f, h):
        return lambda a: tile(f)(a) * h(a)

    columns = (
        (tile(2), 0, ((H, 0),)),
        (product(0, tile(2)), 0, ((UH, 0),)),
        (product(1, tile(2)), 0, ((VH, 0),)),
        (tail, 1, ((H, 0),)),
        (product(3, tail), 1, ((UH, 0), (VH, 1))),
    )
    transform(columns, table_ref, twiddle_ref, spec_ref, left_ref)
    row = row_ref[0]
    x_coef, y_coef, coslat, odd = row[:, 1:2], row[:, 2:3], row[:, 4:5], row[:4, 7:8] > 0.5
    for k1 in range(WAVES):
        damp = damping(row, wave_ref, k1)
        across = x_coef * wave_ref[2 * WAVES + k1 : 2 * WAVES + k1 + 1, :] * damp
        gain_re = across * spec_ref[rows_of(UH, k1), IMAG]
        gain_im = -across * spec_ref[rows_of(UH, k1), REAL]
        scale = damp * coslat
        up, down = [], []
        for span, gain in ((REAL, gain_re), (IMAG, gain_im)):
            spec_ref[rows_of(UH, k1), span] = gain
            mass = spec_ref[rows_of(H, k1), span] + gain
            flux = scale * spec_ref[rows_of(VH, k1), span]
            spec_ref[rows_of(VH, k1), span] = flux
            up += [flux[7:8], mass[7:8] + y_coef[7:8] * flux[6:7]]
            down += [flux[0:1], mass[0:1] - y_coef[0:1] * flux[1:2]]
        up, down = jnp.concatenate(up, axis=0), jnp.concatenate(down, axis=0)
        near_ref[rows_of(0, k1), :] = to_message(jnp.where(odd, down, up))
        far_ref[rows_of(0, k1), :] = to_message(jnp.where(odd, up, down))


def inverse_kernel(
    spec_ref, wind_ref, damp_ref, far_ref, near_ref, table_ref, twiddle_ref, wave_ref, row_ref, out_ref, left_ref,
    right_ref, last_ref
):
    row = row_ref[0]
    x_coef, y_coef = row[:, 1:2], row[:, 2:3]
    y_below, y_above = row[0:1, 5:6], row[0:1, 6:7]
    odd = row[:, 7:8] > 0.5
    for k1 in range(WAVES):
        near, far = near_ref[rows_of(0, k1), :], far_ref[rows_of(0, k1), :]
        below, above = from_message(jnp.where(odd, near, far)), from_message(jnp.where(odd, far, near))
        damp = damp_ref[rows_of(0, k1), :]
        across = damp * x_coef * wave_ref[2 * WAVES + k1 : 2 * WAVES + k1 + 1, :]
        along = -PUSH_COEF * damp
        mass = []
        for part, span in enumerate((REAL, IMAG)):
            flux = spec_ref[rows_of(VH, k1), span]
            flux_below, flux_above = below[2 * part : 2 * part + 1], above[2 * part : 2 * part + 1]
            prev = jnp.concatenate([flux_below, flux[:-1]], axis=0)
            following = jnp.concatenate([flux[1:], flux_above], axis=0)
            change = spec_ref[rows_of(UH, k1), span] - y_coef * (following - prev)
            new = spec_ref[rows_of(H, k1), span] + change
            new_below = below[2 * part + 1 : 2 * part + 2] - y_below * flux[0:1]
            new_above = above[2 * part + 1 : 2 * part + 2] + y_above * flux[7:8]
            mass.append(new)
            prev = jnp.concatenate([new_below, new[:-1]], axis=0)
            following = jnp.concatenate([new[1:], new_above], axis=0)
            left_ref[rows_of(2, k1), span] = along * (following - prev) + wind_ref[rows_of(U, k1), span]
            left_ref[rows_of(0, k1), span] = SCALE * change
        left_ref[rows_of(1, k1), REAL] = across * mass[1] + wind_ref[rows_of(V, k1), REAL]
        left_ref[rows_of(1, k1), IMAG] = wind_ref[rows_of(V, k1), IMAG] - across * mass[0]
    right_ref[...] = dot(left_ref[...], table_ref[: 2 * WIDE, :], 1)
    last_ref[...] = dot(left_ref[:BLOCK, :], table_ref[2 * WIDE :, :], 1)
    at = lane((ROWS, LANES))
    for f, part, fields in ((0, 0, (1,)), (1, 0, (2,)), (2, 0, (0,)), (3, 1, (0, 1, 2)), (4, 2, (0,))):
        lanes = slice(part * LANES, (part + 1) * LANES)
        source, start, late = (last_ref, 0, LANES) if part == 2 else (right_ref, part * LANES, WIDE + part * LANES)
        waves = []
        for k1 in range(WAVES):
            cos = twiddle_ref[k1 : k1 + 1, lanes]
            sin = twiddle_ref[WAVES + k1 : WAVES + k1 + 1, lanes]
            re = [source[rows_of(g, k1), start : start + LANES] for g in fields]
            im = [source[rows_of(g, k1), late : late + LANES] for g in fields]
            if len(fields) == 3:
                own = (at < TAIL, (at >= HALF) & (at < HALF + TAIL))
                re = [jnp.where(own[0], re[1], jnp.where(own[1], re[2], re[0]))]
                im = [jnp.where(own[0], im[1], jnp.where(own[1], im[2], im[0]))]
            re, im = re[0], im[0]
            waves.append((re * cos - im * sin, None if k1 in (0, WAVES - 1) else im * cos + re * sin))
        for a, value in enumerate(real_ifft(waves)):
            start = a * CHUNK + f * ROWS
            if f == 4:
                value = fold(value)
                value = jnp.concatenate([value[0:1], value[4:5]], axis=0)
            out_ref[start : start + value.shape[0], :] = value


def in_vmem():
    return pl.BlockSpec(memory_space=pltpu.VMEM)


PARAMS = pltpu.CompilerParams(vmem_limit_bytes=40 * 2**20)


def like(*shape):
    return jax.ShapeDtypeStruct(shape, jnp.float32)


def place(level, r, lat):
    return (level * 16 + (15 - r if lat % 2 else r)) * 16 + lat


def swaps(odd):
    pairs = []
    for level in range(2):
        for lat in range(16):
            pairs += [(place(level, r, lat), place(level, r + 1, lat)) for r in range(odd, 15, 2)]
            if odd and lat < 15:
                pairs.append((place(level, 15, lat), place(level, 0, lat + 1)))
    return pairs + [(b, a) for a, b in pairs]


def in_smem():
    return pl.BlockSpec(memory_space=pltpu.SMEM)


def pack(turned, u, v, h):
    return pl.pallas_call(
        pack_kernel,
        out_shape=like(PARTS * CHUNK, LANES),
        in_specs=[in_smem()] + [pl.BlockSpec(memory_space=pltpu.HBM)] * 3,
        out_specs=in_vmem(),
        scratch_shapes=[pltpu.VMEM((2 * SEG, LANES), jnp.float32)] * 3
        + [pltpu.VMEM((LANES, LANES), jnp.float32)] * 2
        + [pltpu.SemaphoreType.DMA((3,))],
        compiler_params=pltpu.CompilerParams(vmem_limit_bytes=56 * 2**20),
        name="pack",
    )(turned, u, v, h)


def cost(fields):
    size = padded(fields) * 2 * WIDE
    return pl.CostEstimate(flops=6 * size * 2 * WIDE, bytes_accessed=8 * size, transcendentals=0)


def forward_mass(whole, row):
    return pl.pallas_call(
        mass_kernel,
        out_shape=(like(padded(3), 2 * WIDE), like(BLOCK, LANES), like(BLOCK, LANES)),
        in_specs=[in_vmem()] * 5,
        out_specs=(in_vmem(),) * 3,
        scratch_shapes=[pltpu.VMEM((padded(3), 2 * WIDE), jnp.float32), pltpu.VMEM((PARTS * ROWS, LANES), jnp.float32)],
        compiler_params=PARAMS,
        cost_estimate=cost(3),
        name="forward_mass",
    )(whole, dft_table(), twiddle_table(), wave_table(), row)


def forward_wind(whole, row):
    return pl.pallas_call(
        wind_kernel,
        out_shape=(like(padded(2), 2 * WIDE), like(BLOCK, WIDE)),
        in_specs=[in_vmem()] * 5,
        out_specs=(in_vmem(),) * 2,
        scratch_shapes=[pltpu.VMEM((padded(2), 2 * WIDE), jnp.float32)],
        compiler_params=PARAMS,
        cost_estimate=cost(2),
        name="forward_wind",
    )(whole, dft_table(), twiddle_table(), wave_table(), row)


def inverse(spec, wind, damp, far, near, row):
    return pl.pallas_call(
        inverse_kernel,
        out_shape=like(PARTS * CHUNK, LANES),
        in_specs=[in_vmem()] * 9,
        out_specs=in_vmem(),
        scratch_shapes=[pltpu.VMEM((padded(3), 2 * WIDE), jnp.float32)] * 2 + [pltpu.VMEM((BLOCK, WIDE), jnp.float32)],
        compiler_params=PARAMS,
        cost_estimate=cost(3),
        name="inverse",
    )(spec, wind, damp, far, near, dft_table(), twiddle_table(), wave_table(), row)


def unpack(turned, back, u, v, h):
    return pl.pallas_call(
        unpack_kernel,
        out_shape=(like(2 * SEG, LANES),) * 3,
        in_specs=[in_smem()] + [in_vmem()] * 4,
        out_specs=(in_vmem(),) * 3,
        scratch_shapes=[pltpu.VMEM((5, LANES, LANES), jnp.float32)],
        compiler_params=PARAMS,
        name="unpack",
    )(turned, back, u, v, h)


def row_of(group):
    return lax.dynamic_slice_in_dim(jnp.asarray(row_table()), group, 1, axis=0)


def exchange(chunks):
    moved = lax.all_to_all(chunks.reshape(PARTS, CHUNK, 1, LANES), "lon", 0, 0, tiled=True)
    return moved.reshape(PARTS * CHUNK, LANES)


def step(u, v, h):
    lat = lax.axis_index("lat")
    turned = lat % 2
    r = lax.axis_index("lon") % 16
    row = row_of(lat * 16 + jnp.where(turned == 1, 15 - r, r))
    turned = turned.reshape(1)
    u, v, h = (jnp.swapaxes(x, 0, 1).reshape(2 * SEG, LANES) for x in (u, v, h))
    whole = exchange(pack(turned, u, v, h))
    spec, far, near = forward_mass(whole, row)
    far = lax.ppermute(far, ("lon", "lat"), swaps(1))
    near = lax.ppermute(near, ("lon", "lat"), swaps(0))
    wind, damp = forward_wind(whole, row)
    outs = unpack(turned, exchange(inverse(spec, wind, damp, far, near, row)), u, v, h)
    return tuple(jnp.swapaxes(x.reshape(SEG, 2, LANES), 0, 1) for x in outs)


def solution(mesh):
    spec = P(None, "lon", "lat")
    return jax.shard_map(step, mesh=mesh, in_specs=(spec,) * 3, out_specs=(spec,) * 3, check_vma=False)
```

```python
import functools
import math

import jax
import jax.numpy as jnp
import numpy as np
from jax import lax
from jax.experimental import pallas as pl
from jax.experimental.pallas import tpu as pltpu
from jax.sharding import PartitionSpec as P

NLON = 5760
NLAT = 2048
PARTS = 32
SEG = 180
LANES = 128
TAIL = SEG - LANES
HALF = 64
ROWS = 8
WAVES = PARTS // 2 + 1
WIDE = 2 * LANES
SCALE = 1.0 / NLON
SIDE = HALF - TAIL
LAST = TAIL - 2 * SIDE
QUARTER = 32
CHUNK = 4 * ROWS + 2


def placed():
    b = np.arange(SEG)
    tail, side = b[LANES:], LANES + SIDE
    last = np.concatenate([b[-LAST:], np.full(QUARTER - LAST, -1)])
    return np.concatenate([b[:LANES], tail, b[LANES:side], tail, b[side : side + SIDE], np.tile(last, 4)])


def dft_table():
    b = placed()
    angle = (np.outer(b, np.arange(SEG)) % SEG) * (2.0 * math.pi / SEG)
    cos, sin = np.cos(angle) * (b >= 0)[:, None], np.sin(angle) * (b >= 0)[:, None]
    table = np.zeros((6 * LANES, 2 * WIDE))
    for to, (re, im) in ((slice(0, SEG), (cos, sin)), (slice(WIDE, WIDE + SEG), (-sin, cos))):
        table[:WIDE, to], table[WIDE : 2 * WIDE, to] = re[:WIDE], im[:WIDE]
        table[2 * WIDE : 2 * WIDE + LANES, to], table[2 * WIDE + LANES :, to] = re[WIDE:], im[WIDE:]
    return table.astype(np.float32)


def twiddle_table():
    angle = np.outer(np.arange(WAVES), placed()) * (2.0 * math.pi / NLON)
    return np.concatenate([np.cos(angle), np.sin(angle)]).astype(np.float32)


def wave_table():
    k = np.arange(WAVES)[:, None] + PARTS * np.arange(SEG)[None, :]
    step = np.float32(math.pi / NLON)
    here = np.sin(k.astype(np.float32) * step) ** 2
    there = np.sin(((NLON - k) % NLON).astype(np.float32) * step) ** 2
    slope = 2.0 * np.sin(2.0 * math.pi * k / NLON)
    table = np.zeros((3 * WAVES, WIDE), np.float32)
    table[:, :SEG] = np.concatenate([here, there, slope])
    return table


def row_table():
    j = np.arange(-1, NLAT + 1)
    phi = np.float32(-0.5 * math.pi) + (j.astype(np.float32) + np.float32(0.5)) * np.float32(math.pi / NLAT)
    phi = phi.astype(np.float64)
    lat_step, lon_step = math.pi / NLAT, 2.0 * math.pi / NLON
    time_step = 0.25 * lat_step
    cos = np.cos(phi)
    y_coef = time_step / (2.0 * lat_step * cos)
    y_coef[0] = y_coef[-1] = 0.0
    table = np.zeros((NLAT, LANES))
    table[:, 0] = (cos / math.cos(0.25 * math.pi))[1:-1] ** 2
    table[:, 1] = (time_step / (2.0 * lon_step * cos))[1:-1]
    table[:, 2] = y_coef[1:-1]
    table[:, 3] = 0.3 * np.sin(phi)[1:-1]
    table[:, 4] = cos[1:-1]
    table[:, 5] = np.repeat(y_coef[0:NLAT:ROWS], ROWS)
    table[:, 6] = np.repeat(y_coef[ROWS + 1 :: ROWS], ROWS)
    table[:, 7] = np.arange(NLAT) // ROWS % 2
    return table.reshape(NLAT // ROWS, ROWS, LANES).astype(np.float32)


PUSH_COEF = 0.25 / 2.0


def add(x, y):
    if x is None:
        return y
    return x if y is None else x + y


def sub(x, y):
    if y is None:
        return x
    return -y if x is None else x - y


def times(z, cos, sin):
    re, im = z
    if abs(sin) < 1e-15:
        return (re * cos, None if im is None else im * cos)
    if im is None:
        return (re * cos, re * sin)
    return (re * cos - im * sin, re * sin + im * cos)


def real_fft(values):
    n = len(values)
    if n == 2:
        return [(values[0] + values[1], None), (values[0] - values[1], None)]
    even, odd = real_fft(values[0::2]), real_fft(values[1::2])
    out = [None] * (n // 2 + 1)
    out[0] = (even[0][0] + odd[0][0], None)
    out[n // 2] = (even[0][0] - odd[0][0], None)
    for k in range(1, n // 4):
        re, im = times(odd[k], math.cos(2 * math.pi * k / n), -math.sin(2 * math.pi * k / n))
        out[k] = (add(even[k][0], re), add(even[k][1], im))
        out[n // 2 - k] = (sub(even[k][0], re), sub(im, even[k][1]))
    out[n // 4] = (even[n // 4][0], -odd[n // 4][0])
    return out


def real_ifft(waves):
    n = 2 * (len(waves) - 1)
    if n == 2:
        return [waves[0][0] + waves[1][0], waves[0][0] - waves[1][0]]
    even, odd = [None] * (n // 4 + 1), [None] * (n // 4 + 1)
    even[0] = (waves[0][0] + waves[n // 2][0], None)
    odd[0] = (waves[0][0] - waves[n // 2][0], None)
    for k in range(1, n // 4):
        (re, im), (far_re, far_im) = waves[k], waves[n // 2 - k]
        even[k] = (re + far_re, im - far_im)
        odd[k] = times((re - far_re, im + far_im), math.cos(2 * math.pi * k / n), math.sin(2 * math.pi * k / n))
    even[n // 4] = (2.0 * waves[n // 4][0], None)
    odd[n // 4] = (-2.0 * waves[n // 4][1], None)
    out = [None] * n
    out[0::2], out[1::2] = real_ifft(even), real_ifft(odd)
    return out


def lane(shape):
    return lax.broadcasted_iota(jnp.int32, shape, 1)


def own_quarter(shape):
    return lane(shape) // QUARTER == lax.broadcasted_iota(jnp.int32, shape, 0) % 4


def fold(tile):
    size = tile.shape[0]
    mine = jnp.where(own_quarter(tile.shape), tile, 0.0)
    pairs = mine + pltpu.roll(mine, size - 1, 0)
    return pairs + pltpu.roll(pairs, size - 2, 0)


def holder(level, r, turned):
    return level * 16 + (15 - r if turned else r)


def spot(level, r, turned):
    return CHUNK * holder(level, r, turned)


def east(level, start, count):
    return pl.ds(2 * start + level, count, 2)


def pack_kernel(turn_ref, u_hbm, v_hbm, h_hbm, out_ref, u_ref, v_ref, h_ref, tail_ref, last_ref, sems):
    moves = [
        pltpu.make_async_copy(src, dst, sems.at[i])
        for i, (src, dst) in enumerate(((u_hbm, u_ref), (v_hbm, v_ref), (h_hbm, h_ref)))
    ]
    for move in moves:
        move.start()
    last_ref[...] = jnp.zeros_like(last_ref)
    for move in moves:
        move.wait()
    for level in range(2):
        tiles = [ref[east(level, 0, LANES), :].T for ref in (u_ref, v_ref, h_ref)]
        tail_ref[:TAIL, :] = u_ref[east(level, LANES, TAIL), :]
        tail_ref[TAIL:HALF, :] = h_ref[east(level, LANES, SIDE), :]
        tail_ref[HALF : HALF + TAIL, :] = v_ref[east(level, LANES, TAIL), :]
        tail_ref[HALF + TAIL :, :] = h_ref[east(level, LANES + SIDE, SIDE), :]
        tiles.append(tail_ref[...].T)
        last = h_ref[east(level, SEG - LAST, LAST), :]
        for g in range(4):
            last_ref[g * QUARTER : g * QUARTER + LAST, :] = last
        tail_ref[...] = fold(last_ref[...].T)
        folded = tail_ref[pl.ds(0, 32, 4), :]
        for turned in (False, True):

            @pl.when(turn_ref[0] == int(turned))
            def _():
                for r in range(16):
                    at = spot(level, r, turned)
                    for f in range(4):
                        out_ref[at + f * ROWS : at + (f + 1) * ROWS, :] = tiles[f][r * ROWS : (r + 1) * ROWS]
                    out_ref[at + 4 * ROWS : at + CHUNK, :] = folded[2 * r : 2 * r + 2]


def unpack_kernel(turn_ref, in_ref, u_ref, v_ref, h_ref, u_out, v_out, h_out, tile_ref):
    for level in range(2):
        for turned in (False, True):

            @pl.when(turn_ref[0] == int(turned))
            def _():
                for r in range(16):
                    at = spot(level, r, turned)
                    for f in range(4):
                        tile_ref[f, r * ROWS : (r + 1) * ROWS, :] = in_ref[at + f * ROWS : at + (f + 1) * ROWS, :]
                    for t in range(2):
                        row = in_ref[at + 4 * ROWS + t : at + 4 * ROWS + t + 1, :]
                        tile_ref[4, r * ROWS + 4 * t : r * ROWS + 4 * t + 4, :] = jnp.broadcast_to(row, (4, LANES))

        for f, (ref, out) in enumerate(((u_ref, u_out), (v_ref, v_out), (h_ref, h_out))):
            here = east(level, 0, LANES)
            out[here, :] = ref[here, :] + tile_ref[f].T
        mixed, quarters = tile_ref[3].T, tile_ref[4].T
        group = lane((LAST, LANES)) % 4
        last = quarters[:LAST]
        for g in range(1, 4):
            last = jnp.where(group == g, quarters[g * QUARTER : g * QUARTER + LAST], last)
        for ref, out, start, change in (
            (u_ref, u_out, LANES, mixed[:TAIL]),
            (h_ref, h_out, LANES, mixed[TAIL:HALF]),
            (v_ref, v_out, LANES, mixed[HALF : HALF + TAIL]),
            (h_ref, h_out, LANES + SIDE, mixed[HALF + TAIL :]),
            (h_ref, h_out, SEG - LAST, last),
        ):
            here = east(level, start, change.shape[0])
            out[here, :] = ref[here, :] + change


def halves(x):
    high = x.astype(jnp.bfloat16)
    return high, (x - high.astype(jnp.float32)).astype(jnp.bfloat16)


def dot(x, table, contract):
    def product(a, b):
        return lax.dot_general(a, b, (((1,), (contract,)), ((), ())), preferred_element_type=jnp.float32)

    (high, low), (table_high, table_low) = halves(x), halves(table)
    return product(high, table_high) + (product(high, table_low) + product(low, table_high))


BLOCK = WAVES * ROWS


def padded(fields):
    return -(-fields * BLOCK // 16) * 16


def transform(columns, table_ref, twiddle_ref, spec_ref, left_ref):
    at = lane((ROWS, LANES))
    own = (at < TAIL, (at >= HALF) & (at < HALF + TAIL))
    for get, part, fields in columns:
        lanes = slice(part * LANES, (part + 1) * LANES)
        late = slice(WIDE + part * LANES, WIDE + (part + 1) * LANES)
        for k1, (re, im) in enumerate(real_fft([get(a) for a in range(PARTS)])):
            cos = twiddle_ref[k1 : k1 + 1, lanes]
            sin = twiddle_ref[WAVES + k1 : WAVES + k1 + 1, lanes]
            if im is None:
                new_re, new_im = re * cos, -re * sin
            else:
                new_re, new_im = re * cos + im * sin, im * cos - re * sin
            for f, half in fields:
                rows = slice(f * BLOCK + k1 * ROWS, f * BLOCK + (k1 + 1) * ROWS)
                if part == 0:
                    left_ref[rows, lanes], left_ref[rows, late] = new_re, new_im
                else:
                    left_ref[rows, lanes] = jnp.where(own[half], new_re, 0.0)
                    left_ref[rows, late] = jnp.where(own[half], new_im, 0.0)
    spec_ref[...] = dot(left_ref[...], table_ref[: 2 * WIDE, :], 0)


def tiles_of(x_ref):
    def tile(f):
        return lambda a: x_ref[a * CHUNK + f * ROWS : a * CHUNK + (f + 1) * ROWS, :]

    return tile


def gather_tails(x_ref, tails_ref):
    at = lane((ROWS, LANES))
    place_of_four = lax.broadcasted_iota(jnp.int32, at.shape, 0) % 4
    for a in range(PARTS):
        base = a * CHUNK + 3 * ROWS
        mixed = x_ref[base : base + ROWS, :]
        rows = [jnp.broadcast_to(x_ref[base + ROWS + t : base + ROWS + t + 1, :], (4, LANES)) for t in range(2)]
        quarters, last = jnp.concatenate(rows, axis=0), None
        for g in range(4):
            moved = pltpu.roll(quarters, (2 * SIDE - g * QUARTER) % LANES, 1)
            last = moved if last is None else jnp.where(place_of_four == g, moved, last)
        beside_u, beside_v = pltpu.roll(mixed, LANES - TAIL, 1), pltpu.roll(mixed, HALF - TAIL + SIDE, 1)
        whole = jnp.where(at < SIDE, beside_u, jnp.where(at < 2 * SIDE, beside_v, last))
        tails_ref[a * ROWS : (a + 1) * ROWS, :] = jnp.where(at < HALF, whole, pltpu.roll(whole, HALF, 1))


H, UH, VH = range(3)
U, V = range(2)


def damping(row, wave_ref, k1):
    ratio2 = row[:, 0:1]
    here, there = wave_ref[k1 : k1 + 1, :], wave_ref[WAVES + k1 : WAVES + k1 + 1, :]
    return 0.5 * (ratio2 / jnp.maximum(here, ratio2) + ratio2 / jnp.maximum(there, ratio2))


REAL, IMAG = slice(0, WIDE), slice(WIDE, 2 * WIDE)


def rows_of(f, k1):
    return slice(f * BLOCK + k1 * ROWS, f * BLOCK + (k1 + 1) * ROWS)


def wind_kernel(x_ref, table_ref, twiddle_ref, wave_ref, row_ref, spec_ref, damp_ref, left_ref):
    tile = tiles_of(x_ref)
    columns = ((tile(0), 0, ((U, 0),)), (tile(1), 0, ((V, 0),)), (tile(3), 1, ((U, 0), (V, 1))))
    transform(columns, table_ref, twiddle_ref, spec_ref, left_ref)
    row = row_ref[0]
    rotation = row[:, 3:4]
    for k1 in range(WAVES):
        damp = SCALE * damping(row, wave_ref, k1)
        damp_ref[rows_of(0, k1), :] = damp
        turn = damp * rotation
        for span in (REAL, IMAG):
            spec_ref[rows_of(U, k1), span] = -turn * spec_ref[rows_of(U, k1), span]
            spec_ref[rows_of(V, k1), span] = turn * spec_ref[rows_of(V, k1), span]


def to_message(rows):
    tails = rows[:, LANES:]
    tails = jnp.where(lane((2, LANES)) < HALF, tails[:2], pltpu.roll(tails[2:], HALF, 1))
    return jnp.concatenate([rows[:, :LANES], tails, jnp.zeros((2, LANES), jnp.float32)], axis=0)


def from_message(message):
    tails = message[4:6]
    tails = jnp.concatenate([tails, pltpu.roll(tails, HALF, 1)], axis=0)
    return jnp.concatenate([message[:4], tails], axis=1)


def mass_kernel(
    x_ref, table_ref, twiddle_ref, wave_ref, row_ref, spec_ref, far_ref, near_ref, left_ref, tails_ref
):
    gather_tails(x_ref, tails_ref)
    tile = tiles_of(x_ref)

    def tail(a):
        return tails_ref[a * ROWS : (a + 1) * ROWS, :]

    def product(f, h):
        return lambda a: tile(f)(a) * h(a)

    columns = (
        (tile(2), 0, ((H, 0),)),
        (product(0, tile(2)), 0, ((UH, 0),)),
        (product(1, tile(2)), 0, ((VH, 0),)),
        (tail, 1, ((H, 0),)),
        (product(3, tail), 1, ((UH, 0), (VH, 1))),
    )
    transform(columns, table_ref, twiddle_ref, spec_ref, left_ref)
    row = row_ref[0]
    x_coef, y_coef, coslat, odd = row[:, 1:2], row[:, 2:3], row[:, 4:5], row[:4, 7:8] > 0.5
    for k1 in range(WAVES):
        damp = damping(row, wave_ref, k1)
        across = x_coef * wave_ref[2 * WAVES + k1 : 2 * WAVES + k1 + 1, :] * damp
        gain_re = across * spec_ref[rows_of(UH, k1), IMAG]
        gain_im = -across * spec_ref[rows_of(UH, k1), REAL]
        scale = damp * coslat
        up, down = [], []
        for span, gain in ((REAL, gain_re), (IMAG, gain_im)):
            spec_ref[rows_of(UH, k1), span] = gain
            mass = spec_ref[rows_of(H, k1), span] + gain
            flux = scale * spec_ref[rows_of(VH, k1), span]
            spec_ref[rows_of(VH, k1), span] = flux
            up += [flux[7:8], mass[7:8] + y_coef[7:8] * flux[6:7]]
            down += [flux[0:1], mass[0:1] - y_coef[0:1] * flux[1:2]]
        up, down = jnp.concatenate(up, axis=0), jnp.concatenate(down, axis=0)
        near_ref[rows_of(0, k1), :] = to_message(jnp.where(odd, down, up))
        far_ref[rows_of(0, k1), :] = to_message(jnp.where(odd, up, down))


def inverse_kernel(
    spec_ref, wind_ref, damp_ref, far_ref, near_ref, table_ref, twiddle_ref, wave_ref, row_ref, out_ref, left_ref,
    right_ref, last_ref
):
    row = row_ref[0]
    x_coef, y_coef = row[:, 1:2], row[:, 2:3]
    y_below, y_above = row[0:1, 5:6], row[0:1, 6:7]
    odd = row[:, 7:8] > 0.5
    for k1 in range(WAVES):
        near, far = near_ref[rows_of(0, k1), :], far_ref[rows_of(0, k1), :]
        below, above = from_message(jnp.where(odd, near, far)), from_message(jnp.where(odd, far, near))
        damp = damp_ref[rows_of(0, k1), :]
        across = damp * x_coef * wave_ref[2 * WAVES + k1 : 2 * WAVES + k1 + 1, :]
        along = -PUSH_COEF * damp
        mass = []
        for part, span in enumerate((REAL, IMAG)):
            flux = spec_ref[rows_of(VH, k1), span]
            flux_below, flux_above = below[2 * part : 2 * part + 1], above[2 * part : 2 * part + 1]
            prev = jnp.concatenate([flux_below, flux[:-1]], axis=0)
            following = jnp.concatenate([flux[1:], flux_above], axis=0)
            change = spec_ref[rows_of(UH, k1), span] - y_coef * (following - prev)
            new = spec_ref[rows_of(H, k1), span] + change
            new_below = below[2 * part + 1 : 2 * part + 2] - y_below * flux[0:1]
            new_above = above[2 * part + 1 : 2 * part + 2] + y_above * flux[7:8]
            mass.append(new)
            prev = jnp.concatenate([new_below, new[:-1]], axis=0)
            following = jnp.concatenate([new[1:], new_above], axis=0)
            left_ref[rows_of(2, k1), span] = along * (following - prev) + wind_ref[rows_of(U, k1), span]
            left_ref[rows_of(0, k1), span] = SCALE * change
        left_ref[rows_of(1, k1), REAL] = across * mass[1] + wind_ref[rows_of(V, k1), REAL]
        left_ref[rows_of(1, k1), IMAG] = wind_ref[rows_of(V, k1), IMAG] - across * mass[0]
    right_ref[...] = dot(left_ref[...], table_ref[: 2 * WIDE, :], 1)
    last_ref[...] = dot(left_ref[:BLOCK, :], table_ref[2 * WIDE :, :], 1)
    at = lane((ROWS, LANES))
    for f, part, fields in ((0, 0, (1,)), (1, 0, (2,)), (2, 0, (0,)), (3, 1, (0, 1, 2)), (4, 2, (0,))):
        lanes = slice(part * LANES, (part + 1) * LANES)
        source, start, late = (last_ref, 0, LANES) if part == 2 else (right_ref, part * LANES, WIDE + part * LANES)
        waves = []
        for k1 in range(WAVES):
            cos = twiddle_ref[k1 : k1 + 1, lanes]
            sin = twiddle_ref[WAVES + k1 : WAVES + k1 + 1, lanes]
            re = [source[rows_of(g, k1), start : start + LANES] for g in fields]
            im = [source[rows_of(g, k1), late : late + LANES] for g in fields]
            if len(fields) == 3:
                own = (at < TAIL, (at >= HALF) & (at < HALF + TAIL))
                re = [jnp.where(own[0], re[1], jnp.where(own[1], re[2], re[0]))]
                im = [jnp.where(own[0], im[1], jnp.where(own[1], im[2], im[0]))]
            re, im = re[0], im[0]
            waves.append((re * cos - im * sin, None if k1 in (0, WAVES - 1) else im * cos + re * sin))
        for a, value in enumerate(real_ifft(waves)):
            start = a * CHUNK + f * ROWS
            if f == 4:
                value = fold(value)
                value = jnp.concatenate([value[0:1], value[4:5]], axis=0)
            out_ref[start : start + value.shape[0], :] = value


def in_vmem():
    return pl.BlockSpec(memory_space=pltpu.VMEM)


PARAMS = pltpu.CompilerParams(vmem_limit_bytes=40 * 2**20)


def like(*shape):
    return jax.ShapeDtypeStruct(shape, jnp.float32)


def place(level, r, lat):
    return holder(level, r, lat % 2 == 0) * 16 + lat


def swaps(odd):
    pairs = []
    for level in range(2):
        for lat in range(16):
            pairs += [(place(level, r, lat), place(level, r + 1, lat)) for r in range(odd, 15, 2)]
            if odd and lat < 15:
                pairs.append((place(level, 15, lat), place(level, 0, lat + 1)))
    return pairs + [(b, a) for a, b in pairs]


def in_smem():
    return pl.BlockSpec(memory_space=pltpu.SMEM)


def pack(turned, u, v, h):
    return pl.pallas_call(
        pack_kernel,
        out_shape=like(PARTS * CHUNK, LANES),
        in_specs=[in_smem()] + [pl.BlockSpec(memory_space=pltpu.HBM)] * 3,
        out_specs=in_vmem(),
        scratch_shapes=[pltpu.VMEM((2 * SEG, LANES), jnp.float32)] * 3
        + [pltpu.VMEM((LANES, LANES), jnp.float32)] * 2
        + [pltpu.SemaphoreType.DMA((3,))],
        compiler_params=pltpu.CompilerParams(vmem_limit_bytes=56 * 2**20),
        name="pack",
    )(turned, u, v, h)


def cost(fields):
    size = padded(fields) * 2 * WIDE
    return pl.CostEstimate(flops=6 * size * 2 * WIDE, bytes_accessed=8 * size, transcendentals=0)


def forward_mass(whole, row):
    return pl.pallas_call(
        mass_kernel,
        out_shape=(like(padded(3), 2 * WIDE), like(BLOCK, LANES), like(BLOCK, LANES)),
        in_specs=[in_vmem()] * 5,
        out_specs=(in_vmem(),) * 3,
        scratch_shapes=[pltpu.VMEM((padded(3), 2 * WIDE), jnp.float32), pltpu.VMEM((PARTS * ROWS, LANES), jnp.float32)],
        compiler_params=PARAMS,
        cost_estimate=cost(3),
        name="forward_mass",
    )(whole, dft_table(), twiddle_table(), wave_table(), row)


def forward_wind(whole, row):
    return pl.pallas_call(
        wind_kernel,
        out_shape=(like(padded(2), 2 * WIDE), like(BLOCK, WIDE)),
        in_specs=[in_vmem()] * 5,
        out_specs=(in_vmem(),) * 2,
        scratch_shapes=[pltpu.VMEM((padded(2), 2 * WIDE), jnp.float32)],
        compiler_params=PARAMS,
        cost_estimate=cost(2),
        name="forward_wind",
    )(whole, dft_table(), twiddle_table(), wave_table(), row)


def inverse(spec, wind, damp, far, near, row):
    return pl.pallas_call(
        inverse_kernel,
        out_shape=like(PARTS * CHUNK, LANES),
        in_specs=[in_vmem()] * 9,
        out_specs=in_vmem(),
        scratch_shapes=[pltpu.VMEM((padded(3), 2 * WIDE), jnp.float32)] * 2 + [pltpu.VMEM((BLOCK, WIDE), jnp.float32)],
        compiler_params=PARAMS,
        cost_estimate=cost(3),
        name="inverse",
    )(spec, wind, damp, far, near, dft_table(), twiddle_table(), wave_table(), row)


def unpack(turned, back, u, v, h):
    return pl.pallas_call(
        unpack_kernel,
        out_shape=(like(2 * SEG, LANES),) * 3,
        in_specs=[in_smem()] + [in_vmem()] * 4,
        out_specs=(in_vmem(),) * 3,
        scratch_shapes=[pltpu.VMEM((5, LANES, LANES), jnp.float32)],
        compiler_params=PARAMS,
        name="unpack",
    )(turned, back, u, v, h)


def row_of(group):
    return lax.dynamic_slice_in_dim(jnp.asarray(row_table()), group, 1, axis=0)


def exchange(chunks):
    moved = lax.all_to_all(chunks.reshape(PARTS, CHUNK, 1, LANES), "lon", 0, 0, tiled=True)
    return moved.reshape(PARTS * CHUNK, LANES)


def step(u, v, h):
    lat = lax.axis_index("lat")
    turned = 1 - lat % 2
    r = lax.axis_index("lon") % 16
    row = row_of(lat * 16 + jnp.where(turned == 1, 15 - r, r))
    turned = turned.reshape(1)
    u, v, h = (jnp.swapaxes(x, 0, 1).reshape(2 * SEG, LANES) for x in (u, v, h))
    whole = exchange(pack(turned, u, v, h))
    spec, far, near = forward_mass(whole, row)
    far = lax.ppermute(far, ("lon", "lat"), swaps(1))
    near = lax.ppermute(near, ("lon", "lat"), swaps(0))
    wind, damp = forward_wind(whole, row)
    outs = unpack(turned, exchange(inverse(spec, wind, damp, far, near, row)), u, v, h)
    return tuple(jnp.swapaxes(x.reshape(SEG, 2, LANES), 0, 1) for x in outs)


def solution(mesh):
    spec = P(None, "lon", "lat")
    return jax.shard_map(step, mesh=mesh, in_specs=(spec,) * 3, out_specs=(spec,) * 3, check_vma=False)
```

```python
import functools
import math

import jax
import jax.numpy as jnp
import numpy as np
from jax import lax
from jax.experimental import pallas as pl
from jax.experimental.pallas import tpu as pltpu
from jax.sharding import PartitionSpec as P

NLON = 5760
NLAT = 2048
PARTS = 32
SEG = 180
LANES = 128
TAIL = SEG - LANES
HALF = 64
ROWS = 8
WAVES = PARTS // 2 + 1
WIDE = 2 * LANES
SCALE = 1.0 / NLON
SIDE = HALF - TAIL
LAST = TAIL - 2 * SIDE
QUARTER = 32
CHUNK = 4 * ROWS + 2


def placed():
    b = np.arange(SEG)
    tail, side = b[LANES:], LANES + SIDE
    last = np.concatenate([b[-LAST:], np.full(QUARTER - LAST, -1)])
    return np.concatenate([b[:LANES], tail, b[LANES:side], tail, b[side : side + SIDE], np.tile(last, 4)])


def dft_table():
    b = placed()
    angle = (np.outer(b, np.arange(SEG)) % SEG) * (2.0 * math.pi / SEG)
    cos, sin = np.cos(angle) * (b >= 0)[:, None], np.sin(angle) * (b >= 0)[:, None]
    table = np.zeros((6 * LANES, 2 * WIDE))
    for to, (re, im) in ((slice(0, SEG), (cos, sin)), (slice(WIDE, WIDE + SEG), (-sin, cos))):
        table[:WIDE, to], table[WIDE : 2 * WIDE, to] = re[:WIDE], im[:WIDE]
        table[2 * WIDE : 2 * WIDE + LANES, to], table[2 * WIDE + LANES :, to] = re[WIDE:], im[WIDE:]
    return table.astype(np.float32)


def twiddle_table():
    angle = np.outer(np.arange(WAVES), placed()) * (2.0 * math.pi / NLON)
    return np.concatenate([np.cos(angle), np.sin(angle)]).astype(np.float32)


def wave_table():
    k = np.arange(WAVES)[:, None] + PARTS * np.arange(SEG)[None, :]
    step = np.float32(math.pi / NLON)
    here = np.sin(k.astype(np.float32) * step) ** 2
    there = np.sin(((NLON - k) % NLON).astype(np.float32) * step) ** 2
    slope = 2.0 * np.sin(2.0 * math.pi * k / NLON)
    table = np.zeros((3 * WAVES, WIDE), np.float32)
    table[:, :SEG] = np.concatenate([here, there, slope])
    return table


def row_table():
    j = np.arange(-1, NLAT + 1)
    phi = np.float32(-0.5 * math.pi) + (j.astype(np.float32) + np.float32(0.5)) * np.float32(math.pi / NLAT)
    phi = phi.astype(np.float64)
    lat_step, lon_step = math.pi / NLAT, 2.0 * math.pi / NLON
    time_step = 0.25 * lat_step
    cos = np.cos(phi)
    y_coef = time_step / (2.0 * lat_step * cos)
    y_coef[0] = y_coef[-1] = 0.0
    table = np.zeros((NLAT, LANES))
    table[:, 0] = (cos / math.cos(0.25 * math.pi))[1:-1] ** 2
    table[:, 1] = (time_step / (2.0 * lon_step * cos))[1:-1]
    table[:, 2] = y_coef[1:-1]
    table[:, 3] = 0.3 * np.sin(phi)[1:-1]
    table[:, 4] = cos[1:-1]
    table[:, 5] = np.repeat(y_coef[0:NLAT:ROWS], ROWS)
    table[:, 6] = np.repeat(y_coef[ROWS + 1 :: ROWS], ROWS)
    table[:, 7] = np.arange(NLAT) // ROWS % 2
    return table.reshape(NLAT // ROWS, ROWS, LANES).astype(np.float32)


PUSH_COEF = 0.25 / 2.0
FIRST = 20
ORDER = [(i + FIRST) % PARTS for i in range(PARTS)]


def add(x, y):
    if x is None:
        return y
    return x if y is None else x + y


def sub(x, y):
    if y is None:
        return x
    return -y if x is None else x - y


def times(z, cos, sin):
    re, im = z
    if abs(sin) < 1e-15:
        return (re * cos, None if im is None else im * cos)
    if im is None:
        return (re * cos, re * sin)
    return (re * cos - im * sin, re * sin + im * cos)


def real_fft(values):
    n = len(values)
    if n == 2:
        return [(values[0] + values[1], None), (values[0] - values[1], None)]
    even, odd = real_fft(values[0::2]), real_fft(values[1::2])
    out = [None] * (n // 2 + 1)
    out[0] = (even[0][0] + odd[0][0], None)
    out[n // 2] = (even[0][0] - odd[0][0], None)
    for k in range(1, n // 4):
        re, im = times(odd[k], math.cos(2 * math.pi * k / n), -math.sin(2 * math.pi * k / n))
        out[k] = (add(even[k][0], re), add(even[k][1], im))
        out[n // 2 - k] = (sub(even[k][0], re), sub(im, even[k][1]))
    out[n // 4] = (even[n // 4][0], -odd[n // 4][0])
    return out


def real_ifft(waves):
    n = 2 * (len(waves) - 1)
    if n == 2:
        return [waves[0][0] + waves[1][0], waves[0][0] - waves[1][0]]
    even, odd = [None] * (n // 4 + 1), [None] * (n // 4 + 1)
    even[0] = (waves[0][0] + waves[n // 2][0], None)
    odd[0] = (waves[0][0] - waves[n // 2][0], None)
    for k in range(1, n // 4):
        (re, im), (far_re, far_im) = waves[k], waves[n // 2 - k]
        even[k] = (re + far_re, im - far_im)
        odd[k] = times((re - far_re, im + far_im), math.cos(2 * math.pi * k / n), math.sin(2 * math.pi * k / n))
    even[n // 4] = (2.0 * waves[n // 4][0], None)
    odd[n // 4] = (-2.0 * waves[n // 4][1], None)
    out = [None] * n
    out[0::2], out[1::2] = real_ifft(even), real_ifft(odd)
    return out


def lane(shape):
    return lax.broadcasted_iota(jnp.int32, shape, 1)


def own_quarter(shape):
    return lane(shape) // QUARTER == lax.broadcasted_iota(jnp.int32, shape, 0) % 4


def fold(tile):
    size = tile.shape[0]
    mine = jnp.where(own_quarter(tile.shape), tile, 0.0)
    pairs = mine + pltpu.roll(mine, size - 1, 0)
    return pairs + pltpu.roll(pairs, size - 2, 0)


def chunk_at(lon):
    return CHUNK * ORDER.index(lon)


def holder(level, r, turned):
    return level * 16 + (15 - r if turned else r)


def spot(level, r, turned):
    return chunk_at(holder(level, r, turned))


def east(level, start, count):
    return pl.ds(2 * start + level, count, 2)


def pack_kernel(turn_ref, u_hbm, v_hbm, h_hbm, out_ref, u_ref, v_ref, h_ref, tail_ref, last_ref, sems):
    moves = [
        pltpu.make_async_copy(src, dst, sems.at[i])
        for i, (src, dst) in enumerate(((u_hbm, u_ref), (v_hbm, v_ref), (h_hbm, h_ref)))
    ]
    for move in moves:
        move.start()
    last_ref[...] = jnp.zeros_like(last_ref)
    whole = []
    for move, ref in zip(moves, (u_ref, v_ref, h_ref)):
        move.wait()
        whole.append([ref[east(level, 0, LANES), :].T for level in range(2)])
    for level in range(2):
        tiles = [pair[level] for pair in whole]
        tail_ref[:TAIL, :] = u_ref[east(level, LANES, TAIL), :]
        tail_ref[TAIL:HALF, :] = h_ref[east(level, LANES, SIDE), :]
        tail_ref[HALF : HALF + TAIL, :] = v_ref[east(level, LANES, TAIL), :]
        tail_ref[HALF + TAIL :, :] = h_ref[east(level, LANES + SIDE, SIDE), :]
        tiles.append(tail_ref[...].T)
        last = h_ref[east(level, SEG - LAST, LAST), :]
        for g in range(4):
            last_ref[g * QUARTER : g * QUARTER + LAST, :] = last
        tail_ref[...] = fold(last_ref[...].T)
        folded = tail_ref[pl.ds(0, 32, 4), :]
        for turned in (False, True):

            @pl.when(turn_ref[0] == int(turned))
            def _():
                for r in range(16):
                    at = spot(level, r, turned)
                    for f in range(4):
                        out_ref[at + f * ROWS : at + (f + 1) * ROWS, :] = tiles[f][r * ROWS : (r + 1) * ROWS]
                    out_ref[at + 4 * ROWS : at + CHUNK, :] = folded[2 * r : 2 * r + 2]


def unpack_kernel(
    turn_ref, in_ref, u_ref, v_ref, h_ref, u_hbm, v_hbm, h_hbm, u_out, v_out, h_out, tile_ref, sems
):
    for level in range(2):
        for turned in (False, True):

            @pl.when(turn_ref[0] == int(turned))
            def _():
                for r in range(16):
                    at = spot(level, r, turned)
                    here = slice(r * ROWS, (r + 1) * ROWS)
                    for f in range(4):
                        tile_ref[level, f, here, :] = in_ref[at + f * ROWS : at + (f + 1) * ROWS, :]
                    for t in range(2):
                        row = in_ref[at + 4 * ROWS + t : at + 4 * ROWS + t + 1, :]
                        here = slice(r * ROWS + 4 * t, r * ROWS + 4 * t + 4)
                        tile_ref[level, 4, here, :] = jnp.broadcast_to(row, (4, LANES))

    mixed = [tile_ref[level, 3].T for level in range(2)]
    moves = []
    for f, (ref, out, hbm) in enumerate(((u_ref, u_out, u_hbm), (v_ref, v_out, v_hbm), (h_ref, h_out, h_hbm))):
        for level in range(2):
            if f < 2:
                changes = ((LANES, mixed[level][f * HALF : f * HALF + TAIL]),)
            else:
                quarters = tile_ref[level, 4].T
                group = lane((LAST, LANES)) % 4
                last = quarters[:LAST]
                for g in range(1, 4):
                    last = jnp.where(group == g, quarters[g * QUARTER : g * QUARTER + LAST], last)
                changes = (
                    (LANES, mixed[level][TAIL:HALF]), (LANES + SIDE, mixed[level][HALF + TAIL :]), (SEG - LAST, last)
                )
            for start, change in ((0, tile_ref[level, f].T), *changes):
                here = east(level, start, change.shape[0])
                out[here, :] = ref[here, :] + change
        moves.append(pltpu.make_async_copy(out, hbm, sems.at[f]))
        moves[-1].start()
    for move in moves:
        move.wait()


def halves(x):
    high = x.astype(jnp.bfloat16)
    return high, (x - high.astype(jnp.float32)).astype(jnp.bfloat16)


def dot(x, table, contract):
    def product(a, b):
        return lax.dot_general(a, b, (((1,), (contract,)), ((), ())), preferred_element_type=jnp.float32)

    (high, low), (table_high, table_low) = halves(x), table
    return product(high, table_high) + (product(high, table_low) + product(low, table_high))


BLOCK = WAVES * ROWS


def padded(fields):
    return -(-fields * BLOCK // 16) * 16


def transform(columns, high_ref, low_ref, twiddle_ref, spec_ref, left_ref):
    at = lane((ROWS, LANES))
    own = (at < TAIL, (at >= HALF) & (at < HALF + TAIL))
    for get, part, fields in columns:
        lanes = slice(part * LANES, (part + 1) * LANES)
        late = slice(WIDE + part * LANES, WIDE + (part + 1) * LANES)
        for k1, (re, im) in enumerate(real_fft([get(a) for a in range(PARTS)])):
            cos = twiddle_ref[k1 : k1 + 1, lanes]
            sin = twiddle_ref[WAVES + k1 : WAVES + k1 + 1, lanes]
            if im is None:
                new_re, new_im = re * cos, -re * sin
            else:
                new_re, new_im = re * cos + im * sin, im * cos - re * sin
            for f, half in fields:
                rows = slice(f * BLOCK + k1 * ROWS, f * BLOCK + (k1 + 1) * ROWS)
                if part == 0:
                    left_ref[rows, lanes], left_ref[rows, late] = new_re, new_im
                else:
                    left_ref[rows, lanes] = jnp.where(own[half], new_re, 0.0)
                    left_ref[rows, late] = jnp.where(own[half], new_im, 0.0)
    table = high_ref[: 2 * WIDE, :], low_ref[: 2 * WIDE, :]
    spec_ref[...] = dot(left_ref[...], table, 0)


def tiles_of(x_ref):
    def tile(f):
        return lambda a: x_ref[chunk_at(a) + f * ROWS : chunk_at(a) + (f + 1) * ROWS, :]

    return tile


def gather_tails(x_ref, tails_ref):
    at = lane((ROWS, LANES))
    place_of_four = lax.broadcasted_iota(jnp.int32, at.shape, 0) % 4
    for a in range(PARTS):
        base = chunk_at(a) + 3 * ROWS
        mixed = x_ref[base : base + ROWS, :]
        rows = [jnp.broadcast_to(x_ref[base + ROWS + t : base + ROWS + t + 1, :], (4, LANES)) for t in range(2)]
        quarters, last = jnp.concatenate(rows, axis=0), None
        for g in range(4):
            moved = pltpu.roll(quarters, (2 * SIDE - g * QUARTER) % LANES, 1)
            last = moved if last is None else jnp.where(place_of_four == g, moved, last)
        beside_u, beside_v = pltpu.roll(mixed, LANES - TAIL, 1), pltpu.roll(mixed, HALF - TAIL + SIDE, 1)
        whole = jnp.where(at < SIDE, beside_u, jnp.where(at < 2 * SIDE, beside_v, last))
        tails_ref[a * ROWS : (a + 1) * ROWS, :] = jnp.where(at < HALF, whole, pltpu.roll(whole, HALF, 1))


H, UH, VH = range(3)
U, V = range(2)


REAL, IMAG = slice(0, WIDE), slice(WIDE, 2 * WIDE)


def rows_of(f, k1):
    return slice(f * BLOCK + k1 * ROWS, f * BLOCK + (k1 + 1) * ROWS)


def factor_kernel(table_ref, wave_ref, row_ref, high_ref, low_ref, gain_ref, flux_ref, turn_ref, across_ref, along_ref):
    high_ref[...], low_ref[...] = halves(table_ref[...])
    row = row_ref[0]
    ratio2, x_coef, rotation, coslat = row[:, 0:1], row[:, 1:2], row[:, 3:4], row[:, 4:5]
    for k1 in range(WAVES):
        here, there, slope = (wave_ref[i * WAVES + k1 : i * WAVES + k1 + 1, :] for i in range(3))
        damp = 0.5 * (ratio2 / jnp.maximum(here, ratio2) + ratio2 / jnp.maximum(there, ratio2))
        across = x_coef * slope * damp
        gain_ref[rows_of(0, k1), :] = across
        flux_ref[rows_of(0, k1), :] = damp * coslat
        damp = SCALE * damp
        turn_ref[rows_of(0, k1), :] = damp * rotation
        across_ref[rows_of(0, k1), :] = SCALE * across
        along_ref[rows_of(0, k1), :] = -PUSH_COEF * damp


def wind_kernel(x_ref, high_ref, low_ref, twiddle_ref, turn_ref, spec_ref, left_ref):
    tile = tiles_of(x_ref)
    columns = ((tile(0), 0, ((U, 0),)), (tile(1), 0, ((V, 0),)), (tile(3), 1, ((U, 0), (V, 1))))
    transform(columns, high_ref, low_ref, twiddle_ref, spec_ref, left_ref)
    for k1 in range(WAVES):
        turn = turn_ref[rows_of(0, k1), :]
        for span in (REAL, IMAG):
            spec_ref[rows_of(U, k1), span] = -turn * spec_ref[rows_of(U, k1), span]
            spec_ref[rows_of(V, k1), span] = turn * spec_ref[rows_of(V, k1), span]


def to_message(rows):
    tails = rows[:, LANES:]
    tails = jnp.where(lane((2, LANES)) < HALF, tails[:2], pltpu.roll(tails[2:], HALF, 1))
    return jnp.concatenate([rows[:, :LANES], tails, jnp.zeros((2, LANES), jnp.float32)], axis=0)


def from_message(message):
    tails = message[4:6]
    tails = jnp.concatenate([tails, pltpu.roll(tails, HALF, 1)], axis=0)
    return jnp.concatenate([message[:4], tails], axis=1)


def mass_kernel(
    x_ref, high_ref, low_ref, twiddle_ref, gain_ref, scale_ref, row_ref, spec_ref, far_ref, near_ref, left_ref, tails_ref
):
    gather_tails(x_ref, tails_ref)
    tile = tiles_of(x_ref)

    def tail(a):
        return tails_ref[a * ROWS : (a + 1) * ROWS, :]

    def product(f, h):
        return lambda a: tile(f)(a) * h(a)

    columns = (
        (tile(2), 0, ((H, 0),)),
        (product(0, tile(2)), 0, ((UH, 0),)),
        (product(1, tile(2)), 0, ((VH, 0),)),
        (tail, 1, ((H, 0),)),
        (product(3, tail), 1, ((UH, 0), (VH, 1))),
    )
    transform(columns, high_ref, low_ref, twiddle_ref, spec_ref, left_ref)
    row = row_ref[0]
    y_coef, odd = row[:, 2:3], row[:4, 7:8] > 0.5
    for k1 in range(WAVES):
        across, scale = gain_ref[rows_of(0, k1), :], scale_ref[rows_of(0, k1), :]
        gain_re = across * spec_ref[rows_of(UH, k1), IMAG]
        gain_im = -across * spec_ref[rows_of(UH, k1), REAL]
        up, down = [], []
        for span, gain in ((REAL, gain_re), (IMAG, gain_im)):
            spec_ref[rows_of(UH, k1), span] = gain
            mass = spec_ref[rows_of(H, k1), span] + gain
            flux = scale * spec_ref[rows_of(VH, k1), span]
            spec_ref[rows_of(VH, k1), span] = flux
            up += [flux[7:8], mass[7:8] + y_coef[7:8] * flux[6:7]]
            down += [flux[0:1], mass[0:1] - y_coef[0:1] * flux[1:2]]
        up, down = jnp.concatenate(up, axis=0), jnp.concatenate(down, axis=0)
        near_ref[rows_of(0, k1), :] = to_message(jnp.where(odd, down, up))
        far_ref[rows_of(0, k1), :] = to_message(jnp.where(odd, up, down))


def inverse_kernel(
    spec_ref, wind_ref, far_ref, near_ref, high_ref, low_ref, twiddle_ref, across_ref, along_ref, row_ref, out_ref,
    left_ref, right_ref, last_ref
):
    row = row_ref[0]
    y_coef = row[:, 2:3]
    y_below, y_above = row[0:1, 5:6], row[0:1, 6:7]
    odd = row[:, 7:8] > 0.5
    for k1 in range(WAVES):
        near, far = near_ref[rows_of(0, k1), :], far_ref[rows_of(0, k1), :]
        below, above = from_message(jnp.where(odd, near, far)), from_message(jnp.where(odd, far, near))
        across, along = across_ref[rows_of(0, k1), :], along_ref[rows_of(0, k1), :]
        mass = []
        for part, span in enumerate((REAL, IMAG)):
            flux = spec_ref[rows_of(VH, k1), span]
            flux_below, flux_above = below[2 * part : 2 * part + 1], above[2 * part : 2 * part + 1]
            prev = jnp.concatenate([flux_below, flux[:-1]], axis=0)
            following = jnp.concatenate([flux[1:], flux_above], axis=0)
            change = spec_ref[rows_of(UH, k1), span] - y_coef * (following - prev)
            new = spec_ref[rows_of(H, k1), span] + change
            new_below = below[2 * part + 1 : 2 * part + 2] - y_below * flux[0:1]
            new_above = above[2 * part + 1 : 2 * part + 2] + y_above * flux[7:8]
            mass.append(new)
            prev = jnp.concatenate([new_below, new[:-1]], axis=0)
            following = jnp.concatenate([new[1:], new_above], axis=0)
            left_ref[rows_of(2, k1), span] = along * (following - prev) + wind_ref[rows_of(U, k1), span]
            left_ref[rows_of(0, k1), span] = SCALE * change
        left_ref[rows_of(1, k1), REAL] = across * mass[1] + wind_ref[rows_of(V, k1), REAL]
        left_ref[rows_of(1, k1), IMAG] = wind_ref[rows_of(V, k1), IMAG] - across * mass[0]
    right_ref[...] = dot(left_ref[...], (high_ref[: 2 * WIDE, :], low_ref[: 2 * WIDE, :]), 1)
    last_ref[...] = dot(left_ref[:BLOCK, :], (high_ref[2 * WIDE :, :], low_ref[2 * WIDE :, :]), 1)
    at = lane((ROWS, LANES))
    for f, part, fields in ((0, 0, (1,)), (1, 0, (2,)), (2, 0, (0,)), (3, 1, (0, 1, 2)), (4, 2, (0,))):
        lanes = slice(part * LANES, (part + 1) * LANES)
        source, start, late = (last_ref, 0, LANES) if part == 2 else (right_ref, part * LANES, WIDE + part * LANES)
        waves = []
        for k1 in range(WAVES):
            cos = twiddle_ref[k1 : k1 + 1, lanes]
            sin = twiddle_ref[WAVES + k1 : WAVES + k1 + 1, lanes]
            re = [source[rows_of(g, k1), start : start + LANES] for g in fields]
            im = [source[rows_of(g, k1), late : late + LANES] for g in fields]
            if len(fields) == 3:
                own = (at < TAIL, (at >= HALF) & (at < HALF + TAIL))
                re = [jnp.where(own[0], re[1], jnp.where(own[1], re[2], re[0]))]
                im = [jnp.where(own[0], im[1], jnp.where(own[1], im[2], im[0]))]
            re, im = re[0], im[0]
            waves.append((re * cos - im * sin, None if k1 in (0, WAVES - 1) else im * cos + re * sin))
        for a, value in enumerate(real_ifft(waves)):
            start = chunk_at(a) + f * ROWS
            if f == 4:
                value = fold(value)
                value = jnp.concatenate([value[0:1], value[4:5]], axis=0)
            out_ref[start : start + value.shape[0], :] = value


def in_vmem():
    return pl.BlockSpec(memory_space=pltpu.VMEM)


PARAMS = pltpu.CompilerParams(vmem_limit_bytes=40 * 2**20)


def like(*shape):
    return jax.ShapeDtypeStruct(shape, jnp.float32)


def place(level, r, lat):
    return holder(level, r, lat % 2 == 0) * 16 + lat


def swaps(odd):
    pairs = []
    for level in range(2):
        for lat in range(16):
            pairs += [(place(level, r, lat), place(level, r + 1, lat)) for r in range(odd, 15, 2)]
            if odd and lat < 15:
                pairs.append((place(level, 15, lat), place(level, 0, lat + 1)))
    return pairs + [(b, a) for a, b in pairs]


def in_smem():
    return pl.BlockSpec(memory_space=pltpu.SMEM)


def pack(turned, u, v, h):
    return pl.pallas_call(
        pack_kernel,
        out_shape=like(PARTS * CHUNK, LANES),
        in_specs=[in_smem()] + [pl.BlockSpec(memory_space=pltpu.HBM)] * 3,
        out_specs=in_vmem(),
        scratch_shapes=[pltpu.VMEM((2 * SEG, LANES), jnp.float32)] * 3
        + [pltpu.VMEM((LANES, LANES), jnp.float32)] * 2
        + [pltpu.SemaphoreType.DMA((3,))],
        compiler_params=pltpu.CompilerParams(vmem_limit_bytes=56 * 2**20),
        name="pack",
    )(turned, u, v, h)


def cost(fields):
    size = padded(fields) * 2 * WIDE
    return pl.CostEstimate(flops=6 * size * 2 * WIDE, bytes_accessed=8 * size, transcendentals=0)


def factors(row):
    table = jax.ShapeDtypeStruct((6 * LANES, 2 * WIDE), jnp.bfloat16)
    return pl.pallas_call(
        factor_kernel,
        out_shape=(table, table) + (like(BLOCK, WIDE),) * 5,
        in_specs=[in_vmem()] * 3,
        out_specs=(in_vmem(),) * 7,
        compiler_params=PARAMS,
        cost_estimate=pl.CostEstimate(flops=2**24, bytes_accessed=2**24, transcendentals=0),
        name="factors",
    )(dft_table(), wave_table(), row)


def forward_mass(whole, high, low, gain, scale, row):
    return pl.pallas_call(
        mass_kernel,
        out_shape=(like(padded(3), 2 * WIDE), like(BLOCK, LANES), like(BLOCK, LANES)),
        in_specs=[in_vmem()] * 7,
        out_specs=(in_vmem(),) * 3,
        scratch_shapes=[pltpu.VMEM((padded(3), 2 * WIDE), jnp.float32), pltpu.VMEM((PARTS * ROWS, LANES), jnp.float32)],
        compiler_params=PARAMS,
        cost_estimate=cost(3),
        name="forward_mass",
    )(whole, high, low, twiddle_table(), gain, scale, row)


def forward_wind(whole, high, low, turn):
    return pl.pallas_call(
        wind_kernel,
        out_shape=like(padded(2), 2 * WIDE),
        in_specs=[in_vmem()] * 5,
        out_specs=in_vmem(),
        scratch_shapes=[pltpu.VMEM((padded(2), 2 * WIDE), jnp.float32)],
        compiler_params=PARAMS,
        cost_estimate=cost(2),
        name="forward_wind",
    )(whole, high, low, twiddle_table(), turn)


def inverse(spec, wind, far, near, high, low, across, along, row):
    return pl.pallas_call(
        inverse_kernel,
        out_shape=like(PARTS * CHUNK, LANES),
        in_specs=[in_vmem()] * 10,
        out_specs=in_vmem(),
        scratch_shapes=[pltpu.VMEM((padded(3), 2 * WIDE), jnp.float32)] * 2 + [pltpu.VMEM((BLOCK, WIDE), jnp.float32)],
        compiler_params=PARAMS,
        cost_estimate=cost(3),
        name="inverse",
    )(spec, wind, far, near, high, low, twiddle_table(), across, along, row)


def unpack(turned, back, u, v, h):
    return pl.pallas_call(
        unpack_kernel,
        out_shape=(like(2 * SEG, LANES),) * 3,
        in_specs=[in_smem()] + [in_vmem()] * 4,
        out_specs=(pl.BlockSpec(memory_space=pltpu.HBM),) * 3,
        scratch_shapes=[pltpu.VMEM((2 * SEG, LANES), jnp.float32)] * 3
        + [pltpu.VMEM((2, 5, LANES, LANES), jnp.float32), pltpu.SemaphoreType.DMA((3,))],
        compiler_params=PARAMS,
        name="unpack",
    )(turned, back, u, v, h)


def row_of(group):
    return lax.dynamic_slice_in_dim(jnp.asarray(row_table()), group, 1, axis=0)


def exchange(chunks):
    moved = lax.all_to_all(chunks.reshape(PARTS, CHUNK, 1, LANES), "lon", 0, 0, axis_index_groups=[ORDER], tiled=True)
    return moved.reshape(PARTS * CHUNK, LANES)


def step(u, v, h):
    lat = lax.axis_index("lat")
    turned = 1 - lat % 2
    r = lax.axis_index("lon") % 16
    row = row_of(lat * 16 + jnp.where(turned == 1, 15 - r, r))
    turned = turned.reshape(1)
    u, v, h = (jnp.swapaxes(x, 0, 1).reshape(2 * SEG, LANES) for x in (u, v, h))
    high, low, gain, scale, turn, across, along = factors(row)
    whole = exchange(pack(turned, u, v, h))
    spec, far, near = forward_mass(whole, high, low, gain, scale, row)
    far = lax.ppermute(far, ("lon", "lat"), swaps(1))
    near = lax.ppermute(near, ("lon", "lat"), swaps(0))
    wind = forward_wind(whole, high, low, turn)
    back = exchange(inverse(spec, wind, far, near, high, low, across, along, row))
    outs = unpack(turned, back, u, v, h)
    return tuple(jnp.swapaxes(x.reshape(SEG, 2, LANES), 0, 1) for x in outs)


def solution(mesh):
    spec = P(None, "lon", "lat")
    return jax.shard_map(step, mesh=mesh, in_specs=(spec,) * 3, out_specs=(spec,) * 3, check_vma=False)
```

```python
import functools
import math

import jax
import jax.numpy as jnp
import numpy as np
from jax import lax
from jax.experimental import pallas as pl
from jax.experimental.pallas import tpu as pltpu
from jax.sharding import PartitionSpec as P

NLON = 5760
NLAT = 2048
PARTS = 32
SEG = 180
LANES = 128
TAIL = SEG - LANES
HALF = 64
ROWS = 8
WAVES = PARTS // 2 + 1
WIDE = 2 * LANES
SCALE = 1.0 / NLON
SIDE = HALF - TAIL
LAST = TAIL - 2 * SIDE
QUARTER = 32
CHUNK = 4 * ROWS + 2


def placed():
    b = np.arange(SEG)
    tail, side = b[LANES:], LANES + SIDE
    last = np.concatenate([b[-LAST:], np.full(QUARTER - LAST, -1)])
    return np.concatenate([b[:LANES], tail, b[LANES:side], tail, b[side : side + SIDE], np.tile(last, 4)])


def dft_table():
    b = placed()
    angle = (np.outer(b, np.arange(SEG)) % SEG) * (2.0 * math.pi / SEG)
    cos, sin = np.cos(angle) * (b >= 0)[:, None], np.sin(angle) * (b >= 0)[:, None]
    table = np.zeros((6 * LANES, 2 * WIDE))
    for to, (re, im) in ((slice(0, SEG), (cos, sin)), (slice(WIDE, WIDE + SEG), (-sin, cos))):
        table[:WIDE, to], table[WIDE : 2 * WIDE, to] = re[:WIDE], im[:WIDE]
        table[2 * WIDE : 2 * WIDE + LANES, to], table[2 * WIDE + LANES :, to] = re[WIDE:], im[WIDE:]
    return table.astype(np.float32)


def twiddle_table():
    angle = np.outer(np.arange(WAVES), placed()) * (2.0 * math.pi / NLON)
    return np.concatenate([np.cos(angle), np.sin(angle)]).astype(np.float32)


def wave_table():
    k = np.arange(WAVES)[:, None] + PARTS * np.arange(SEG)[None, :]
    step = np.float32(math.pi / NLON)
    here = np.sin(k.astype(np.float32) * step) ** 2
    there = np.sin(((NLON - k) % NLON).astype(np.float32) * step) ** 2
    slope = 2.0 * np.sin(2.0 * math.pi * k / NLON)
    table = np.zeros((3 * WAVES, WIDE), np.float32)
    table[:, :SEG] = np.concatenate([here, there, slope])
    return table


def row_table():
    j = np.arange(-1, NLAT + 1)
    phi = np.float32(-0.5 * math.pi) + (j.astype(np.float32) + np.float32(0.5)) * np.float32(math.pi / NLAT)
    phi = phi.astype(np.float64)
    lat_step, lon_step = math.pi / NLAT, 2.0 * math.pi / NLON
    time_step = 0.25 * lat_step
    cos = np.cos(phi)
    y_coef = time_step / (2.0 * lat_step * cos)
    y_coef[0] = y_coef[-1] = 0.0
    table = np.zeros((NLAT, LANES))
    table[:, 0] = (cos / math.cos(0.25 * math.pi))[1:-1] ** 2
    table[:, 1] = (time_step / (2.0 * lon_step * cos))[1:-1]
    table[:, 2] = y_coef[1:-1]
    table[:, 3] = 0.3 * np.sin(phi)[1:-1]
    table[:, 4] = cos[1:-1]
    table[:, 5] = np.repeat(y_coef[0:NLAT:ROWS], ROWS)
    table[:, 6] = np.repeat(y_coef[ROWS + 1 :: ROWS], ROWS)
    table[:, 7] = np.arange(NLAT) // ROWS % 2
    return table.reshape(NLAT // ROWS, ROWS, LANES).astype(np.float32)


PUSH_COEF = 0.25 / 2.0
FIRST = 20
ORDER = [(i + FIRST) % PARTS for i in range(PARTS)]
ORDER[13], ORDER[26] = ORDER[26], ORDER[13]


def add(x, y):
    if x is None:
        return y
    return x if y is None else x + y


def sub(x, y):
    if y is None:
        return x
    return -y if x is None else x - y


def times(z, cos, sin):
    re, im = z
    if abs(sin) < 1e-15:
        return (re * cos, None if im is None else im * cos)
    if im is None:
        return (re * cos, re * sin)
    return (re * cos - im * sin, re * sin + im * cos)


def real_fft(values):
    n = len(values)
    if n == 2:
        return [(values[0] + values[1], None), (values[0] - values[1], None)]
    even, odd = real_fft(values[0::2]), real_fft(values[1::2])
    out = [None] * (n // 2 + 1)
    out[0] = (even[0][0] + odd[0][0], None)
    out[n // 2] = (even[0][0] - odd[0][0], None)
    for k in range(1, n // 4):
        re, im = times(odd[k], math.cos(2 * math.pi * k / n), -math.sin(2 * math.pi * k / n))
        out[k] = (add(even[k][0], re), add(even[k][1], im))
        out[n // 2 - k] = (sub(even[k][0], re), sub(im, even[k][1]))
    out[n // 4] = (even[n // 4][0], -odd[n // 4][0])
    return out


def real_ifft(waves):
    n = 2 * (len(waves) - 1)
    if n == 2:
        return [waves[0][0] + waves[1][0], waves[0][0] - waves[1][0]]
    even, odd = [None] * (n // 4 + 1), [None] * (n // 4 + 1)
    even[0] = (waves[0][0] + waves[n // 2][0], None)
    odd[0] = (waves[0][0] - waves[n // 2][0], None)
    for k in range(1, n // 4):
        (re, im), (far_re, far_im) = waves[k], waves[n // 2 - k]
        even[k] = (re + far_re, im - far_im)
        odd[k] = times((re - far_re, im + far_im), math.cos(2 * math.pi * k / n), math.sin(2 * math.pi * k / n))
    even[n // 4] = (2.0 * waves[n // 4][0], None)
    odd[n // 4] = (-2.0 * waves[n // 4][1], None)
    out = [None] * n
    out[0::2], out[1::2] = real_ifft(even), real_ifft(odd)
    return out


def lane(shape):
    return lax.broadcasted_iota(jnp.int32, shape, 1)


def own_quarter(shape):
    return lane(shape) // QUARTER == lax.broadcasted_iota(jnp.int32, shape, 0) % 4


def fold(tile):
    size = tile.shape[0]
    mine = jnp.where(own_quarter(tile.shape), tile, 0.0)
    pairs = mine + pltpu.roll(mine, size - 1, 0)
    return pairs + pltpu.roll(pairs, size - 2, 0)


def chunk_at(lon):
    return CHUNK * ORDER.index(lon)


def holder(level, r, turned):
    return level * 16 + (15 - r if turned else r)


def spot(level, r, turned):
    return chunk_at(holder(level, r, turned))


def east(level, start, count):
    return pl.ds(2 * start + level, count, 2)


def pack_kernel(turn_ref, u_hbm, v_hbm, h_hbm, out_ref, u_ref, v_ref, h_ref, tail_ref, last_ref, sems):
    moves = [
        pltpu.make_async_copy(src, dst, sems.at[i])
        for i, (src, dst) in enumerate(((u_hbm, u_ref), (v_hbm, v_ref), (h_hbm, h_ref)))
    ]
    for move in moves:
        move.start()
    last_ref[...] = jnp.zeros_like(last_ref)
    whole = []
    for move, ref in zip(moves, (u_ref, v_ref, h_ref)):
        move.wait()
        whole.append([ref[east(level, 0, LANES), :].T for level in range(2)])
    for level in range(2):
        tiles = [pair[level] for pair in whole]
        tail_ref[:TAIL, :] = u_ref[east(level, LANES, TAIL), :]
        tail_ref[TAIL:HALF, :] = h_ref[east(level, LANES, SIDE), :]
        tail_ref[HALF : HALF + TAIL, :] = v_ref[east(level, LANES, TAIL), :]
        tail_ref[HALF + TAIL :, :] = h_ref[east(level, LANES + SIDE, SIDE), :]
        tiles.append(tail_ref[...].T)
        last = h_ref[east(level, SEG - LAST, LAST), :]
        for g in range(4):
            last_ref[g * QUARTER : g * QUARTER + LAST, :] = last
        tail_ref[...] = fold(last_ref[...].T)
        folded = tail_ref[pl.ds(0, 32, 4), :]
        for turned in (False, True):

            @pl.when(turn_ref[0] == int(turned))
            def _():
                for r in range(16):
                    at = spot(level, r, turned)
                    for f in range(4):
                        out_ref[at + f * ROWS : at + (f + 1) * ROWS, :] = tiles[f][r * ROWS : (r + 1) * ROWS]
                    out_ref[at + 4 * ROWS : at + CHUNK, :] = folded[2 * r : 2 * r + 2]


def unpack_kernel(
    turn_ref, in_ref, u_ref, v_ref, h_ref, u_hbm, v_hbm, h_hbm, u_out, v_out, h_out, tile_ref, sems
):
    for level in range(2):
        for turned in (False, True):

            @pl.when(turn_ref[0] == int(turned))
            def _():
                for r in range(16):
                    at = spot(level, r, turned)
                    here = slice(r * ROWS, (r + 1) * ROWS)
                    for f in range(4):
                        tile_ref[level, f, here, :] = in_ref[at + f * ROWS : at + (f + 1) * ROWS, :]
                    for t in range(2):
                        row = in_ref[at + 4 * ROWS + t : at + 4 * ROWS + t + 1, :]
                        here = slice(r * ROWS + 4 * t, r * ROWS + 4 * t + 4)
                        tile_ref[level, 4, here, :] = jnp.broadcast_to(row, (4, LANES))

    mixed = [tile_ref[level, 3].T for level in range(2)]
    moves = []
    for f, (ref, out, hbm) in enumerate(((u_ref, u_out, u_hbm), (v_ref, v_out, v_hbm), (h_ref, h_out, h_hbm))):
        for level in range(2):
            if f < 2:
                changes = ((LANES, mixed[level][f * HALF : f * HALF + TAIL]),)
            else:
                quarters = tile_ref[level, 4].T
                group = lane((LAST, LANES)) % 4
                last = quarters[:LAST]
                for g in range(1, 4):
                    last = jnp.where(group == g, quarters[g * QUARTER : g * QUARTER + LAST], last)
                changes = (
                    (LANES, mixed[level][TAIL:HALF]), (LANES + SIDE, mixed[level][HALF + TAIL :]), (SEG - LAST, last)
                )
            for start, change in ((0, tile_ref[level, f].T), *changes):
                here = east(level, start, change.shape[0])
                out[here, :] = ref[here, :] + change
        moves.append(pltpu.make_async_copy(out, hbm, sems.at[f]))
        moves[-1].start()
    for move in moves:
        move.wait()


def halves(x):
    high = x.astype(jnp.bfloat16)
    return high, (x - high.astype(jnp.float32)).astype(jnp.bfloat16)


def dot(x, table, contract):
    def product(a, b):
        return lax.dot_general(a, b, (((1,), (contract,)), ((), ())), preferred_element_type=jnp.float32)

    (high, low), (table_high, table_low) = halves(x), table
    return product(high, table_high) + (product(high, table_low) + product(low, table_high))


BLOCK = WAVES * ROWS


def padded(fields):
    return -(-fields * BLOCK // 16) * 16


def transform(columns, high_ref, low_ref, twiddle_ref, spec_ref, left_ref):
    at = lane((ROWS, LANES))
    own = (at < TAIL, (at >= HALF) & (at < HALF + TAIL))
    for get, part, fields in columns:
        lanes = slice(part * LANES, (part + 1) * LANES)
        late = slice(WIDE + part * LANES, WIDE + (part + 1) * LANES)
        for k1, (re, im) in enumerate(real_fft([get(a) for a in range(PARTS)])):
            cos = twiddle_ref[k1 : k1 + 1, lanes]
            sin = twiddle_ref[WAVES + k1 : WAVES + k1 + 1, lanes]
            if im is None:
                new_re, new_im = re * cos, -re * sin
            else:
                new_re, new_im = re * cos + im * sin, im * cos - re * sin
            for f, half in fields:
                rows = slice(f * BLOCK + k1 * ROWS, f * BLOCK + (k1 + 1) * ROWS)
                if part == 0:
                    left_ref[rows, lanes], left_ref[rows, late] = new_re, new_im
                else:
                    left_ref[rows, lanes] = jnp.where(own[half], new_re, 0.0)
                    left_ref[rows, late] = jnp.where(own[half], new_im, 0.0)
    table = high_ref[: 2 * WIDE, :], low_ref[: 2 * WIDE, :]
    spec_ref[...] = dot(left_ref[...], table, 0)


def tiles_of(x_ref):
    def tile(f):
        return lambda a: x_ref[chunk_at(a) + f * ROWS : chunk_at(a) + (f + 1) * ROWS, :]

    return tile


def gather_tails(x_ref, tails_ref):
    at = lane((ROWS, LANES))
    place_of_four = lax.broadcasted_iota(jnp.int32, at.shape, 0) % 4
    for a in range(PARTS):
        base = chunk_at(a) + 3 * ROWS
        mixed = x_ref[base : base + ROWS, :]
        rows = [jnp.broadcast_to(x_ref[base + ROWS + t : base + ROWS + t + 1, :], (4, LANES)) for t in range(2)]
        quarters, last = jnp.concatenate(rows, axis=0), None
        for g in range(4):
            moved = pltpu.roll(quarters, (2 * SIDE - g * QUARTER) % LANES, 1)
            last = moved if last is None else jnp.where(place_of_four == g, moved, last)
        beside_u, beside_v = pltpu.roll(mixed, LANES - TAIL, 1), pltpu.roll(mixed, HALF - TAIL + SIDE, 1)
        whole = jnp.where(at < SIDE, beside_u, jnp.where(at < 2 * SIDE, beside_v, last))
        tails_ref[a * ROWS : (a + 1) * ROWS, :] = jnp.where(at < HALF, whole, pltpu.roll(whole, HALF, 1))


H, UH, VH = range(3)
U, V = range(2)


REAL, IMAG = slice(0, WIDE), slice(WIDE, 2 * WIDE)


def rows_of(f, k1):
    return slice(f * BLOCK + k1 * ROWS, f * BLOCK + (k1 + 1) * ROWS)


def factor_kernel(table_ref, wave_ref, row_ref, high_ref, low_ref, gain_ref, flux_ref, turn_ref, across_ref, along_ref):
    high_ref[...], low_ref[...] = halves(table_ref[...])
    row = row_ref[0]
    ratio2, x_coef, rotation, coslat = row[:, 0:1], row[:, 1:2], row[:, 3:4], row[:, 4:5]
    for k1 in range(WAVES):
        here, there, slope = (wave_ref[i * WAVES + k1 : i * WAVES + k1 + 1, :] for i in range(3))
        damp = 0.5 * (ratio2 / jnp.maximum(here, ratio2) + ratio2 / jnp.maximum(there, ratio2))
        across = x_coef * slope * damp
        gain_ref[rows_of(0, k1), :] = across
        flux_ref[rows_of(0, k1), :] = damp * coslat
        damp = SCALE * damp
        turn_ref[rows_of(0, k1), :] = damp * rotation
        across_ref[rows_of(0, k1), :] = SCALE * across
        along_ref[rows_of(0, k1), :] = -PUSH_COEF * damp


def wind_kernel(x_ref, high_ref, low_ref, twiddle_ref, turn_ref, spec_ref, left_ref):
    tile = tiles_of(x_ref)
    columns = ((tile(0), 0, ((U, 0),)), (tile(1), 0, ((V, 0),)), (tile(3), 1, ((U, 0), (V, 1))))
    transform(columns, high_ref, low_ref, twiddle_ref, spec_ref, left_ref)
    for k1 in range(WAVES):
        turn = turn_ref[rows_of(0, k1), :]
        for span in (REAL, IMAG):
            spec_ref[rows_of(U, k1), span] = -turn * spec_ref[rows_of(U, k1), span]
            spec_ref[rows_of(V, k1), span] = turn * spec_ref[rows_of(V, k1), span]


def to_message(rows):
    tails = rows[:, LANES:]
    tails = jnp.where(lane((2, LANES)) < HALF, tails[:2], pltpu.roll(tails[2:], HALF, 1))
    return jnp.concatenate([rows[:, :LANES], tails, jnp.zeros((2, LANES), jnp.float32)], axis=0)


def from_message(message):
    tails = message[4:6]
    tails = jnp.concatenate([tails, pltpu.roll(tails, HALF, 1)], axis=0)
    return jnp.concatenate([message[:4], tails], axis=1)


def mass_kernel(
    x_ref, high_ref, low_ref, twiddle_ref, gain_ref, scale_ref, row_ref, spec_ref, far_ref, near_ref, left_ref, tails_ref
):
    gather_tails(x_ref, tails_ref)
    tile = tiles_of(x_ref)

    def tail(a):
        return tails_ref[a * ROWS : (a + 1) * ROWS, :]

    def product(f, h):
        return lambda a: tile(f)(a) * h(a)

    columns = (
        (tile(2), 0, ((H, 0),)),
        (product(0, tile(2)), 0, ((UH, 0),)),
        (product(1, tile(2)), 0, ((VH, 0),)),
        (tail, 1, ((H, 0),)),
        (product(3, tail), 1, ((UH, 0), (VH, 1))),
    )
    transform(columns, high_ref, low_ref, twiddle_ref, spec_ref, left_ref)
    row = row_ref[0]
    y_coef, odd = row[:, 2:3], row[:4, 7:8] > 0.5
    for k1 in range(WAVES):
        across, scale = gain_ref[rows_of(0, k1), :], scale_ref[rows_of(0, k1), :]
        gain_re = across * spec_ref[rows_of(UH, k1), IMAG]
        gain_im = -across * spec_ref[rows_of(UH, k1), REAL]
        up, down = [], []
        for span, gain in ((REAL, gain_re), (IMAG, gain_im)):
            spec_ref[rows_of(UH, k1), span] = gain
            mass = spec_ref[rows_of(H, k1), span] + gain
            flux = scale * spec_ref[rows_of(VH, k1), span]
            spec_ref[rows_of(VH, k1), span] = flux
            up += [flux[7:8], mass[7:8] + y_coef[7:8] * flux[6:7]]
            down += [flux[0:1], mass[0:1] - y_coef[0:1] * flux[1:2]]
        up, down = jnp.concatenate(up, axis=0), jnp.concatenate(down, axis=0)
        near_ref[rows_of(0, k1), :] = to_message(jnp.where(odd, down, up))
        far_ref[rows_of(0, k1), :] = to_message(jnp.where(odd, up, down))


def inverse_kernel(
    spec_ref, wind_ref, far_ref, near_ref, high_ref, low_ref, twiddle_ref, across_ref, along_ref, row_ref, out_ref,
    left_ref, right_ref, last_ref
):
    row = row_ref[0]
    y_coef = row[:, 2:3]
    y_below, y_above = row[0:1, 5:6], row[0:1, 6:7]
    odd = row[:, 7:8] > 0.5
    for k1 in range(WAVES):
        near, far = near_ref[rows_of(0, k1), :], far_ref[rows_of(0, k1), :]
        below, above = from_message(jnp.where(odd, near, far)), from_message(jnp.where(odd, far, near))
        across, along = across_ref[rows_of(0, k1), :], along_ref[rows_of(0, k1), :]
        mass = []
        for part, span in enumerate((REAL, IMAG)):
            flux = spec_ref[rows_of(VH, k1), span]
            flux_below, flux_above = below[2 * part : 2 * part + 1], above[2 * part : 2 * part + 1]
            prev = jnp.concatenate([flux_below, flux[:-1]], axis=0)
            following = jnp.concatenate([flux[1:], flux_above], axis=0)
            change = spec_ref[rows_of(UH, k1), span] - y_coef * (following - prev)
            new = spec_ref[rows_of(H, k1), span] + change
            new_below = below[2 * part + 1 : 2 * part + 2] - y_below * flux[0:1]
            new_above = above[2 * part + 1 : 2 * part + 2] + y_above * flux[7:8]
            mass.append(new)
            prev = jnp.concatenate([new_below, new[:-1]], axis=0)
            following = jnp.concatenate([new[1:], new_above], axis=0)
            left_ref[rows_of(2, k1), span] = along * (following - prev) + wind_ref[rows_of(U, k1), span]
            left_ref[rows_of(0, k1), span] = SCALE * change
        left_ref[rows_of(1, k1), REAL] = across * mass[1] + wind_ref[rows_of(V, k1), REAL]
        left_ref[rows_of(1, k1), IMAG] = wind_ref[rows_of(V, k1), IMAG] - across * mass[0]
    right_ref[...] = dot(left_ref[...], (high_ref[: 2 * WIDE, :], low_ref[: 2 * WIDE, :]), 1)
    last_ref[...] = dot(left_ref[:BLOCK, :], (high_ref[2 * WIDE :, :], low_ref[2 * WIDE :, :]), 1)
    at = lane((ROWS, LANES))
    for f, part, fields in ((0, 0, (1,)), (1, 0, (2,)), (2, 0, (0,)), (3, 1, (0, 1, 2)), (4, 2, (0,))):
        lanes = slice(part * LANES, (part + 1) * LANES)
        source, start, late = (last_ref, 0, LANES) if part == 2 else (right_ref, part * LANES, WIDE + part * LANES)
        waves = []
        for k1 in range(WAVES):
            cos = twiddle_ref[k1 : k1 + 1, lanes]
            sin = twiddle_ref[WAVES + k1 : WAVES + k1 + 1, lanes]
            re = [source[rows_of(g, k1), start : start + LANES] for g in fields]
            im = [source[rows_of(g, k1), late : late + LANES] for g in fields]
            if len(fields) == 3:
                own = (at < TAIL, (at >= HALF) & (at < HALF + TAIL))
                re = [jnp.where(own[0], re[1], jnp.where(own[1], re[2], re[0]))]
                im = [jnp.where(own[0], im[1], jnp.where(own[1], im[2], im[0]))]
            re, im = re[0], im[0]
            waves.append((re * cos - im * sin, None if k1 in (0, WAVES - 1) else im * cos + re * sin))
        for a, value in enumerate(real_ifft(waves)):
            start = chunk_at(a) + f * ROWS
            if f == 4:
                value = fold(value)
                value = jnp.concatenate([value[0:1], value[4:5]], axis=0)
            out_ref[start : start + value.shape[0], :] = value


def in_vmem():
    return pl.BlockSpec(memory_space=pltpu.VMEM)


PARAMS = pltpu.CompilerParams(vmem_limit_bytes=40 * 2**20)


def like(*shape):
    return jax.ShapeDtypeStruct(shape, jnp.float32)


def place(level, r, lat):
    return holder(level, r, lat % 2 == 0) * 16 + lat


def swaps(odd):
    pairs = []
    for level in range(2):
        for lat in range(16):
            pairs += [(place(level, r, lat), place(level, r + 1, lat)) for r in range(odd, 15, 2)]
            if odd and lat < 15:
                pairs.append((place(level, 15, lat), place(level, 0, lat + 1)))
    return pairs + [(b, a) for a, b in pairs]


def in_smem():
    return pl.BlockSpec(memory_space=pltpu.SMEM)


def pack(turned, u, v, h):
    return pl.pallas_call(
        pack_kernel,
        out_shape=like(PARTS * CHUNK, LANES),
        in_specs=[in_smem()] + [pl.BlockSpec(memory_space=pltpu.HBM)] * 3,
        out_specs=in_vmem(),
        scratch_shapes=[pltpu.VMEM((2 * SEG, LANES), jnp.float32)] * 3
        + [pltpu.VMEM((LANES, LANES), jnp.float32)] * 2
        + [pltpu.SemaphoreType.DMA((3,))],
        compiler_params=pltpu.CompilerParams(vmem_limit_bytes=56 * 2**20),
        name="pack",
    )(turned, u, v, h)


def cost(fields):
    size = padded(fields) * 2 * WIDE
    return pl.CostEstimate(flops=6 * size * 2 * WIDE, bytes_accessed=8 * size, transcendentals=0)


def factors(row):
    table = jax.ShapeDtypeStruct((6 * LANES, 2 * WIDE), jnp.bfloat16)
    return pl.pallas_call(
        factor_kernel,
        out_shape=(table, table) + (like(BLOCK, WIDE),) * 5,
        in_specs=[in_vmem()] * 3,
        out_specs=(in_vmem(),) * 7,
        compiler_params=PARAMS,
        cost_estimate=pl.CostEstimate(flops=2**24, bytes_accessed=2**24, transcendentals=0),
        name="factors",
    )(dft_table(), wave_table(), row)


def forward_mass(whole, high, low, gain, scale, row):
    return pl.pallas_call(
        mass_kernel,
        out_shape=(like(padded(3), 2 * WIDE), like(BLOCK, LANES), like(BLOCK, LANES)),
        in_specs=[in_vmem()] * 7,
        out_specs=(in_vmem(),) * 3,
        scratch_shapes=[pltpu.VMEM((padded(3), 2 * WIDE), jnp.float32), pltpu.VMEM((PARTS * ROWS, LANES), jnp.float32)],
        compiler_params=PARAMS,
        cost_estimate=cost(3),
        name="forward_mass",
    )(whole, high, low, twiddle_table(), gain, scale, row)


def forward_wind(whole, high, low, turn):
    return pl.pallas_call(
        wind_kernel,
        out_shape=like(padded(2), 2 * WIDE),
        in_specs=[in_vmem()] * 5,
        out_specs=in_vmem(),
        scratch_shapes=[pltpu.VMEM((padded(2), 2 * WIDE), jnp.float32)],
        compiler_params=PARAMS,
        cost_estimate=cost(2),
        name="forward_wind",
    )(whole, high, low, twiddle_table(), turn)


def inverse(spec, wind, far, near, high, low, across, along, row):
    return pl.pallas_call(
        inverse_kernel,
        out_shape=like(PARTS * CHUNK, LANES),
        in_specs=[in_vmem()] * 10,
        out_specs=in_vmem(),
        scratch_shapes=[pltpu.VMEM((padded(3), 2 * WIDE), jnp.float32)] * 2 + [pltpu.VMEM((BLOCK, WIDE), jnp.float32)],
        compiler_params=PARAMS,
        cost_estimate=cost(3),
        name="inverse",
    )(spec, wind, far, near, high, low, twiddle_table(), across, along, row)


def unpack(turned, back, u, v, h):
    return pl.pallas_call(
        unpack_kernel,
        out_shape=(like(2 * SEG, LANES),) * 3,
        in_specs=[in_smem()] + [in_vmem()] * 4,
        out_specs=(pl.BlockSpec(memory_space=pltpu.HBM),) * 3,
        scratch_shapes=[pltpu.VMEM((2 * SEG, LANES), jnp.float32)] * 3
        + [pltpu.VMEM((2, 5, LANES, LANES), jnp.float32), pltpu.SemaphoreType.DMA((3,))],
        compiler_params=PARAMS,
        name="unpack",
    )(turned, back, u, v, h)


def row_of(group):
    return lax.dynamic_slice_in_dim(jnp.asarray(row_table()), group, 1, axis=0)


def exchange(chunks):
    moved = lax.all_to_all(chunks.reshape(PARTS, CHUNK, 1, LANES), "lon", 0, 0, axis_index_groups=[ORDER], tiled=True)
    return moved.reshape(PARTS * CHUNK, LANES)


def step(u, v, h):
    lat = lax.axis_index("lat")
    turned = 1 - lat % 2
    r = lax.axis_index("lon") % 16
    row = row_of(lat * 16 + jnp.where(turned == 1, 15 - r, r))
    turned = turned.reshape(1)
    u, v, h = (jnp.swapaxes(x, 0, 1).reshape(2 * SEG, LANES) for x in (u, v, h))
    high, low, gain, scale, turn, across, along = factors(row)
    whole = exchange(pack(turned, u, v, h))
    spec, far, near = forward_mass(whole, high, low, gain, scale, row)
    far = lax.ppermute(far, ("lon", "lat"), swaps(1))
    near = lax.ppermute(near, ("lon", "lat"), swaps(0))
    wind = forward_wind(whole, high, low, turn)
    back = exchange(inverse(spec, wind, far, near, high, low, across, along, row))
    outs = unpack(turned, back, u, v, h)
    return tuple(jnp.swapaxes(x.reshape(SEG, 2, LANES), 0, 1) for x in outs)


def solution(mesh):
    spec = P(None, "lon", "lat")
    return jax.shard_map(step, mesh=mesh, in_specs=(spec,) * 3, out_specs=(spec,) * 3, check_vma=False)
```

```python
import functools
import math

import jax
import jax.numpy as jnp
import numpy as np
from jax import lax
from jax.experimental import pallas as pl
from jax.experimental.pallas import tpu as pltpu
from jax.sharding import PartitionSpec as P

NLON = 5760
NLAT = 2048
PARTS = 32
SEG = 180
LANES = 128
TAIL = SEG - LANES
HALF = 64
ROWS = 8
WAVES = PARTS // 2 + 1
WIDE = 2 * LANES
SCALE = 1.0 / NLON
SIDE = HALF - TAIL
LAST = TAIL - 2 * SIDE
QUARTER = 32
CHUNK = 4 * ROWS + 2


def placed():
    b = np.arange(SEG)
    tail, side = b[LANES:], LANES + SIDE
    last = np.concatenate([b[-LAST:], np.full(QUARTER - LAST, -1)])
    return np.concatenate([b[:LANES], tail, b[LANES:side], tail, b[side : side + SIDE], np.tile(last, 4)])


def dft_table():
    b = placed()
    angle = (np.outer(b, np.arange(SEG)) % SEG) * (2.0 * math.pi / SEG)
    cos, sin = np.cos(angle) * (b >= 0)[:, None], np.sin(angle) * (b >= 0)[:, None]
    table = np.zeros((6 * LANES, 2 * WIDE))
    for to, (re, im) in ((slice(0, SEG), (cos, sin)), (slice(WIDE, WIDE + SEG), (-sin, cos))):
        table[:WIDE, to], table[WIDE : 2 * WIDE, to] = re[:WIDE], im[:WIDE]
        table[2 * WIDE : 2 * WIDE + LANES, to], table[2 * WIDE + LANES :, to] = re[WIDE:], im[WIDE:]
    return table.astype(np.float32)


def twiddle_table():
    angle = np.outer(np.arange(WAVES), placed()) * (2.0 * math.pi / NLON)
    return np.concatenate([np.cos(angle), np.sin(angle)]).astype(np.float32)


def wave_table():
    k = np.arange(WAVES)[:, None] + PARTS * np.arange(SEG)[None, :]
    step = np.float32(math.pi / NLON)
    here = np.sin(k.astype(np.float32) * step) ** 2
    there = np.sin(((NLON - k) % NLON).astype(np.float32) * step) ** 2
    slope = 2.0 * np.sin(2.0 * math.pi * k / NLON)
    table = np.zeros((3 * WAVES, WIDE), np.float32)
    table[:, :SEG] = np.concatenate([here, there, slope])
    return table


def row_table():
    j = np.arange(-1, NLAT + 1)
    phi = np.float32(-0.5 * math.pi) + (j.astype(np.float32) + np.float32(0.5)) * np.float32(math.pi / NLAT)
    phi = phi.astype(np.float64)
    lat_step, lon_step = math.pi / NLAT, 2.0 * math.pi / NLON
    time_step = 0.25 * lat_step
    cos = np.cos(phi)
    y_coef = time_step / (2.0 * lat_step * cos)
    y_coef[0] = y_coef[-1] = 0.0
    table = np.zeros((NLAT, LANES))
    table[:, 0] = (cos / math.cos(0.25 * math.pi))[1:-1] ** 2
    table[:, 1] = (time_step / (2.0 * lon_step * cos))[1:-1]
    table[:, 2] = y_coef[1:-1]
    table[:, 3] = 0.3 * np.sin(phi)[1:-1]
    table[:, 4] = cos[1:-1]
    table[:, 5] = np.repeat(y_coef[0:NLAT:ROWS], ROWS)
    table[:, 6] = np.repeat(y_coef[ROWS + 1 :: ROWS], ROWS)
    table[:, 7] = np.arange(NLAT) // ROWS % 2
    return table.reshape(NLAT // ROWS, ROWS, LANES).astype(np.float32)


PUSH_COEF = 0.25 / 2.0
FIRST = 20
ORDER = [(i + FIRST) % PARTS for i in range(PARTS)]
ORDER[13], ORDER[26] = ORDER[26], ORDER[13]
ORDER[15], ORDER[31] = ORDER[31], ORDER[15]


def add(x, y):
    if x is None:
        return y
    return x if y is None else x + y


def sub(x, y):
    if y is None:
        return x
    return -y if x is None else x - y


def times(z, cos, sin):
    re, im = z
    if abs(sin) < 1e-15:
        return (re * cos, None if im is None else im * cos)
    if im is None:
        return (re * cos, re * sin)
    return (re * cos - im * sin, re * sin + im * cos)


def real_fft(values):
    n = len(values)
    if n == 2:
        return [(values[0] + values[1], None), (values[0] - values[1], None)]
    even, odd = real_fft(values[0::2]), real_fft(values[1::2])
    out = [None] * (n // 2 + 1)
    out[0] = (even[0][0] + odd[0][0], None)
    out[n // 2] = (even[0][0] - odd[0][0], None)
    for k in range(1, n // 4):
        re, im = times(odd[k], math.cos(2 * math.pi * k / n), -math.sin(2 * math.pi * k / n))
        out[k] = (add(even[k][0], re), add(even[k][1], im))
        out[n // 2 - k] = (sub(even[k][0], re), sub(im, even[k][1]))
    out[n // 4] = (even[n // 4][0], -odd[n // 4][0])
    return out


def real_ifft(waves):
    n = 2 * (len(waves) - 1)
    if n == 2:
        return [waves[0][0] + waves[1][0], waves[0][0] - waves[1][0]]
    even, odd = [None] * (n // 4 + 1), [None] * (n // 4 + 1)
    even[0] = (waves[0][0] + waves[n // 2][0], None)
    odd[0] = (waves[0][0] - waves[n // 2][0], None)
    for k in range(1, n // 4):
        (re, im), (far_re, far_im) = waves[k], waves[n // 2 - k]
        even[k] = (re + far_re, im - far_im)
        odd[k] = times((re - far_re, im + far_im), math.cos(2 * math.pi * k / n), math.sin(2 * math.pi * k / n))
    even[n // 4] = (2.0 * waves[n // 4][0], None)
    odd[n // 4] = (-2.0 * waves[n // 4][1], None)
    out = [None] * n
    out[0::2], out[1::2] = real_ifft(even), real_ifft(odd)
    return out


def lane(shape):
    return lax.broadcasted_iota(jnp.int32, shape, 1)


def own_quarter(shape):
    return lane(shape) // QUARTER == lax.broadcasted_iota(jnp.int32, shape, 0) % 4


def fold(tile):
    size = tile.shape[0]
    mine = jnp.where(own_quarter(tile.shape), tile, 0.0)
    pairs = mine + pltpu.roll(mine, size - 1, 0)
    return pairs + pltpu.roll(pairs, size - 2, 0)


def chunk_at(lon):
    return CHUNK * ORDER.index(lon)


def holder(level, r, turned):
    return level * 16 + (15 - r if turned else r)


def spot(level, r, turned):
    return chunk_at(holder(level, r, turned))


def east(level, start, count):
    return pl.ds(2 * start + level, count, 2)


def pack_kernel(turn_ref, u_hbm, v_hbm, h_hbm, out_ref, u_ref, v_ref, h_ref, tail_ref, last_ref, sems):
    moves = [
        pltpu.make_async_copy(src, dst, sems.at[i])
        for i, (src, dst) in enumerate(((u_hbm, u_ref), (v_hbm, v_ref), (h_hbm, h_ref)))
    ]
    for move in moves:
        move.start()
    last_ref[...] = jnp.zeros_like(last_ref)
    whole = []
    for move, ref in zip(moves, (u_ref, v_ref, h_ref)):
        move.wait()
        whole.append([ref[east(level, 0, LANES), :].T for level in range(2)])
    for level in range(2):
        tiles = [pair[level] for pair in whole]
        tail_ref[:TAIL, :] = u_ref[east(level, LANES, TAIL), :]
        tail_ref[TAIL:HALF, :] = h_ref[east(level, LANES, SIDE), :]
        tail_ref[HALF : HALF + TAIL, :] = v_ref[east(level, LANES, TAIL), :]
        tail_ref[HALF + TAIL :, :] = h_ref[east(level, LANES + SIDE, SIDE), :]
        tiles.append(tail_ref[...].T)
        last = h_ref[east(level, SEG - LAST, LAST), :]
        for g in range(4):
            last_ref[g * QUARTER : g * QUARTER + LAST, :] = last
        tail_ref[...] = fold(last_ref[...].T)
        folded = tail_ref[pl.ds(0, 32, 4), :]
        for turned in (False, True):

            @pl.when(turn_ref[0] == int(turned))
            def _():
                for r in range(16):
                    at = spot(level, r, turned)
                    for f in range(4):
                        out_ref[at + f * ROWS : at + (f + 1) * ROWS, :] = tiles[f][r * ROWS : (r + 1) * ROWS]
                    out_ref[at + 4 * ROWS : at + CHUNK, :] = folded[2 * r : 2 * r + 2]


def unpack_kernel(
    turn_ref, in_ref, u_ref, v_ref, h_ref, u_hbm, v_hbm, h_hbm, u_out, v_out, h_out, tile_ref, sems
):
    for level in range(2):
        for turned in (False, True):

            @pl.when(turn_ref[0] == int(turned))
            def _():
                for r in range(16):
                    at = spot(level, r, turned)
                    here = slice(r * ROWS, (r + 1) * ROWS)
                    for f in range(4):
                        tile_ref[level, f, here, :] = in_ref[at + f * ROWS : at + (f + 1) * ROWS, :]
                    for t in range(2):
                        row = in_ref[at + 4 * ROWS + t : at + 4 * ROWS + t + 1, :]
                        here = slice(r * ROWS + 4 * t, r * ROWS + 4 * t + 4)
                        tile_ref[level, 4, here, :] = jnp.broadcast_to(row, (4, LANES))

    mixed = [tile_ref[level, 3].T for level in range(2)]
    moves = []
    for f, (ref, out, hbm) in enumerate(((u_ref, u_out, u_hbm), (v_ref, v_out, v_hbm), (h_ref, h_out, h_hbm))):
        for level in range(2):
            if f < 2:
                changes = ((LANES, mixed[level][f * HALF : f * HALF + TAIL]),)
            else:
                quarters = tile_ref[level, 4].T
                group = lane((LAST, LANES)) % 4
                last = quarters[:LAST]
                for g in range(1, 4):
                    last = jnp.where(group == g, quarters[g * QUARTER : g * QUARTER + LAST], last)
                changes = (
                    (LANES, mixed[level][TAIL:HALF]), (LANES + SIDE, mixed[level][HALF + TAIL :]), (SEG - LAST, last)
                )
            for start, change in ((0, tile_ref[level, f].T), *changes):
                here = east(level, start, change.shape[0])
                out[here, :] = ref[here, :] + change
        moves.append(pltpu.make_async_copy(out, hbm, sems.at[f]))
        moves[-1].start()
    for move in moves:
        move.wait()


def halves(x):
    high = x.astype(jnp.bfloat16)
    return high, (x - high.astype(jnp.float32)).astype(jnp.bfloat16)


def dot(x, table, contract):
    def product(a, b):
        return lax.dot_general(a, b, (((1,), (contract,)), ((), ())), preferred_element_type=jnp.float32)

    (high, low), (table_high, table_low) = halves(x), table
    return product(high, table_high) + (product(high, table_low) + product(low, table_high))


BLOCK = WAVES * ROWS


def padded(fields):
    return -(-fields * BLOCK // 16) * 16


def transform(columns, high_ref, low_ref, twiddle_ref, spec_ref, left_ref):
    at = lane((ROWS, LANES))
    own = (at < TAIL, (at >= HALF) & (at < HALF + TAIL))
    for get, part, fields in columns:
        lanes = slice(part * LANES, (part + 1) * LANES)
        late = slice(WIDE + part * LANES, WIDE + (part + 1) * LANES)
        for k1, (re, im) in enumerate(real_fft([get(a) for a in range(PARTS)])):
            cos = twiddle_ref[k1 : k1 + 1, lanes]
            sin = twiddle_ref[WAVES + k1 : WAVES + k1 + 1, lanes]
            if im is None:
                new_re, new_im = re * cos, -re * sin
            else:
                new_re, new_im = re * cos + im * sin, im * cos - re * sin
            for f, half in fields:
                rows = slice(f * BLOCK + k1 * ROWS, f * BLOCK + (k1 + 1) * ROWS)
                if part == 0:
                    left_ref[rows, lanes], left_ref[rows, late] = new_re, new_im
                else:
                    left_ref[rows, lanes] = jnp.where(own[half], new_re, 0.0)
                    left_ref[rows, late] = jnp.where(own[half], new_im, 0.0)
    table = high_ref[: 2 * WIDE, :], low_ref[: 2 * WIDE, :]
    spec_ref[...] = dot(left_ref[...], table, 0)


def tiles_of(x_ref):
    def tile(f):
        return lambda a: x_ref[chunk_at(a) + f * ROWS : chunk_at(a) + (f + 1) * ROWS, :]

    return tile


def gather_tails(x_ref, tails_ref):
    at = lane((ROWS, LANES))
    place_of_four = lax.broadcasted_iota(jnp.int32, at.shape, 0) % 4
    for a in range(PARTS):
        base = chunk_at(a) + 3 * ROWS
        mixed = x_ref[base : base + ROWS, :]
        rows = [jnp.broadcast_to(x_ref[base + ROWS + t : base + ROWS + t + 1, :], (4, LANES)) for t in range(2)]
        quarters, last = jnp.concatenate(rows, axis=0), None
        for g in range(4):
            moved = pltpu.roll(quarters, (2 * SIDE - g * QUARTER) % LANES, 1)
            last = moved if last is None else jnp.where(place_of_four == g, moved, last)
        beside_u, beside_v = pltpu.roll(mixed, LANES - TAIL, 1), pltpu.roll(mixed, HALF - TAIL + SIDE, 1)
        whole = jnp.where(at < SIDE, beside_u, jnp.where(at < 2 * SIDE, beside_v, last))
        tails_ref[a * ROWS : (a + 1) * ROWS, :] = jnp.where(at < HALF, whole, pltpu.roll(whole, HALF, 1))


H, UH, VH = range(3)
U, V = range(2)


REAL, IMAG = slice(0, WIDE), slice(WIDE, 2 * WIDE)


def rows_of(f, k1):
    return slice(f * BLOCK + k1 * ROWS, f * BLOCK + (k1 + 1) * ROWS)


def factor_kernel(table_ref, wave_ref, row_ref, high_ref, low_ref, gain_ref, flux_ref, turn_ref, across_ref, along_ref):
    high_ref[...], low_ref[...] = halves(table_ref[...])
    row = row_ref[0]
    ratio2, x_coef, rotation, coslat = row[:, 0:1], row[:, 1:2], row[:, 3:4], row[:, 4:5]
    for k1 in range(WAVES):
        here, there, slope = (wave_ref[i * WAVES + k1 : i * WAVES + k1 + 1, :] for i in range(3))
        damp = 0.5 * (ratio2 / jnp.maximum(here, ratio2) + ratio2 / jnp.maximum(there, ratio2))
        across = x_coef * slope * damp
        gain_ref[rows_of(0, k1), :] = across
        flux_ref[rows_of(0, k1), :] = damp * coslat
        damp = SCALE * damp
        turn_ref[rows_of(0, k1), :] = damp * rotation
        across_ref[rows_of(0, k1), :] = SCALE * across
        along_ref[rows_of(0, k1), :] = -PUSH_COEF * damp


def wind_kernel(x_ref, high_ref, low_ref, twiddle_ref, turn_ref, spec_ref, left_ref):
    tile = tiles_of(x_ref)
    columns = ((tile(0), 0, ((U, 0),)), (tile(1), 0, ((V, 0),)), (tile(3), 1, ((U, 0), (V, 1))))
    transform(columns, high_ref, low_ref, twiddle_ref, spec_ref, left_ref)
    for k1 in range(WAVES):
        turn = turn_ref[rows_of(0, k1), :]
        for span in (REAL, IMAG):
            spec_ref[rows_of(U, k1), span] = -turn * spec_ref[rows_of(U, k1), span]
            spec_ref[rows_of(V, k1), span] = turn * spec_ref[rows_of(V, k1), span]


def to_message(rows):
    tails = rows[:, LANES:]
    tails = jnp.where(lane((2, LANES)) < HALF, tails[:2], pltpu.roll(tails[2:], HALF, 1))
    return jnp.concatenate([rows[:, :LANES], tails, jnp.zeros((2, LANES), jnp.float32)], axis=0)


def from_message(message):
    tails = message[4:6]
    tails = jnp.concatenate([tails, pltpu.roll(tails, HALF, 1)], axis=0)
    return jnp.concatenate([message[:4], tails], axis=1)


def mass_kernel(
    x_ref, high_ref, low_ref, twiddle_ref, gain_ref, scale_ref, row_ref, spec_ref, far_ref, near_ref, left_ref, tails_ref
):
    gather_tails(x_ref, tails_ref)
    tile = tiles_of(x_ref)

    def tail(a):
        return tails_ref[a * ROWS : (a + 1) * ROWS, :]

    def product(f, h):
        return lambda a: tile(f)(a) * h(a)

    columns = (
        (tile(2), 0, ((H, 0),)),
        (product(0, tile(2)), 0, ((UH, 0),)),
        (product(1, tile(2)), 0, ((VH, 0),)),
        (tail, 1, ((H, 0),)),
        (product(3, tail), 1, ((UH, 0), (VH, 1))),
    )
    transform(columns, high_ref, low_ref, twiddle_ref, spec_ref, left_ref)
    row = row_ref[0]
    y_coef, odd = row[:, 2:3], row[:4, 7:8] > 0.5
    for k1 in range(WAVES):
        across, scale = gain_ref[rows_of(0, k1), :], scale_ref[rows_of(0, k1), :]
        gain_re = across * spec_ref[rows_of(UH, k1), IMAG]
        gain_im = -across * spec_ref[rows_of(UH, k1), REAL]
        up, down = [], []
        for span, gain in ((REAL, gain_re), (IMAG, gain_im)):
            spec_ref[rows_of(UH, k1), span] = gain
            mass = spec_ref[rows_of(H, k1), span] + gain
            flux = scale * spec_ref[rows_of(VH, k1), span]
            spec_ref[rows_of(VH, k1), span] = flux
            up += [flux[7:8], mass[7:8] + y_coef[7:8] * flux[6:7]]
            down += [flux[0:1], mass[0:1] - y_coef[0:1] * flux[1:2]]
        up, down = jnp.concatenate(up, axis=0), jnp.concatenate(down, axis=0)
        near_ref[rows_of(0, k1), :] = to_message(jnp.where(odd, down, up))
        far_ref[rows_of(0, k1), :] = to_message(jnp.where(odd, up, down))


def inverse_kernel(
    spec_ref, wind_ref, far_ref, near_ref, high_ref, low_ref, twiddle_ref, across_ref, along_ref, row_ref, out_ref,
    left_ref, right_ref, last_ref
):
    row = row_ref[0]
    y_coef = row[:, 2:3]
    y_below, y_above = row[0:1, 5:6], row[0:1, 6:7]
    odd = row[:, 7:8] > 0.5
    for k1 in range(WAVES):
        near, far = near_ref[rows_of(0, k1), :], far_ref[rows_of(0, k1), :]
        below, above = from_message(jnp.where(odd, near, far)), from_message(jnp.where(odd, far, near))
        across, along = across_ref[rows_of(0, k1), :], along_ref[rows_of(0, k1), :]
        mass = []
        for part, span in enumerate((REAL, IMAG)):
            flux = spec_ref[rows_of(VH, k1), span]
            flux_below, flux_above = below[2 * part : 2 * part + 1], above[2 * part : 2 * part + 1]
            prev = jnp.concatenate([flux_below, flux[:-1]], axis=0)
            following = jnp.concatenate([flux[1:], flux_above], axis=0)
            change = spec_ref[rows_of(UH, k1), span] - y_coef * (following - prev)
            new = spec_ref[rows_of(H, k1), span] + change
            new_below = below[2 * part + 1 : 2 * part + 2] - y_below * flux[0:1]
            new_above = above[2 * part + 1 : 2 * part + 2] + y_above * flux[7:8]
            mass.append(new)
            prev = jnp.concatenate([new_below, new[:-1]], axis=0)
            following = jnp.concatenate([new[1:], new_above], axis=0)
            left_ref[rows_of(2, k1), span] = along * (following - prev) + wind_ref[rows_of(U, k1), span]
            left_ref[rows_of(0, k1), span] = SCALE * change
        left_ref[rows_of(1, k1), REAL] = across * mass[1] + wind_ref[rows_of(V, k1), REAL]
        left_ref[rows_of(1, k1), IMAG] = wind_ref[rows_of(V, k1), IMAG] - across * mass[0]
    right_ref[...] = dot(left_ref[...], (high_ref[: 2 * WIDE, :], low_ref[: 2 * WIDE, :]), 1)
    last_ref[...] = dot(left_ref[:BLOCK, :], (high_ref[2 * WIDE :, :], low_ref[2 * WIDE :, :]), 1)
    at = lane((ROWS, LANES))
    for f, part, fields in ((0, 0, (1,)), (1, 0, (2,)), (2, 0, (0,)), (3, 1, (0, 1, 2)), (4, 2, (0,))):
        lanes = slice(part * LANES, (part + 1) * LANES)
        source, start, late = (last_ref, 0, LANES) if part == 2 else (right_ref, part * LANES, WIDE + part * LANES)
        waves = []
        for k1 in range(WAVES):
            cos = twiddle_ref[k1 : k1 + 1, lanes]
            sin = twiddle_ref[WAVES + k1 : WAVES + k1 + 1, lanes]
            re = [source[rows_of(g, k1), start : start + LANES] for g in fields]
            im = [source[rows_of(g, k1), late : late + LANES] for g in fields]
            if len(fields) == 3:
                own = (at < TAIL, (at >= HALF) & (at < HALF + TAIL))
                re = [jnp.where(own[0], re[1], jnp.where(own[1], re[2], re[0]))]
                im = [jnp.where(own[0], im[1], jnp.where(own[1], im[2], im[0]))]
            re, im = re[0], im[0]
            waves.append((re * cos - im * sin, None if k1 in (0, WAVES - 1) else im * cos + re * sin))
        for a, value in enumerate(real_ifft(waves)):
            start = chunk_at(a) + f * ROWS
            if f == 4:
                value = fold(value)
                value = jnp.concatenate([value[0:1], value[4:5]], axis=0)
            out_ref[start : start + value.shape[0], :] = value


def in_vmem():
    return pl.BlockSpec(memory_space=pltpu.VMEM)


PARAMS = pltpu.CompilerParams(vmem_limit_bytes=40 * 2**20)


def like(*shape):
    return jax.ShapeDtypeStruct(shape, jnp.float32)


def place(level, r, lat):
    return holder(level, r, lat % 2 == 0) * 16 + lat


def swaps(odd):
    pairs = []
    for level in range(2):
        for lat in range(16):
            pairs += [(place(level, r, lat), place(level, r + 1, lat)) for r in range(odd, 15, 2)]
            if odd and lat < 15:
                pairs.append((place(level, 15, lat), place(level, 0, lat + 1)))
    return pairs + [(b, a) for a, b in pairs]


def in_smem():
    return pl.BlockSpec(memory_space=pltpu.SMEM)


def pack(turned, u, v, h):
    return pl.pallas_call(
        pack_kernel,
        out_shape=like(PARTS * CHUNK, LANES),
        in_specs=[in_smem()] + [pl.BlockSpec(memory_space=pltpu.HBM)] * 3,
        out_specs=in_vmem(),
        scratch_shapes=[pltpu.VMEM((2 * SEG, LANES), jnp.float32)] * 3
        + [pltpu.VMEM((LANES, LANES), jnp.float32)] * 2
        + [pltpu.SemaphoreType.DMA((3,))],
        compiler_params=pltpu.CompilerParams(vmem_limit_bytes=56 * 2**20),
        name="pack",
    )(turned, u, v, h)


def cost(fields):
    size = padded(fields) * 2 * WIDE
    return pl.CostEstimate(flops=6 * size * 2 * WIDE, bytes_accessed=8 * size, transcendentals=0)


def factors(row):
    table = jax.ShapeDtypeStruct((6 * LANES, 2 * WIDE), jnp.bfloat16)
    return pl.pallas_call(
        factor_kernel,
        out_shape=(table, table) + (like(BLOCK, WIDE),) * 5,
        in_specs=[in_vmem()] * 3,
        out_specs=(in_vmem(),) * 7,
        compiler_params=PARAMS,
        cost_estimate=pl.CostEstimate(flops=2**24, bytes_accessed=2**24, transcendentals=0),
        name="factors",
    )(dft_table(), wave_table(), row)


def forward_mass(whole, high, low, gain, scale, row):
    return pl.pallas_call(
        mass_kernel,
        out_shape=(like(padded(3), 2 * WIDE), like(BLOCK, LANES), like(BLOCK, LANES)),
        in_specs=[in_vmem()] * 7,
        out_specs=(in_vmem(),) * 3,
        scratch_shapes=[pltpu.VMEM((padded(3), 2 * WIDE), jnp.float32), pltpu.VMEM((PARTS * ROWS, LANES), jnp.float32)],
        compiler_params=PARAMS,
        cost_estimate=cost(3),
        name="forward_mass",
    )(whole, high, low, twiddle_table(), gain, scale, row)


def forward_wind(whole, high, low, turn):
    return pl.pallas_call(
        wind_kernel,
        out_shape=like(padded(2), 2 * WIDE),
        in_specs=[in_vmem()] * 5,
        out_specs=in_vmem(),
        scratch_shapes=[pltpu.VMEM((padded(2), 2 * WIDE), jnp.float32)],
        compiler_params=PARAMS,
        cost_estimate=cost(2),
        name="forward_wind",
    )(whole, high, low, twiddle_table(), turn)


def inverse(spec, wind, far, near, high, low, across, along, row):
    return pl.pallas_call(
        inverse_kernel,
        out_shape=like(PARTS * CHUNK, LANES),
        in_specs=[in_vmem()] * 10,
        out_specs=in_vmem(),
        scratch_shapes=[pltpu.VMEM((padded(3), 2 * WIDE), jnp.float32)] * 2 + [pltpu.VMEM((BLOCK, WIDE), jnp.float32)],
        compiler_params=PARAMS,
        cost_estimate=cost(3),
        name="inverse",
    )(spec, wind, far, near, high, low, twiddle_table(), across, along, row)


def unpack(turned, back, u, v, h):
    return pl.pallas_call(
        unpack_kernel,
        out_shape=(like(2 * SEG, LANES),) * 3,
        in_specs=[in_smem()] + [in_vmem()] * 4,
        out_specs=(pl.BlockSpec(memory_space=pltpu.HBM),) * 3,
        scratch_shapes=[pltpu.VMEM((2 * SEG, LANES), jnp.float32)] * 3
        + [pltpu.VMEM((2, 5, LANES, LANES), jnp.float32), pltpu.SemaphoreType.DMA((3,))],
        compiler_params=PARAMS,
        name="unpack",
    )(turned, back, u, v, h)


def row_of(group):
    return lax.dynamic_slice_in_dim(jnp.asarray(row_table()), group, 1, axis=0)


def exchange(chunks):
    moved = lax.all_to_all(chunks.reshape(PARTS, CHUNK, 1, LANES), "lon", 0, 0, axis_index_groups=[ORDER], tiled=True)
    return moved.reshape(PARTS * CHUNK, LANES)


def step(u, v, h):
    lat = lax.axis_index("lat")
    turned = 1 - lat % 2
    r = lax.axis_index("lon") % 16
    row = row_of(lat * 16 + jnp.where(turned == 1, 15 - r, r))
    turned = turned.reshape(1)
    u, v, h = (jnp.swapaxes(x, 0, 1).reshape(2 * SEG, LANES) for x in (u, v, h))
    high, low, gain, scale, turn, across, along = factors(row)
    whole = exchange(pack(turned, u, v, h))
    spec, far, near = forward_mass(whole, high, low, gain, scale, row)
    far = lax.ppermute(far, ("lon", "lat"), swaps(1))
    near = lax.ppermute(near, ("lon", "lat"), swaps(0))
    wind = forward_wind(whole, high, low, turn)
    back = exchange(inverse(spec, wind, far, near, high, low, across, along, row))
    outs = unpack(turned, back, u, v, h)
    return tuple(jnp.swapaxes(x.reshape(SEG, 2, LANES), 0, 1) for x in outs)


def solution(mesh):
    spec = P(None, "lon", "lat")
    return jax.shard_map(step, mesh=mesh, in_specs=(spec,) * 3, out_specs=(spec,) * 3, check_vma=False)
```
